32 devices in a mesh: parts: 2 (over y), gz: 4 (over z), gy: 4 (over x, core).
Axes of the slice: x: 2, y: 2, z: 4, core: 2. Of those that a mesh axis runs over, the one named last changes fastest.
Arguments:
- initial_class_tags: int32 [64, 64, 384], P(('parts', 'gz'), 'gy'), parts along dimension 0, may hold values from 0 to 15
- depth_affinity: int32 [64, 64, 384], P(('parts', 'gz'), 'gy'), parts along dimension 0, may hold values from 0 to 255
- row_affinity: int32 [64, 64, 384], P(('parts', 'gz'), 'gy'), parts along dimension 0, may hold values from 0 to 255
- column_affinity: int32 [64, 64, 384], P(('parts', 'gz'), 'gy'), parts along dimension 0, may hold values from 0 to 255
Outputs:
- potentials: float32 [4, 64, 64, 384], P(None, ('parts', 'gz'), 'gy'), parts along dimension 1
The draws below stay inside these ranges and needn't reach their ends.
There are 2 independent parts, one for each index of `parts`. The reference program is written for one: setup_inputs(seed, part) draws one part's arguments, and reference() takes and returns one part's arrays. A program takes and returns all parts, laid end to end along the dimension named above; each array names one. Nothing has to cross between parts.
All inputs are finite; a program needn't handle non-finite values.
Results may differ from the reference program's by a relative error of at most 0.00025.
Values sent between devices are 32-bit elements; how exact they have to be, the bound alone decides.
No kernel may reach another device: no remote copies, remote signals or barrier semaphores. Data moves between devices by JAX's collectives and lax.ppermute only.
A program may use at most 64 MiB of HBM per device.

```python
import jax
import jax.numpy as jnp
from jax import lax

CZ = 8
CY = 16
CX = 384
LABELS = 4
ITERS = 3
NZ = 32
NY = 64


def region_table(key, lowest, highest):
    return jax.random.randint(key, (NZ // CZ, NY // CY), lowest, highest)


def spread_blocks(table):
    widened = jnp.repeat(table, CZ, axis=0)
    widened = jnp.repeat(widened, CY, axis=1)
    return widened[:, :, None]


def shared_strength(key):
    shared_key = jax.random.fold_in(key, 101)
    ceilings = region_table(shared_key, 52, 257)
    chosen = jax.random.randint(jax.random.fold_in(shared_key, 1), (), 0, ceilings.size)
    flattened = jnp.where(jnp.arange(ceilings.size) == chosen, 256, ceilings.reshape(-1))
    return spread_blocks(flattened.reshape(ceilings.shape))


def plant_values(key, values, planted):
    volume = NZ * NY * CX
    anchor = jax.random.randint(key, (), 0, volume - len(planted))
    flattened = values.reshape(-1)
    position = jnp.arange(volume)
    for offset, amount in enumerate(planted):
        flattened = jnp.where(position == anchor + offset, amount, flattened)
    return flattened.reshape(values.shape)


def affinity_field(key, constant):
    ceilings = shared_strength(key)
    own_key = jax.random.fold_in(key, constant)
    values = jax.random.randint(own_key, (NZ, NY, CX), 0, ceilings)
    return plant_values(jax.random.fold_in(own_key, 7), values, (255, 0))


def draw_initial_class_tags(key, part):
    key = jax.random.fold_in(key, 3)
    density = spread_blocks(region_table(jax.random.fold_in(key, 1), 2, 33))
    chance = jax.random.randint(jax.random.fold_in(key, 2), (NZ, NY, CX), 0, 64)
    labeled = jax.random.randint(jax.random.fold_in(key, 4), (NZ, NY, CX), 0, 4)
    unlabeled = jax.random.randint(jax.random.fold_in(key, 5), (NZ, NY, CX), 4, 16)
    labels = jnp.where(chance < density, labeled, unlabeled)
    return plant_values(jax.random.fold_in(key, 6), labels, (15, 0, 1, 2, 3))


def draw_depth_affinity(key, part):
    return affinity_field(key, 11)


def draw_row_affinity(key, part):
    return affinity_field(key, 13)


def draw_column_affinity(key, part):
    return affinity_field(key, 17)


def setup_inputs(seed: int = 0, part: int = 0) -> dict:
    seeds = jax.random.split(jax.random.key(seed), 5)
    part_keys = jax.random.split(jax.random.fold_in(seeds[4], part), 5)
    initial_class_tags = draw_initial_class_tags(jax.random.fold_in(jax.random.fold_in(seeds[4], part), 71), part)
    depth_affinity = draw_depth_affinity(jax.random.fold_in(jax.random.fold_in(seeds[4], part), 71), part)
    row_affinity = draw_row_affinity(jax.random.fold_in(jax.random.fold_in(seeds[4], part), 71), part)
    column_affinity = draw_column_affinity(jax.random.fold_in(jax.random.fold_in(seeds[4], part), 71), part)
    return dict(initial_class_tags=initial_class_tags, depth_affinity=depth_affinity, row_affinity=row_affinity, column_affinity=column_affinity)


def next_along(coupling_strengths, axis):
    rest = lax.slice_in_dim(coupling_strengths, 1, coupling_strengths.shape[axis], axis=axis)
    zeros = jnp.zeros_like(lax.slice_in_dim(coupling_strengths, 0, 1, axis=axis))
    return jnp.concatenate([rest, zeros], axis)

def prev_along(coupling_strengths, axis):
    rest = lax.slice_in_dim(coupling_strengths, 0, coupling_strengths.shape[axis] - 1, axis=axis)
    zeros = jnp.zeros_like(lax.slice_in_dim(coupling_strengths, 0, 1, axis=axis))
    return jnp.concatenate([zeros, rest], axis)

def gram(left, linear_system_source):
    return jnp.einsum('izyx,jzyx->ij', left, linear_system_source, precision=lax.Precision.HIGHEST)

def combine(coupling_strengths, coeffs):
    return jnp.einsum('kzyx,kc->czyx', coupling_strengths, coeffs, precision=lax.Precision.HIGHEST)

def solve_small(matrix, target):
    factor = jnp.linalg.cholesky(matrix)
    return jax.scipy.linalg.cho_solve((factor, True), target)

def reference(initial_class_tags, depth_affinity, row_affinity, column_affinity):
    free_point_flags = (initial_class_tags >= 4).astype(jnp.float32)
    marked_point_flags = jnp.stack([(initial_class_tags == c).astype(jnp.float32) for c in range(LABELS)])
    shape = initial_class_tags.shape
    zpos = lax.broadcasted_iota(jnp.int32, shape, 0)
    ypos = lax.broadcasted_iota(jnp.int32, shape, 1)
    xpos = lax.broadcasted_iota(jnp.int32, shape, 2)
    weight_z = jnp.where(zpos < NZ - 1, (depth_affinity.astype(jnp.float32) + 1.0) / 256.0, 0.0)
    weight_y = jnp.where(ypos < NY - 1, (row_affinity.astype(jnp.float32) + 1.0) / 256.0, 0.0)
    weight_x = jnp.where(xpos < CX - 1, (column_affinity.astype(jnp.float32) + 1.0) / 256.0, 0.0)
    back_z = prev_along(weight_z, 0)
    back_y = prev_along(weight_y, 1)
    back_x = prev_along(weight_x, 2)
    node_strength_entries = weight_z + back_z + weight_y + back_y + weight_x + back_x

    def adjacent_sample(coupling_strengths):
        total = weight_z * next_along(coupling_strengths, 1) + back_z * prev_along(coupling_strengths, 1)
        total = total + weight_y * next_along(coupling_strengths, 2) + back_y * prev_along(coupling_strengths, 2)
        total = total + weight_x * next_along(coupling_strengths, 3) + back_x * prev_along(coupling_strengths, 3)
        return total

    def operate(coupling_strengths):
        return free_point_flags * (node_strength_entries * coupling_strengths - adjacent_sample(coupling_strengths))
    linear_system_source = free_point_flags * adjacent_sample(marked_point_flags)
    solution = jnp.zeros_like(linear_system_source)
    residual = linear_system_source
    search_direction = linear_system_source
    gram_rr = gram(residual, residual)
    for step in range(ITERS):
        grey_level_image = operate(search_direction)
        gram_pq = gram(search_direction, grey_level_image)
        alpha = solve_small(gram_pq, gram_rr)
        solution = solution + combine(search_direction, alpha)
        residual = residual - combine(grey_level_image, alpha)
        gram_next = gram(residual, residual)
        beta = solve_small(gram_rr, gram_next)
        search_direction = residual + combine(search_direction, beta)
        gram_rr = gram_next
    return solution + marked_point_flags
```

```python
import functools

import jax
import jax.numpy as jnp
from jax import lax
from jax.experimental import pallas as pl
from jax.experimental.pallas import tpu as pltpu
from jax.sharding import PartitionSpec as P

LABELS = 4
PIVOT_FLOOR = 1e-7
LO, HI = 3, 4
VMEM = pltpu.VMEM


def even_partner(i, count):
    return i ^ 1 if (i ^ 1) < count else i


def odd_partner(i, count):
    j = ((i + 1) ^ 1) - 1
    return j if 0 <= j < count else i


def exchanged(array, axes, counts, pair):
    nz, ny = counts
    route = []
    for z in range(nz):
        for y in range(ny):
            pz, py = pair(z, y)
            if (pz, py) != (z, y):
                route.append((z * ny + y, pz * ny + py))
    return lax.ppermute(array, axes, route)


def pack_kernel(tags, wz, wy, wx, z_even, z_odd, y_even, y_odd, *corners):
    zi, yi = lax.axis_index("gz"), lax.axis_index("gy")
    depth, rows, cols = tags.shape
    z_is_odd, y_is_odd = zi % 2, yi % 2
    row = lax.broadcasted_iota(jnp.int32, (8, cols), 0)
    for up, out in ((1 - z_is_odd, z_even), (z_is_odd, z_odd)):
        start = up * (depth - 4)
        for i in range(4):
            out[i] = tags[start + i]
        start = up * (depth - 3)
        for a, ref in enumerate((wz, wy, wx)):
            for i in range(3):
                out[4 + 3 * a + i] = ref[start + i]

    def strips(sources, up, out):
        tile = pl.multiple_of(up * (rows - 8), 8)
        first = (row >= 4) == (up == 1)
        for k in range(0, len(sources), 2):
            (ra, pa), (rb, pb) = sources[k], sources[k + 1]
            a = ra[pa, pl.ds(tile, 8), :]
            b = rb[pb, pl.ds(tile, 8), :]
            out[k // 2] = jnp.where(first, a, pltpu.roll(b, 4, 0))

    y_ups = (1 - y_is_odd, y_is_odd)
    z_ups = (1 - z_is_odd, z_is_odd)
    for up, out in zip(y_ups, (y_even, y_odd)):
        strips([(ref, p) for ref in (tags, wz, wy, wx) for p in range(depth)], up, out)
    for n, out in enumerate(corners):
        z_up, y_up = z_ups[n // 2], y_ups[n % 2]
        sources = []
        for ref, width in ((tags, 3), (wz, 3), (wy, 2), (wx, 2)):
            start = z_up * (depth - width)
            sources += [(ref, start + i) for i in range(width)]
        strips(sources, y_up, out)


def pack(tags, wz, wy, wx):
    depth, rows, cols = tags.shape
    i32 = jnp.int32
    return pl.pallas_call(
        pack_kernel,
        out_shape=[jax.ShapeDtypeStruct((13, rows, cols), i32)] * 2
        + [jax.ShapeDtypeStruct((2 * depth, 8, cols), i32)] * 2
        + [jax.ShapeDtypeStruct((5, 8, cols), i32)] * 4,
        in_specs=[pl.BlockSpec(memory_space=VMEM)] * 4,
        out_specs=[pl.BlockSpec(memory_space=VMEM)] * 8,
        compiler_params=pltpu.CompilerParams(vmem_limit_bytes=16 * 2**20),
    )(tags, wz, wy, wx)


def krylov_kernel(
    counts, tags, wz, wy, wx, z_even, z_odd, y_even, y_odd, c_ee, c_eo, c_oe, c_oo,
    fields, moments,
    t_pad, w_pad, coef, b_pad, v1, v2, sums,
):
    nz, ny = counts
    zi, yi = lax.axis_index("gz"), lax.axis_index("gy")
    depth, rows, cols = tags.shape
    z_is_even, y_is_even = zi % 2 == 0, yi % 2 == 0
    wide = rows + 8
    f32 = jnp.float32
    half = lax.broadcasted_iota(jnp.int32, (8, cols), 0) < 4
    row = lax.broadcasted_iota(jnp.int32, (wide, cols), 0)
    col = lax.broadcasted_iota(jnp.int32, (wide, cols), 1)
    own = slice(0, rows)
    ring = slice(rows, wide)

    def weight(values):
        return (values.astype(f32) + 1.0) * (1.0 / 256.0)

    def put(a, plane, where, values):
        if a == 0:
            t_pad[plane, where, :] = values
        else:
            w_pad[a - 1, plane, where, :] = weight(values)

    def strip_pair(from_next, from_prev):
        first = jnp.where(half, from_next, from_prev)
        second = pltpu.roll(jnp.where(half, from_prev, from_next), 4, 0)
        return first, second

    arrays = (tags, wz, wy, wx)
    for a, ref in enumerate(arrays):
        for p in range(depth):
            put(a, LO + p, own, ref[p])
    for i in range(13):
        e, o = z_even[i], z_odd[i]
        after = jnp.where(z_is_even, e, o)
        before = jnp.where(z_is_even, o, e)
        if i < 4:
            put(0, LO + depth + i, own, after)
            if i >= 1:
                put(0, i - 1, own, before)
        else:
            a, k = 1 + (i - 4) // 3, (i - 4) % 3
            put(a, LO + depth + k, own, after)
            put(a, k, own, before)
    for k in range(2 * depth):
        e, o = y_even[k], y_odd[k]
        pair = strip_pair(jnp.where(y_is_even, e, o), jnp.where(y_is_even, o, e))
        for j in range(2):
            a, p = divmod(2 * k + j, depth)
            put(a, LO + p, ring, pair[j])
    places = [(0, 0), (0, 1), (0, 2), (1, 0), (1, 1), (1, 2), (2, 0), (2, 1), (3, 0), (3, 1)]
    for k in range(5):
        ee, eo, oe, oo = c_ee[k], c_eo[k], c_oe[k], c_oo[k]
        e_next, e_prev = jnp.where(y_is_even, ee, eo), jnp.where(y_is_even, eo, ee)
        o_next, o_prev = jnp.where(y_is_even, oe, oo), jnp.where(y_is_even, oo, oe)
        after = strip_pair(
            jnp.where(z_is_even, e_next, o_next), jnp.where(z_is_even, e_prev, o_prev)
        )
        before = strip_pair(
            jnp.where(z_is_even, o_next, e_next), jnp.where(z_is_even, o_prev, e_prev)
        )
        for j in range(2):
            a, i = places[2 * k + j]
            put(a, LO + depth + i, ring, after[j])
            put(a, i + (1 if a >= 2 else 0), ring, before[j])
    zero_tile = jnp.zeros((8, cols), jnp.int32)
    put(0, LO + depth + 3, ring, zero_tile)
    put(1, LO + depth + 2, ring, zero_tile)
    for a in (2, 3):
        put(a, LO + depth + 2, ring, zero_tile)
        put(a, 0, ring, zero_tile)

    w_pad[0, LO + depth - 1] = jnp.where(zi == nz - 1, 0.0, w_pad[0, LO + depth - 1])
    w_pad[0, LO - 1] = jnp.where(zi == 0, 0.0, w_pad[0, LO - 1])
    last_row = jnp.where(yi == ny - 1, rows - 1, -1)
    first_row = jnp.where(yi == 0, wide - 1, -1)
    y_cut = (row == last_row) | (row == first_row)
    x_cut = col == cols - 1

    def prepare(p, _):
        tag = t_pad[p]
        w_z, w_zb = w_pad[0, p], w_pad[0, p - 1]
        w_y = jnp.where(y_cut, 0.0, w_pad[1, p])
        w_x = jnp.where(x_cut, 0.0, w_pad[2, p])
        w_yb, w_xb = pltpu.roll(w_y, 1, 0), pltpu.roll(w_x, 1, 1)
        free = tag >= 4
        degree = (w_z + w_zb) + (w_y + w_yb) + (w_x + w_xb)
        weights = [jnp.where(free, w, 0.0) for w in (w_z, w_zb, w_y, w_yb, w_x, w_xb, degree)]
        for i, w in enumerate(weights):
            coef[i, p] = w
        near = (
            t_pad[p + 1], t_pad[p - 1],
            pltpu.roll(tag, wide - 1, 0), pltpu.roll(tag, 1, 0),
            pltpu.roll(tag, cols - 1, 1), pltpu.roll(tag, 1, 1),
        )
        for c in range(LABELS):
            terms = [jnp.where(n == c, w, 0.0) for n, w in zip(near, weights)]
            b_pad[c, p] = (terms[0] + terms[1]) + (terms[2] + terms[3]) + (terms[4] + terms[5])
        return 0

    lax.fori_loop(1, LO + depth + 3, prepare, 0)

    def apply(source, target):
        def body(p, _):
            for c in range(LABELS):
                v = source[c, p]
                z = coef[0, p] * source[c, p + 1] + coef[1, p] * source[c, p - 1]
                y = coef[2, p] * pltpu.roll(v, wide - 1, 0) + coef[3, p] * pltpu.roll(v, 1, 0)
                x = coef[4, p] * pltpu.roll(v, cols - 1, 1) + coef[5, p] * pltpu.roll(v, 1, 1)
                target[c, p] = coef[6, p] * v - (z + y + x)
            return 0
        return body

    lax.fori_loop(2, LO + depth + 2, apply(b_pad, v1), 0)
    lax.fori_loop(3, LO + depth + 1, apply(v1, v2), 0)

    spots = [(r, l) for r in range(0, rows, 8) for l in range(0, cols, 128)]
    half_pairs = [(a, b) for a in range(LABELS) for b in range(a, LABELS)]
    all_pairs = [(a, b) for a in range(LABELS) for b in range(LABELS)]

    def block(ref, c, p, spot):
        return ref[c, p, spot[0] : spot[0] + 8, spot[1] : spot[1] + 128]

    def total(products):
        while len(products) > 1:
            products = [x + y for x, y in zip(products[::2], products[1::2])] + (
                [products[-1]] if len(products) % 2 else []
            )
        return products[0]

    def accumulate(p, acc):
        parts = [[] for _ in acc]
        for spot in spots:
            b = [block(b_pad, c, p, spot) for c in range(LABELS)]
            ab = [block(v1, c, p, spot) for c in range(LABELS)]
            products = [b[i] * b[j] for i, j in half_pairs]
            products += [b[i] * ab[j] for i, j in half_pairs]
            products += [ab[i] * ab[j] for i, j in half_pairs]
            for part, product in zip(parts, products):
                part.append(product)
            for c in range(LABELS):
                where = (p - LO, slice(spot[0], spot[0] + 8), slice(spot[1], spot[1] + 128))
                fields[(0, c) + where] = b[c]
                fields[(1, c) + where] = ab[c]
        return tuple(x + total(part) for x, part in zip(acc, parts))

    def accumulate_last(p, acc):
        parts = [[] for _ in acc]
        ahead = []
        for c in range(LABELS):
            v = v2[c, p]
            n = coef[0, p] * v2[c, p + 1] + coef[2, p] * pltpu.roll(v, wide - 1, 0)
            n = n + coef[4, p] * pltpu.roll(v, cols - 1, 1)
            ahead.append(coef[6, p] * v - 2.0 * n)
        for spot in spots:
            cut = (slice(spot[0], spot[0] + 8), slice(spot[1], spot[1] + 128))
            ab = [block(v1, c, p, spot) for c in range(LABELS)]
            aab = [block(v2, c, p, spot) for c in range(LABELS)]
            q = [x[cut] for x in ahead]
            products = [ab[i] * aab[j] for i, j in half_pairs]
            products += [aab[i] * aab[j] for i, j in half_pairs]
            products += [aab[i] * q[j] for i, j in all_pairs]
            for part, product in zip(parts, products):
                part.append(product)
            for c in range(LABELS):
                fields[(2, c, p - LO) + cut] = aab[c]
        return tuple(x + total(part) for x, part in zip(acc, parts))

    zero = jnp.zeros((8, 128), f32)
    low = lax.fori_loop(LO, LO + depth, accumulate, (zero,) * 30)
    high = lax.fori_loop(LO, LO + depth, accumulate_last, (zero,) * 36)
    kept = {}
    for k in range(5):
        part = low[10 * k : 10 * k + 10] if k < 3 else high[10 * (k - 3) : 10 * (k - 3) + 10]
        for (a, b), x in zip(half_pairs, part):
            kept[k, a, b] = kept[k, b, a] = x
    last = dict(zip(all_pairs, high[20:]))
    for a, b in half_pairs:
        kept[5, a, b] = kept[5, b, a] = 0.5 * (last[a, b] + last[b, a])
    for k in range(6):
        for a, b in half_pairs:
            x = jnp.sum(kept[k, a, b], axis=0, keepdims=True)
            for i, j in {(a, b), (b, a)}:
                at = (2 * k + j // 2) * 8 + (j % 2) * 4 + i
                sums[at : at + 1, :] = x
    lane = lax.broadcasted_iota(jnp.int32, (8, 128), 1)
    packed = zero
    for g in range(12):
        x = jnp.sum(sums[8 * g : 8 * g + 8, :], axis=1, keepdims=True)
        packed = jnp.where(lane == g, x, packed)
    moments[...] = packed


def krylov(counts, arrays, halos):
    depth, rows, cols = arrays[0].shape
    planes, wide = depth + LO + HI, rows + 8
    f32 = jnp.float32
    return pl.pallas_call(
        functools.partial(krylov_kernel, counts),
        out_shape=[
            jax.ShapeDtypeStruct((3, LABELS, depth, rows, cols), f32),
            jax.ShapeDtypeStruct((8, 128), f32),
        ],
        in_specs=[pl.BlockSpec(memory_space=VMEM)] * 12,
        out_specs=[pl.BlockSpec(memory_space=VMEM)] * 2,
        scratch_shapes=[
            VMEM((planes, wide, cols), jnp.int32),
            VMEM((3, planes, wide, cols), f32),
            VMEM((7, planes, wide, cols), f32),
            VMEM((LABELS, planes, wide, cols), f32),
            VMEM((LABELS, planes, wide, cols), f32),
            VMEM((LABELS, planes, wide, cols), f32),
            VMEM((96, 128), f32),
        ],
        compiler_params=pltpu.CompilerParams(vmem_limit_bytes=48 * 2**20),
    )(*arrays, *halos)


def combine_kernel(mine, theirs, fields, tags, out, coeffs):
    f32 = jnp.float32
    depth, rows, cols = tags.shape
    sums = mine[...] + theirs[...]
    lane = lax.broadcasted_iota(jnp.int32, (8, 128), 1)
    row = lax.broadcasted_iota(jnp.int32, (8, 128), 0)

    def splat(column):
        return jnp.broadcast_to(column, (8, 128))

    columns = {}
    for k in range(6):
        for h in range(2):
            x = splat(sums[:, 2 * k + h : 2 * k + h + 1])
            columns[k, 2 * h] = x
            columns[k, 2 * h + 1] = pltpu.roll(x, 4, 0)
    blocks = []
    for i in range(3):
        x = jnp.zeros((8, 128), f32)
        for j, k in enumerate((i + 1, i + 2, i + 3, i)):
            for b in range(LABELS):
                x = jnp.where(lane == 4 * j + b, columns[k, b], x)
        blocks.append(x)
    system = [
        jnp.where(row < 4, blocks[0], pltpu.roll(blocks[1], 4, 0)),
        jnp.where(row < 4, blocks[2], 0.0),
    ]
    start = list(system)
    for k in range(3 * LABELS):
        n, r = divmod(k, 8)
        pivot_row = system[n][r : r + 1, :]
        pivot = pivot_row[:, k : k + 1]
        sound = pivot > PIVOT_FLOOR * start[n][r : r + 1, k : k + 1]
        scale = jnp.where(sound, 1.0 / jnp.where(sound, pivot, 1.0), 0.0)
        pivot_row = pivot_row * scale
        for m in range(2):
            x = system[m] - system[m][:, k : k + 1] * pivot_row
            system[m] = jnp.where(row == r, pivot_row, x) if m == n else x
    for c in range(LABELS):
        for m in range(2):
            at = 3 * LABELS + c
            coeffs[c, 8 * m : 8 * m + 8, :] = splat(system[m][:, at : at + 1])

    for first in range(0, LABELS, 2):
        weights = {
            (c, k): jnp.broadcast_to(coeffs[c, k : k + 1, :], (8, 128))
            for c in (first, first + 1)
            for k in range(3 * LABELS)
        }

        def body(p, _):
            for r in range(0, rows, 8):
                for l in range(0, cols, 128):
                    cut = (p, slice(r, r + 8), slice(l, l + 128))
                    v = [fields[(k // LABELS, k % LABELS) + cut] for k in range(3 * LABELS)]
                    tag = tags[cut]
                    for c in (first, first + 1):
                        s = [v[k] * weights[c, k] for k in range(3 * LABELS)]
                        while len(s) > 1:
                            s = [x + y for x, y in zip(s[::2], s[1::2])] + (
                                [s[-1]] if len(s) % 2 else []
                            )
                        out[(c,) + cut] = jnp.where(tag == c, 1.0, s[0])
            return 0

        lax.fori_loop(0, depth, body, 0)


def combined(mine, theirs, fields, tags):
    return pl.pallas_call(
        combine_kernel,
        out_shape=jax.ShapeDtypeStruct((LABELS,) + tags.shape, jnp.float32),
        in_specs=[pl.BlockSpec(memory_space=VMEM)] * 4,
        out_specs=pl.BlockSpec(memory_space=VMEM),
        scratch_shapes=[VMEM((LABELS, 16, 128), jnp.float32)],
        compiler_params=pltpu.CompilerParams(vmem_limit_bytes=32 * 2**20),
    )(mine, theirs, fields, tags)


def per_device(counts, tags, depth_affinity, row_affinity, column_affinity):
    nz, ny = counts
    arrays = (tags, depth_affinity, row_affinity, column_affinity)
    axes = ("gz", "gy")
    packed = pack(*arrays)
    ze, zo = (lambda z: even_partner(z, nz)), (lambda z: odd_partner(z, nz))
    ye, yo = (lambda y: even_partner(y, ny)), (lambda y: odd_partner(y, ny))

    def z_pair(pz):
        return lambda z, y: (pz(z), y) if pz(z) != z else (z, ye(y))

    def y_pair(py):
        return lambda z, y: (z, py(y)) if py(y) != y else (ze(z), y)

    def corner(pz, py):
        def pair(z, y):
            if pz(z) != z and py(y) != y:
                return pz(z), py(y)
            return (pz(z), y) if pz(z) != z else (z, ye(y))
        return pair

    pairs = [z_pair(ze), z_pair(zo), y_pair(ye), y_pair(yo)]
    pairs += [corner(a, b) for a in (ze, zo) for b in (ye, yo)]
    halos = [exchanged(x, axes, counts, pair) for x, pair in zip(packed, pairs)]
    fields, moments = krylov(counts, arrays, halos)

    steps = [lambda z, y, d=d: (z, y ^ d) for d in powers(ny)]
    steps += [lambda z, y, d=d: (z ^ d, y) for d in powers(nz)]
    for n, pair in enumerate(steps):
        theirs = exchanged(moments, axes, counts, pair)
        if n < len(steps) - 1:
            moments = moments + theirs
    return combined(moments, theirs, fields, tags)


def powers(count):
    return [1 << n for n in range(count.bit_length() - 1)]


def solution(mesh):
    counts = (mesh.shape["gz"], mesh.shape["gy"])
    placed = P(("parts", "gz"), "gy", None)
    return jax.shard_map(
        functools.partial(per_device, counts),
        mesh=mesh,
        in_specs=(placed,) * 4,
        out_specs=P(None, ("parts", "gz"), "gy", None),
        check_vma=False,
    )
```

```python
import functools

import jax
import jax.numpy as jnp
from jax import lax
from jax.experimental import pallas as pl
from jax.experimental.pallas import tpu as pltpu
from jax.sharding import PartitionSpec as P

LABELS = 4
PIVOT_FLOOR = 1e-7
LO, HI = 3, 4
CORNER_WIDTHS = (3, 3, 2, 2)
CORNERS = [(a, i) for a, width in enumerate(CORNER_WIDTHS) for i in range(width)]
VMEM = pltpu.VMEM


def even_partner(i, count):
    return i ^ 1 if (i ^ 1) < count else i


def odd_partner(i, count):
    j = ((i + 1) ^ 1) - 1
    return j if 0 <= j < count else i


def exchanged(array, axes, counts, pair):
    nz, ny = counts
    route = []
    for z in range(nz):
        for y in range(ny):
            pz, py = pair(z, y)
            if (pz, py) != (z, y):
                route.append((z * ny + y, pz * ny + py))
    return lax.ppermute(array, axes, route)


def pack_kernel(tags_hbm, wz_hbm, wy_hbm, wx_hbm, tags, wz, wy, wx, z_even, z_odd, y_even, y_odd, sems):
    zi, yi = lax.axis_index("gz"), lax.axis_index("gy")
    depth, rows, cols = tags.shape
    hbm, own = (tags_hbm, wz_hbm, wy_hbm, wx_hbm), (tags, wz, wy, wx)
    copies = [pltpu.make_async_copy(h, o, sems.at[n]) for n, (h, o) in enumerate(zip(hbm, own))]
    for copy in copies:
        copy.start()
    for copy in copies:
        copy.wait()
    z_is_odd, y_is_odd = zi % 2, yi % 2
    row = lax.broadcasted_iota(jnp.int32, (8, cols), 0)
    for up, out in ((1 - z_is_odd, z_even), (z_is_odd, z_odd)):
        start = up * (depth - 4)
        for i in range(4):
            out[i] = tags[start + i]
        start = up * (depth - 3)
        for a, ref in enumerate((wz, wy, wx)):
            for i in range(3):
                out[4 + 3 * a + i] = ref[start + i]
    for up, out in ((1 - y_is_odd, y_even), (y_is_odd, y_odd)):
        tile = pl.multiple_of(up * (rows - 8), 8)
        first = (row >= 4) == (up == 1)
        for k in range(2 * depth):
            ref, p = own[2 * k // depth], 2 * k % depth
            a, b = ref[p, pl.ds(tile, 8), :], ref[p + 1, pl.ds(tile, 8), :]
            out[k] = jnp.where(first, a, pltpu.roll(b, 4, 0))


def pack(*arrays):
    depth, rows, cols = arrays[0].shape
    i32 = jnp.int32
    return pl.pallas_call(
        pack_kernel,
        out_shape=[jax.ShapeDtypeStruct((depth, rows, cols), i32)] * 4
        + [jax.ShapeDtypeStruct((13, rows, cols), i32)] * 2
        + [jax.ShapeDtypeStruct((2 * depth, 8, cols), i32)] * 2,
        in_specs=[pl.BlockSpec(memory_space=pltpu.HBM)] * 4,
        out_specs=[pl.BlockSpec(memory_space=VMEM)] * 8,
        scratch_shapes=[pltpu.SemaphoreType.DMA((4,))],
        compiler_params=pltpu.CompilerParams(vmem_limit_bytes=16 * 2**20),
    )(*arrays)


def ring_kernel(y_even, y_odd, rings, z_even, z_odd):
    zi, yi = lax.axis_index("gz"), lax.axis_index("gy")
    cols = rings.shape[2]
    depth = rings.shape[0] // 4
    half = lax.broadcasted_iota(jnp.int32, (8, cols), 0) < 4
    from_next = half == (yi % 2 == 0)
    for k in range(2 * depth):
        e, o = y_even[k], y_odd[k]
        rings[2 * k] = jnp.where(from_next, e, o)
        rings[2 * k + 1] = pltpu.roll(jnp.where(from_next, o, e), 4, 0)
    z_is_odd = zi % 2
    for up, out in ((1 - z_is_odd, z_even), (z_is_odd, z_odd)):
        for n, (a, i) in enumerate(CORNERS):
            out[n] = rings[a * depth + up * (depth - CORNER_WIDTHS[a]) + i]


def make_rings(y_even, y_odd):
    tiles, _, cols = y_even.shape
    i32 = jnp.int32
    return pl.pallas_call(
        ring_kernel,
        out_shape=[jax.ShapeDtypeStruct((2 * tiles, 8, cols), i32)]
        + [jax.ShapeDtypeStruct((len(CORNERS), 8, cols), i32)] * 2,
        in_specs=[pl.BlockSpec(memory_space=VMEM)] * 2,
        out_specs=[pl.BlockSpec(memory_space=VMEM)] * 3,
        compiler_params=pltpu.CompilerParams(vmem_limit_bytes=16 * 2**20),
    )(y_even, y_odd)


def krylov_kernel(
    counts, tags, wz, wy, wx, z_even, z_odd, rings, c_even, c_odd,
    fields, moments,
    t_pad, w_pad, coef, b_pad, v1, v2, sums,
):
    nz, ny = counts
    zi, yi = lax.axis_index("gz"), lax.axis_index("gy")
    depth, rows, cols = tags.shape
    z_is_even = zi % 2 == 0
    wide = rows + 8
    f32 = jnp.float32
    row = lax.broadcasted_iota(jnp.int32, (wide, cols), 0)
    col = lax.broadcasted_iota(jnp.int32, (wide, cols), 1)
    own = slice(0, rows)
    ring = slice(rows, wide)

    def weight(values):
        return (values.astype(f32) + 1.0) * (1.0 / 256.0)

    def put(a, plane, where, values):
        if a == 0:
            t_pad[plane, where, :] = values
        else:
            w_pad[a - 1, plane, where, :] = weight(values)

    arrays = (tags, wz, wy, wx)
    for a, ref in enumerate(arrays):
        for p in range(depth):
            put(a, LO + p, own, ref[p])
    for i in range(13):
        e, o = z_even[i], z_odd[i]
        after = jnp.where(z_is_even, e, o)
        before = jnp.where(z_is_even, o, e)
        if i < 4:
            put(0, LO + depth + i, own, after)
            if i >= 1:
                put(0, i - 1, own, before)
        else:
            a, k = 1 + (i - 4) // 3, (i - 4) % 3
            put(a, LO + depth + k, own, after)
            put(a, k, own, before)
    for a in range(4):
        for p in range(depth):
            put(a, LO + p, ring, rings[a * depth + p])
    for n, (a, i) in enumerate(CORNERS):
        e, o = c_even[n], c_odd[n]
        put(a, LO + depth + i, ring, jnp.where(z_is_even, e, o))
        put(a, LO - CORNER_WIDTHS[a] + i, ring, jnp.where(z_is_even, o, e))
    zero_tile = jnp.zeros((8, cols), jnp.int32)
    put(0, LO + depth + 3, ring, zero_tile)
    put(1, LO + depth + 2, ring, zero_tile)
    for a in (2, 3):
        put(a, LO + depth + 2, ring, zero_tile)
        put(a, 0, ring, zero_tile)

    w_pad[0, LO + depth - 1] = jnp.where(zi == nz - 1, 0.0, w_pad[0, LO + depth - 1])
    w_pad[0, LO - 1] = jnp.where(zi == 0, 0.0, w_pad[0, LO - 1])
    last_row = jnp.where(yi == ny - 1, rows - 1, -1)
    first_row = jnp.where(yi == 0, wide - 1, -1)
    y_cut = (row == last_row) | (row == first_row)
    x_cut = col == cols - 1

    def prepare(p, _):
        tag = t_pad[p]
        w_z, w_zb = w_pad[0, p], w_pad[0, p - 1]
        w_y = jnp.where(y_cut, 0.0, w_pad[1, p])
        w_x = jnp.where(x_cut, 0.0, w_pad[2, p])
        w_yb, w_xb = pltpu.roll(w_y, 1, 0), pltpu.roll(w_x, 1, 1)
        free = tag >= 4
        degree = (w_z + w_zb) + (w_y + w_yb) + (w_x + w_xb)
        weights = [jnp.where(free, w, 0.0) for w in (w_z, w_zb, w_y, w_yb, w_x, w_xb, degree)]
        for i, w in enumerate(weights):
            coef[i, p] = w
        near = (
            t_pad[p + 1], t_pad[p - 1],
            pltpu.roll(tag, wide - 1, 0), pltpu.roll(tag, 1, 0),
            pltpu.roll(tag, cols - 1, 1), pltpu.roll(tag, 1, 1),
        )
        for c in range(LABELS):
            terms = [jnp.where(n == c, w, 0.0) for n, w in zip(near, weights)]
            b_pad[c, p] = (terms[0] + terms[1]) + (terms[2] + terms[3]) + (terms[4] + terms[5])
        return 0

    lax.fori_loop(1, LO + depth + 3, prepare, 0)

    def apply(source, target):
        def body(p, _):
            for c in range(LABELS):
                v = source[c, p]
                z = coef[0, p] * source[c, p + 1] + coef[1, p] * source[c, p - 1]
                y = coef[2, p] * pltpu.roll(v, wide - 1, 0) + coef[3, p] * pltpu.roll(v, 1, 0)
                x = coef[4, p] * pltpu.roll(v, cols - 1, 1) + coef[5, p] * pltpu.roll(v, 1, 1)
                target[c, p] = coef[6, p] * v - (z + y + x)
            return 0
        return body

    lax.fori_loop(2, LO + depth + 2, apply(b_pad, v1), 0)
    lax.fori_loop(3, LO + depth + 1, apply(v1, v2), 0)

    spots = [(r, l) for r in range(0, rows, 8) for l in range(0, cols, 128)]
    half_pairs = [(a, b) for a in range(LABELS) for b in range(a, LABELS)]
    all_pairs = [(a, b) for a in range(LABELS) for b in range(LABELS)]

    def block(ref, c, p, spot):
        return ref[c, p, spot[0] : spot[0] + 8, spot[1] : spot[1] + 128]

    def total(products):
        while len(products) > 1:
            products = [x + y for x, y in zip(products[::2], products[1::2])] + (
                [products[-1]] if len(products) % 2 else []
            )
        return products[0]

    def accumulate(p, acc):
        parts = [[] for _ in acc]
        for spot in spots:
            b = [block(b_pad, c, p, spot) for c in range(LABELS)]
            ab = [block(v1, c, p, spot) for c in range(LABELS)]
            products = [b[i] * b[j] for i, j in half_pairs]
            products += [b[i] * ab[j] for i, j in half_pairs]
            products += [ab[i] * ab[j] for i, j in half_pairs]
            for part, product in zip(parts, products):
                part.append(product)
            for c in range(LABELS):
                where = (p - LO, slice(spot[0], spot[0] + 8), slice(spot[1], spot[1] + 128))
                fields[(0, c) + where] = b[c]
                fields[(1, c) + where] = ab[c]
        return tuple(x + total(part) for x, part in zip(acc, parts))

    def accumulate_last(p, acc):
        parts = [[] for _ in acc]
        ahead = []
        for c in range(LABELS):
            v = v2[c, p]
            n = coef[0, p] * v2[c, p + 1] + coef[2, p] * pltpu.roll(v, wide - 1, 0)
            n = n + coef[4, p] * pltpu.roll(v, cols - 1, 1)
            ahead.append(coef[6, p] * v - 2.0 * n)
        for spot in spots:
            cut = (slice(spot[0], spot[0] + 8), slice(spot[1], spot[1] + 128))
            ab = [block(v1, c, p, spot) for c in range(LABELS)]
            aab = [block(v2, c, p, spot) for c in range(LABELS)]
            q = [x[cut] for x in ahead]
            products = [ab[i] * aab[j] for i, j in half_pairs]
            products += [aab[i] * aab[j] for i, j in half_pairs]
            products += [aab[i] * q[j] for i, j in all_pairs]
            for part, product in zip(parts, products):
                part.append(product)
            for c in range(LABELS):
                fields[(2, c, p - LO) + cut] = aab[c]
        return tuple(x + total(part) for x, part in zip(acc, parts))

    zero = jnp.zeros((8, 128), f32)
    low = lax.fori_loop(LO, LO + depth, accumulate, (zero,) * 30)
    high = lax.fori_loop(LO, LO + depth, accumulate_last, (zero,) * 36)
    kept = {}
    for k in range(5):
        part = low[10 * k : 10 * k + 10] if k < 3 else high[10 * (k - 3) : 10 * (k - 3) + 10]
        for (a, b), x in zip(half_pairs, part):
            kept[k, a, b] = kept[k, b, a] = x
    last = dict(zip(all_pairs, high[20:]))
    for a, b in half_pairs:
        kept[5, a, b] = kept[5, b, a] = 0.5 * (last[a, b] + last[b, a])
    for k in range(6):
        for a, b in half_pairs:
            x = jnp.sum(kept[k, a, b], axis=0, keepdims=True)
            for i, j in {(a, b), (b, a)}:
                at = (2 * k + j // 2) * 8 + (j % 2) * 4 + i
                sums[at : at + 1, :] = x
    lane = lax.broadcasted_iota(jnp.int32, (8, 128), 1)
    packed = zero
    for g in range(12):
        x = jnp.sum(sums[8 * g : 8 * g + 8, :], axis=1, keepdims=True)
        packed = jnp.where(lane == g, x, packed)
    moments[...] = packed


def krylov(counts, arrays, halos):
    depth, rows, cols = arrays[0].shape
    planes, wide = depth + LO + HI, rows + 8
    f32 = jnp.float32
    return pl.pallas_call(
        functools.partial(krylov_kernel, counts),
        out_shape=[
            jax.ShapeDtypeStruct((3, LABELS, depth, rows, cols), f32),
            jax.ShapeDtypeStruct((8, 128), f32),
        ],
        in_specs=[pl.BlockSpec(memory_space=VMEM)] * 9,
        out_specs=[pl.BlockSpec(memory_space=VMEM)] * 2,
        scratch_shapes=[
            VMEM((planes, wide, cols), jnp.int32),
            VMEM((3, planes, wide, cols), f32),
            VMEM((7, planes, wide, cols), f32),
            VMEM((LABELS, planes, wide, cols), f32),
            VMEM((LABELS, planes, wide, cols), f32),
            VMEM((LABELS, planes, wide, cols), f32),
            VMEM((96, 128), f32),
        ],
        compiler_params=pltpu.CompilerParams(vmem_limit_bytes=48 * 2**20),
    )(*arrays, *halos)


def combine_kernel(mine, theirs, fields, tags, out, coeffs):
    f32 = jnp.float32
    depth, rows, cols = tags.shape
    sums = mine[...] + theirs[...]
    lane = lax.broadcasted_iota(jnp.int32, (8, 128), 1)
    row = lax.broadcasted_iota(jnp.int32, (8, 128), 0)

    def splat(column):
        return jnp.broadcast_to(column, (8, 128))

    columns = {}
    for k in range(6):
        for h in range(2):
            x = splat(sums[:, 2 * k + h : 2 * k + h + 1])
            columns[k, 2 * h] = x
            columns[k, 2 * h + 1] = pltpu.roll(x, 4, 0)
    blocks = []
    for i in range(3):
        x = jnp.zeros((8, 128), f32)
        for j, k in enumerate((i + 1, i + 2, i + 3, i)):
            for b in range(LABELS):
                x = jnp.where(lane == 4 * j + b, columns[k, b], x)
        blocks.append(x)
    system = [
        jnp.where(row < 4, blocks[0], pltpu.roll(blocks[1], 4, 0)),
        jnp.where(row < 4, blocks[2], 0.0),
    ]
    start = list(system)
    for k in range(3 * LABELS):
        n, r = divmod(k, 8)
        pivot_row = system[n][r : r + 1, :]
        pivot = pivot_row[:, k : k + 1]
        sound = pivot > PIVOT_FLOOR * start[n][r : r + 1, k : k + 1]
        scale = jnp.where(sound, 1.0 / jnp.where(sound, pivot, 1.0), 0.0)
        pivot_row = pivot_row * scale
        for m in range(2):
            x = system[m] - system[m][:, k : k + 1] * pivot_row
            system[m] = jnp.where(row == r, pivot_row, x) if m == n else x
    for c in range(LABELS):
        for m in range(2):
            at = 3 * LABELS + c
            coeffs[c, 8 * m : 8 * m + 8, :] = splat(system[m][:, at : at + 1])

    for first in range(0, LABELS, 2):
        weights = {
            (c, k): jnp.broadcast_to(coeffs[c, k : k + 1, :], (8, 128))
            for c in (first, first + 1)
            for k in range(3 * LABELS)
        }

        def body(p, _):
            for r in range(0, rows, 8):
                for l in range(0, cols, 128):
                    cut = (p, slice(r, r + 8), slice(l, l + 128))
                    v = [fields[(k // LABELS, k % LABELS) + cut] for k in range(3 * LABELS)]
                    tag = tags[cut]
                    for c in (first, first + 1):
                        s = [v[k] * weights[c, k] for k in range(3 * LABELS)]
                        while len(s) > 1:
                            s = [x + y for x, y in zip(s[::2], s[1::2])] + (
                                [s[-1]] if len(s) % 2 else []
                            )
                        out[(c,) + cut] = jnp.where(tag == c, 1.0, s[0])
            return 0

        lax.fori_loop(0, depth, body, 0)


def combined(mine, theirs, fields, tags):
    return pl.pallas_call(
        combine_kernel,
        out_shape=jax.ShapeDtypeStruct((LABELS,) + tags.shape, jnp.float32),
        in_specs=[pl.BlockSpec(memory_space=VMEM)] * 4,
        out_specs=pl.BlockSpec(memory_space=VMEM),
        scratch_shapes=[VMEM((LABELS, 16, 128), jnp.float32)],
        compiler_params=pltpu.CompilerParams(vmem_limit_bytes=32 * 2**20),
    )(mine, theirs, fields, tags)


def per_device(counts, tags, depth_affinity, row_affinity, column_affinity):
    nz, ny = counts
    arrays = (tags, depth_affinity, row_affinity, column_affinity)
    axes = ("gz", "gy")
    *own, z_even, z_odd, y_even, y_odd = pack(*arrays)
    ze, zo = (lambda z: even_partner(z, nz)), (lambda z: odd_partner(z, nz))
    ye, yo = (lambda y: even_partner(y, ny)), (lambda y: odd_partner(y, ny))

    def z_pair(pz):
        return lambda z, y: (pz(z), y) if pz(z) != z else (z, ye(y))

    def y_pair(py):
        return lambda z, y: (z, py(y)) if py(y) != y else (ze(z), y)

    def swap(array, pair):
        return exchanged(array, axes, counts, pair)

    z_halos = [swap(z_even, z_pair(ze)), swap(z_odd, z_pair(zo))]
    rings, c_even, c_odd = make_rings(swap(y_even, y_pair(ye)), swap(y_odd, y_pair(yo)))
    corners = [swap(c_even, z_pair(ze)), swap(c_odd, z_pair(zo))]
    fields, moments = krylov(counts, own, [*z_halos, rings, *corners])

    steps = [lambda z, y: (z, y ^ 1)]
    steps += [lambda z, y, d=d: (z, y ^ d ^ 1) for d in powers(ny)[1:]]
    steps += [lambda z, y, d=d: (z ^ d, y ^ 1) for d in powers(nz)]
    for n, pair in enumerate(steps):
        theirs = swap(moments, pair)
        if n < len(steps) - 1:
            moments = moments + theirs
    return combined(moments, theirs, fields, own[0])


def powers(count):
    return [1 << n for n in range(count.bit_length() - 1)]


def solution(mesh):
    counts = (mesh.shape["gz"], mesh.shape["gy"])
    placed = P(("parts", "gz"), "gy", None)
    return jax.shard_map(
        functools.partial(per_device, counts),
        mesh=mesh,
        in_specs=(placed,) * 4,
        out_specs=P(None, ("parts", "gz"), "gy", None),
        check_vma=False,
    )
```

```python
import functools

import jax
import jax.numpy as jnp
from jax import lax
from jax.experimental import pallas as pl
from jax.experimental.pallas import tpu as pltpu
from jax.sharding import PartitionSpec as P

LABELS = 4
PIVOT_FLOOR = 1e-7
LO, HI = 3, 4
Z_WIDTHS = (4, 3, 3, 3)
Z_PLANES = [(a, i) for a, width in enumerate(Z_WIDTHS) for i in range(width)]
CORNER_WIDTHS = (3, 3, 3, 2)
CORNERS = [(a, i) for a, width in enumerate(CORNER_WIDTHS) for i in range(width)]
PAIR = 4096.0
VMEM = pltpu.VMEM


def even_partner(i, count):
    return i ^ 1 if (i ^ 1) < count else i


def odd_partner(i, count):
    j = ((i + 1) ^ 1) - 1
    return j if 0 <= j < count else i


def exchanged(array, axes, counts, pair):
    parts, nz, ny = counts
    route = []
    for p in range(parts):
        for z in range(nz):
            for y in range(ny):
                q = (p,) + pair(z, y)
                if q == (p, z, y):
                    q = (even_partner(p, parts), z, y)
                source, target = ((a * nz + b) * ny + c for a, b, c in ((p, z, y), q))
                if source != target:
                    route.append((source, target))
    return lax.ppermute(array, axes, route)


def tile_pairs(sources, up, out):
    rows, cols = sources[0][0].shape[-2:]
    row = lax.broadcasted_iota(jnp.int32, (8, cols), 0)
    tile = pl.multiple_of(up * (rows - 8), 8)
    first = (row >= 4) == (up == 1)
    for k in range(0, len(sources), 2):
        (ra, *pa), (rb, *pb) = sources[k], sources[min(k + 1, len(sources) - 1)]
        a = ra[(*pa, pl.ds(tile, 8), slice(None))]
        b = rb[(*pb, pl.ds(tile, 8), slice(None))]
        out[k // 2] = jnp.where(first, a, pltpu.roll(b, 4, 0))


def pack_kernel(arrays, z_even, z_odd, y_odd, d_even, d_odd):
    z_is_odd, y_is_odd = lax.axis_index("gz") % 2, lax.axis_index("gy") % 2
    depth = arrays.shape[1]
    z_ups, y_ups = (1 - z_is_odd, z_is_odd), (1 - y_is_odd, y_is_odd)
    for up, out in zip(z_ups, (z_even, z_odd)):
        for n, (a, i) in enumerate(Z_PLANES):
            out[n] = arrays[a, up * (depth - Z_WIDTHS[a]) + i]
    planes = [(arrays, a, p) for a in range(4) for p in range(depth)]
    tile_pairs(planes, y_ups[1], y_odd)
    for up, out in zip(z_ups, (d_even, d_odd)):
        corners = [(arrays, a, up * (depth - CORNER_WIDTHS[a]) + i) for a, i in CORNERS]
        tile_pairs(corners, y_ups[1], out)


def pack(arrays):
    _, depth, rows, cols = arrays.shape
    sizes = [(len(Z_PLANES), rows)] * 2 + [(2 * depth, 8)] + [(len(CORNERS) // 2 + 1, 8)] * 2
    return pl.pallas_call(
        pack_kernel,
        out_shape=[jax.ShapeDtypeStruct((*size, cols), jnp.int32) for size in sizes],
        in_specs=[pl.BlockSpec(memory_space=VMEM)],
        out_specs=[pl.BlockSpec(memory_space=VMEM)] * 5,
        compiler_params=pltpu.CompilerParams(vmem_limit_bytes=16 * 2**20),
    )(arrays)


def relay_kernel(
    arrays, z_even, z_odd, y_odd, d_even, d_odd, before, after, ring, d_before, d_after, relay
):
    z_is_even = lax.axis_index("gz") % 2 == 0
    y_is_odd = lax.axis_index("gy") % 2
    for n in range(len(Z_PLANES)):
        e, o = z_even[n], z_odd[n]
        before[n] = jnp.where(z_is_even, o, e)
        after[n] = jnp.where(z_is_even, e, o)
    sources = [(arrays, a, p) for a in range(4) for p in range(arrays.shape[1])]
    for a, i in CORNERS:
        n = Z_PLANES.index((a, 0))
        sources += [(before, n + Z_WIDTHS[a] - CORNER_WIDTHS[a] + i), (after, n + i)]
    tile_pairs(sources, 1 - y_is_odd, relay)

    def unpack(out, n, pair):
        out[n] = pair
        if n + 1 < out.shape[0]:
            out[n + 1] = pltpu.roll(pair, 4, 0)

    for k in range(y_odd.shape[0]):
        unpack(ring, 2 * k, y_odd[k])
    for k in range(d_even.shape[0]):
        e, o = d_even[k], d_odd[k]
        unpack(d_before, 2 * k, jnp.where(z_is_even, o, e))
        unpack(d_after, 2 * k, jnp.where(z_is_even, e, o))


def relayed(arrays, z_even, z_odd, y_odd, d_even, d_odd):
    cols = z_even.shape[2]
    own = 2 * y_odd.shape[0]
    shapes = [z_even.shape] * 2 + [
        (n, 8, cols) for n in (own, len(CORNERS), len(CORNERS), own // 2 + len(CORNERS))
    ]
    return pl.pallas_call(
        relay_kernel,
        out_shape=[jax.ShapeDtypeStruct(shape, jnp.int32) for shape in shapes],
        in_specs=[pl.BlockSpec(memory_space=VMEM)] * 6,
        out_specs=[pl.BlockSpec(memory_space=VMEM)] * 6,
        compiler_params=pltpu.CompilerParams(vmem_limit_bytes=16 * 2**20),
    )(arrays, z_even, z_odd, y_odd, d_even, d_odd)


def krylov_kernel(
    counts, arrays, before, after, ring_odd, d_before, d_after, relay,
    fields, moments,
    m_pad, w_pad, coef, b_pad, v1, v2, sums,
):
    _, nz, ny = counts
    zi, yi = lax.axis_index("gz"), lax.axis_index("gy")
    _, depth, rows, cols = arrays.shape
    z_is_even, y_is_even = zi % 2 == 0, yi % 2 == 0
    wide = rows + 8
    f32 = jnp.float32
    ring_row = lax.broadcasted_iota(jnp.int32, (8, cols), 0)
    half = ring_row < 4
    own = slice(0, rows)
    ring = slice(rows, wide)

    def put(a, plane, where, values):
        if a == 0:
            m_pad[0, plane, where, :] = jnp.where(
                values == 0, 1.0, jnp.where(values == 1, PAIR, 0.0)
            )
            m_pad[1, plane, where, :] = jnp.where(
                values == 2, 1.0, jnp.where(values == 3, PAIR, 0.0)
            )
        else:
            w_pad[a - 1, plane, where, :] = values.astype(f32) + 1.0

    for a in range(4):
        for p in range(depth):
            put(a, LO + p, own, arrays[a, p])
    for n, (a, i) in enumerate(Z_PLANES):
        put(a, LO + depth + i, own, after[n])
        if LO - Z_WIDTHS[a] + i >= 0:
            put(a, LO - Z_WIDTHS[a] + i, own, before[n])

    from_even = half == y_is_even
    for k in range(2 * depth):
        pair = relay[k]
        for j, tile_even in enumerate((pair, pltpu.roll(pair, 4, 0))):
            a, p = divmod(2 * k + j, depth)
            put(a, LO + p, ring, jnp.where(from_even, tile_even, ring_odd[2 * k + j]))
    for n, (a, i) in enumerate(CORNERS):
        pair = relay[2 * depth + n]
        put(a, LO - CORNER_WIDTHS[a] + i, ring, jnp.where(from_even, pair, d_before[n]))
        put(a, LO + depth + i, ring, jnp.where(from_even, pltpu.roll(pair, 4, 0), d_after[n]))
    zero_tile = jnp.zeros((8, cols), jnp.int32)
    put(0, LO + depth + 3, ring, zero_tile)
    put(3, LO + depth + 2, ring, zero_tile)
    put(3, 0, ring, zero_tile)

    w_pad[0, LO + depth - 1] = jnp.where(zi == nz - 1, 0.0, w_pad[0, LO + depth - 1])
    w_pad[0, LO - 1] = jnp.where(zi == 0, 0.0, w_pad[0, LO - 1])
    at_end = (yi == ny - 1) & (ring_row == 7)
    at_start = (yi == 0) & (ring_row == 7)
    for p in range(LO + depth + 3):
        here = slice(rows - 8, rows)
        w_pad[1, p, here, :] = jnp.where(at_end, 0.0, w_pad[1, p, here, :])
        w_pad[1, p, ring, :] = jnp.where(at_start, 0.0, w_pad[1, p, ring, :])

    lanes = [slice(l, l + 128) for l in range(0, cols, 128)]
    lane = lax.broadcasted_iota(jnp.int32, (8, 128), 1)
    row = lax.broadcasted_iota(jnp.int32, (8, 128), 0)

    def tile(ref, index, r):
        return [ref[(*index, slice(r, r + 8), l)] for l in lanes]

    def store(ref, index, r, values):
        for l, x in zip(lanes, values):
            ref[(*index, slice(r, r + 8), l)] = x

    def next_x(v):
        turned = [pltpu.roll(x, 127, 1) for x in v]
        return [jnp.where(lane == 127, b, a) for a, b in zip(turned, turned[1:] + turned[:1])]

    def prev_x(v):
        turned = [pltpu.roll(x, 1, 1) for x in v]
        return [jnp.where(lane == 0, b, a) for a, b in zip(turned, turned[-1:] + turned[:-1])]

    def next_y(ref, index, r, v):
        other = tile(ref, index, (r + 8) % wide)
        return [pltpu.roll(jnp.where(row == 0, b, a), 7, 0) for a, b in zip(v, other)]

    def prev_y(ref, index, r, v):
        other = tile(ref, index, (r - 8) % wide)
        return [pltpu.roll(jnp.where(row == 7, b, a), 1, 0) for a, b in zip(v, other)]

    def near(weights, ref, c, p, r, v):
        neighbours = (
            tile(ref, (c, p + 1), r), tile(ref, (c, p - 1), r),
            next_y(ref, (c, p), r, v), prev_y(ref, (c, p), r, v),
            next_x(v), prev_x(v),
        )
        out = []
        for l in range(len(lanes)):
            t = [w[l] * n[l] for w, n in zip(weights, neighbours)]
            out.append((t[0] + t[1]) + (t[2] + t[3]) + (t[4] + t[5]))
        return out

    def prepare(p, _):
        for r in range(0, wide, 8):
            m = [tile(m_pad, (h, p), r) for h in range(2)]
            w_z, w_zb = tile(w_pad, (0, p), r), tile(w_pad, (0, p - 1), r)
            w_y, w_x = tile(w_pad, (1, p), r), tile(w_pad, (2, p), r)
            w_x = w_x[:-1] + [jnp.where(lane == 127, 0.0, w_x[-1])]
            w_yb, w_xb = prev_y(w_pad, (1, p), r, w_y), prev_x(w_x)
            weights = [[] for _ in range(7)]
            for l in range(len(lanes)):
                free = (m[0][l] + m[1][l]) == 0.0
                edges = [w[l] for w in (w_z, w_zb, w_y, w_yb, w_x, w_xb)]
                edges.append((edges[0] + edges[1]) + (edges[2] + edges[3]) + (edges[4] + edges[5]))
                for kept, w in zip(weights, edges):
                    kept.append(jnp.where(free, w, 0.0))
            for i, w in enumerate(weights):
                store(coef, (i, p), r, w)
            for h in range(2):
                both = near(weights, m_pad, h, p, r, m[h])
                second = [jnp.floor(x * (1.0 / PAIR)) for x in both]
                store(b_pad, (2 * h, p), r, [x - PAIR * y for x, y in zip(both, second)])
                store(b_pad, (2 * h + 1, p), r, second)
        return 0

    lax.fori_loop(1, LO + depth + 3, prepare, 0)

    def apply(source, target):
        def body(p, _):
            for r in range(0, wide, 8):
                weights = [tile(coef, (i, p), r) for i in range(7)]
                results = []
                for c in range(LABELS):
                    v = tile(source, (c, p), r)
                    n = near(weights[:6], source, c, p, r, v)
                    results.append([d * x - y for d, x, y in zip(weights[6], v, n)])
                for c in range(LABELS):
                    store(target, (c, p), r, results[c])
            return 0
        return body

    lax.fori_loop(2, LO + depth + 2, apply(b_pad, v1), 0)
    lax.fori_loop(3, LO + depth + 1, apply(v1, v2), 0)

    half_pairs = [(a, b) for a in range(LABELS) for b in range(a, LABELS)]
    all_pairs = [(a, b) for a in range(LABELS) for b in range(LABELS)]

    def total(products):
        while len(products) > 1:
            products = [x + y for x, y in zip(products[::2], products[1::2])] + (
                [products[-1]] if len(products) % 2 else []
            )
        return products[0]

    def accumulate(p, acc):
        parts = [[] for _ in acc]
        for r in range(0, rows, 8):
            bs = [tile(b_pad, (c, p), r) for c in range(LABELS)]
            abs_ = [tile(v1, (c, p), r) for c in range(LABELS)]
            for l in range(len(lanes)):
                b, ab = [x[l] for x in bs], [x[l] for x in abs_]
                products = [b[i] * b[j] for i, j in half_pairs]
                products += [b[i] * ab[j] for i, j in half_pairs]
                products += [ab[i] * ab[j] for i, j in half_pairs]
                for part, product in zip(parts, products):
                    part.append(product)
            for c in range(LABELS):
                store(fields, (0, c, p - LO), r, bs[c])
                store(fields, (1, c, p - LO), r, abs_[c])
        return tuple(x + total(part) for x, part in zip(acc, parts))

    def accumulate_last(p, acc):
        parts = [[] for _ in acc]
        for r in range(0, rows, 8):
            abs_ = [tile(v1, (c, p), r) for c in range(LABELS)]
            aabs = [tile(v2, (c, p), r) for c in range(LABELS)]
            w = [tile(coef, (i, p), r) for i in (0, 2, 4, 6)]
            qs = []
            for c in range(LABELS):
                v = aabs[c]
                z, y, x = tile(v2, (c, p + 1), r), next_y(v2, (c, p), r, v), next_x(v)
                qs.append([
                    w[3][l] * v[l] - 2.0 * (w[0][l] * z[l] + w[1][l] * y[l] + w[2][l] * x[l])
                    for l in range(len(lanes))
                ])
            for l in range(len(lanes)):
                ab, aab, q = [x[l] for x in abs_], [x[l] for x in aabs], [x[l] for x in qs]
                products = [ab[i] * aab[j] for i, j in half_pairs]
                products += [aab[i] * aab[j] for i, j in half_pairs]
                products += [aab[i] * q[j] for i, j in all_pairs]
                for part, product in zip(parts, products):
                    part.append(product)
            for c in range(LABELS):
                store(fields, (2, c, p - LO), r, aabs[c])
        return tuple(x + total(part) for x, part in zip(acc, parts))

    zero = jnp.zeros((8, 128), f32)
    low = lax.fori_loop(LO, LO + depth, accumulate, (zero,) * 30)
    high = lax.fori_loop(LO, LO + depth, accumulate_last, (zero,) * 36)
    kept = {}
    for k in range(5):
        part = low[10 * k : 10 * k + 10] if k < 3 else high[10 * (k - 3) : 10 * (k - 3) + 10]
        for (a, b), x in zip(half_pairs, part):
            kept[k, a, b] = kept[k, b, a] = x
    last = dict(zip(all_pairs, high[20:]))
    for a, b in half_pairs:
        kept[5, a, b] = kept[5, b, a] = 0.5 * (last[a, b] + last[b, a])
    for k in range(6):
        for a, b in half_pairs:
            x = jnp.sum(kept[k, a, b], axis=0, keepdims=True)
            for i, j in {(a, b), (b, a)}:
                at = (2 * k + j // 2) * 8 + (j % 2) * 4 + i
                sums[at : at + 1, :] = x
    packed = zero
    for g in range(12):
        x = jnp.sum(sums[8 * g : 8 * g + 8, :], axis=1, keepdims=True)
        packed = jnp.where(lane == g, x, packed)
    moments[...] = packed


def krylov(counts, arrays, halos):
    _, depth, rows, cols = arrays.shape
    planes, wide = depth + LO + HI, rows + 8
    f32 = jnp.float32
    return pl.pallas_call(
        functools.partial(krylov_kernel, counts),
        out_shape=[
            jax.ShapeDtypeStruct((3, LABELS, depth, rows, cols), f32),
            jax.ShapeDtypeStruct((8, 128), f32),
        ],
        in_specs=[pl.BlockSpec(memory_space=VMEM)] * 7,
        out_specs=[pl.BlockSpec(memory_space=VMEM)] * 2,
        scratch_shapes=[
            VMEM((2, planes, wide, cols), f32),
            VMEM((3, planes, wide, cols), f32),
            VMEM((7, planes, wide, cols), f32),
            VMEM((LABELS, planes, wide, cols), f32),
            VMEM((LABELS, planes, wide, cols), f32),
            VMEM((LABELS, planes, wide, cols), f32),
            VMEM((96, 128), f32),
        ],
        compiler_params=pltpu.CompilerParams(vmem_limit_bytes=48 * 2**20),
    )(arrays, *halos)


def combine_kernel(mine, theirs, fields, arrays, out, coeffs):
    f32 = jnp.float32
    _, depth, rows, cols = arrays.shape
    sums = mine[...] + theirs[...]
    lane = lax.broadcasted_iota(jnp.int32, (8, 128), 1)
    row = lax.broadcasted_iota(jnp.int32, (8, 128), 0)

    def splat(column):
        return jnp.broadcast_to(column, (8, 128))

    columns = {}
    for k in range(6):
        for h in range(2):
            x = splat(sums[:, 2 * k + h : 2 * k + h + 1])
            columns[k, 2 * h] = x
            columns[k, 2 * h + 1] = pltpu.roll(x, 4, 0)
    blocks = []
    for i in range(3):
        x = jnp.zeros((8, 128), f32)
        for j, k in enumerate((i + 1, i + 2, i + 3, i)):
            for b in range(LABELS):
                x = jnp.where(lane == 4 * j + b, columns[k, b], x)
        blocks.append(x)
    system = [
        jnp.where(row < 4, blocks[0], pltpu.roll(blocks[1], 4, 0)),
        jnp.where(row < 4, blocks[2], 0.0),
    ]
    start = list(system)
    for k in range(3 * LABELS):
        n, r = divmod(k, 8)
        pivot_row = system[n][r : r + 1, :]
        pivot = pivot_row[:, k : k + 1]
        sound = pivot > PIVOT_FLOOR * start[n][r : r + 1, k : k + 1]
        scale = jnp.where(sound, 1.0 / jnp.where(sound, pivot, 1.0), 0.0)
        pivot_row = pivot_row * scale
        for m in range(2):
            x = system[m] - system[m][:, k : k + 1] * pivot_row
            system[m] = jnp.where(row == r, pivot_row, x) if m == n else x
    for c in range(LABELS):
        for m in range(2):
            at = 3 * LABELS + c
            coeffs[c, 8 * m : 8 * m + 8, :] = splat(system[m][:, at : at + 1])

    for first in range(0, LABELS, 2):
        weights = {
            (c, k): jnp.broadcast_to(coeffs[c, k : k + 1, :], (8, 128))
            for c in (first, first + 1)
            for k in range(3 * LABELS)
        }

        def body(p, _):
            for r in range(0, rows, 8):
                for l in range(0, cols, 128):
                    cut = (p, slice(r, r + 8), slice(l, l + 128))
                    v = [fields[(k // LABELS, k % LABELS) + cut] for k in range(3 * LABELS)]
                    tag = arrays[(0,) + cut]
                    for c in (first, first + 1):
                        s = [v[k] * weights[c, k] for k in range(3 * LABELS)]
                        while len(s) > 1:
                            s = [x + y for x, y in zip(s[::2], s[1::2])] + (
                                [s[-1]] if len(s) % 2 else []
                            )
                        out[(c,) + cut] = jnp.where(tag == c, 1.0, s[0])
            return 0

        lax.fori_loop(0, depth, body, 0)


def combined(mine, theirs, fields, arrays):
    return pl.pallas_call(
        combine_kernel,
        out_shape=jax.ShapeDtypeStruct((LABELS,) + arrays.shape[1:], jnp.float32),
        in_specs=[pl.BlockSpec(memory_space=VMEM)] * 4,
        out_specs=pl.BlockSpec(memory_space=VMEM),
        scratch_shapes=[VMEM((LABELS, 16, 128), jnp.float32)],
        compiler_params=pltpu.CompilerParams(vmem_limit_bytes=32 * 2**20),
    )(mine, theirs, fields, arrays)


def per_device(counts, tags, depth_affinity, row_affinity, column_affinity):
    parts, nz, ny = counts
    arrays = jnp.stack([tags, depth_affinity, row_affinity, column_affinity])
    axes = ("parts", "gz", "gy")
    ze, zo = (lambda z: even_partner(z, nz)), (lambda z: odd_partner(z, nz))
    ye, yo = (lambda y: even_partner(y, ny)), (lambda y: odd_partner(y, ny))

    def swap(array, pz, py):
        def pair(z, y):
            if pz and pz(z) == z:
                return z, ye(y)
            if py and py(y) == y:
                return z, y
            return pz(z) if pz else z, py(y) if py else y
        return exchanged(array, axes, counts, pair)

    z_even, z_odd, y_odd, d_even, d_odd = pack(arrays)
    *sorted_halos, relay = relayed(
        arrays, swap(z_even, ze, None), swap(z_odd, zo, None), swap(y_odd, None, yo),
        swap(d_even, ze, yo), swap(d_odd, zo, yo),
    )
    halos = [*sorted_halos, swap(relay, None, ye)]
    fields, moments = krylov(counts, arrays, halos)

    steps = [lambda z, y: (z, y ^ 1)]
    steps += [lambda z, y, d=d: (z, y ^ d ^ 1) for d in powers(ny)[1:]]
    steps += [lambda z, y, d=d: (z ^ d, y ^ 1) for d in powers(nz)]
    for n, pair in enumerate(steps):
        theirs = exchanged(moments, axes, counts, pair)
        if n < len(steps) - 1:
            moments = moments + theirs
    return combined(moments, theirs, fields, arrays)


def powers(count):
    return [1 << n for n in range(count.bit_length() - 1)]


def solution(mesh):
    counts = tuple(mesh.shape[axis] for axis in ("parts", "gz", "gy"))
    placed = P(("parts", "gz"), "gy", None)
    return jax.shard_map(
        functools.partial(per_device, counts),
        mesh=mesh,
        in_specs=(placed,) * 4,
        out_specs=P(None, ("parts", "gz"), "gy", None),
        check_vma=False,
    )
```

```python
import functools

import jax
import jax.numpy as jnp
from jax import lax
from jax.experimental import pallas as pl
from jax.experimental.pallas import tpu as pltpu
from jax.sharding import PartitionSpec as P

LABELS = 4
PIVOT_FLOOR = 1e-7
LO, HI = 3, 4
Z_WIDTHS = (4, 3, 3, 3)
Z_PLANES = [(a, i) for a, width in enumerate(Z_WIDTHS) for i in range(width)]
CORNER_WIDTHS = (3, 3, 3, 2)
CORNERS = [(a, i) for a, width in enumerate(CORNER_WIDTHS) for i in range(width)]
PAIR = 4096.0
GROUP = 4
VMEM = pltpu.VMEM


def even_partner(i, count):
    return i ^ 1 if (i ^ 1) < count else i


def odd_partner(i, count):
    j = ((i + 1) ^ 1) - 1
    return j if 0 <= j < count else i


def exchanged(array, axes, counts, pair):
    parts, nz, ny = counts
    route = []
    for p in range(parts):
        for z in range(nz):
            for y in range(ny):
                q = (p,) + pair(z, y)
                if q == (p, z, y):
                    q = (even_partner(p, parts), z, y)
                source, target = ((a * nz + b) * ny + c for a, b, c in ((p, z, y), q))
                if source != target:
                    route.append((source, target))
    return lax.ppermute(array, axes, route)


def tile_pairs(sources, up, out):
    rows, cols = sources[0][0].shape[-2:]
    row = lax.broadcasted_iota(jnp.int32, (8, cols), 0)
    tile = pl.multiple_of(up * (rows - 8), 8)
    first = (row >= 4) == (up == 1)
    for k in range(0, len(sources), 2):
        (ra, *pa), (rb, *pb) = sources[k], sources[min(k + 1, len(sources) - 1)]
        a = ra[(*pa, pl.ds(tile, 8), slice(None))]
        b = rb[(*pb, pl.ds(tile, 8), slice(None))]
        out[k // 2] = jnp.where(first, a, pltpu.roll(b, 4, 0))


def interleave(cols, back=False):
    tiles = cols // 128
    i, j = (lax.broadcasted_iota(jnp.int32, (cols, cols), n) for n in ((1, 0) if back else (0, 1)))
    return (i == tiles * (j % 128) + j // 128).astype(jnp.float32).astype(jnp.bfloat16)


def pack_kernel(natural, arrays, z_even, z_odd, y_odd, d_even, d_odd):
    cols = natural.shape[-1]
    flat = natural[...].reshape(-1, cols).astype(jnp.float32).astype(jnp.bfloat16)
    turned = jnp.dot(flat, interleave(cols), preferred_element_type=jnp.float32)
    turned = turned.reshape(arrays.shape)
    arrays[0] = turned[0]
    arrays[1:] = turned[1:] + 1.0
    z_is_odd, y_is_odd = lax.axis_index("gz") % 2, lax.axis_index("gy") % 2
    depth = arrays.shape[1]
    z_ups, y_ups = (1 - z_is_odd, z_is_odd), (1 - y_is_odd, y_is_odd)
    for up, out in zip(z_ups, (z_even, z_odd)):
        for n, (a, i) in enumerate(Z_PLANES):
            out[n] = arrays[a, up * (depth - Z_WIDTHS[a]) + i]
    planes = [(arrays, a, p) for a in range(4) for p in range(depth)]
    tile_pairs(planes, y_ups[1], y_odd)
    for up, out in zip(z_ups, (d_even, d_odd)):
        corners = [(arrays, a, up * (depth - CORNER_WIDTHS[a]) + i) for a, i in CORNERS]
        tile_pairs(corners, y_ups[1], out)


def pack(arrays):
    _, depth, rows, cols = arrays.shape
    sizes = [(len(Z_PLANES), rows)] * 2 + [(2 * depth, 8)] + [(len(CORNERS) // 2 + 1, 8)] * 2
    return pl.pallas_call(
        pack_kernel,
        out_shape=[jax.ShapeDtypeStruct(arrays.shape, jnp.float32)]
        + [jax.ShapeDtypeStruct((*size, cols), jnp.float32) for size in sizes],
        in_specs=[pl.BlockSpec(memory_space=VMEM)],
        out_specs=[pl.BlockSpec(memory_space=VMEM)] * 6,
        compiler_params=pltpu.CompilerParams(vmem_limit_bytes=16 * 2**20),
    )(arrays)


def relay_kernel(
    arrays, z_even, z_odd, y_odd, d_even, d_odd, before, after, ring, d_before, d_after, relay
):
    z_is_even = lax.axis_index("gz") % 2 == 0
    y_is_odd = lax.axis_index("gy") % 2
    for n in range(len(Z_PLANES)):
        e, o = z_even[n], z_odd[n]
        before[n] = jnp.where(z_is_even, o, e)
        after[n] = jnp.where(z_is_even, e, o)
    sources = [(arrays, a, p) for a in range(4) for p in range(arrays.shape[1])]
    for a, i in CORNERS:
        n = Z_PLANES.index((a, 0))
        sources += [(before, n + Z_WIDTHS[a] - CORNER_WIDTHS[a] + i), (after, n + i)]
    tile_pairs(sources, 1 - y_is_odd, relay)

    def unpack(out, n, pair):
        out[n] = pair
        if n + 1 < out.shape[0]:
            out[n + 1] = pltpu.roll(pair, 4, 0)

    for k in range(y_odd.shape[0]):
        unpack(ring, 2 * k, y_odd[k])
    for k in range(d_even.shape[0]):
        e, o = d_even[k], d_odd[k]
        unpack(d_before, 2 * k, jnp.where(z_is_even, o, e))
        unpack(d_after, 2 * k, jnp.where(z_is_even, e, o))


def relayed(arrays, z_even, z_odd, y_odd, d_even, d_odd):
    cols = z_even.shape[2]
    own = 2 * y_odd.shape[0]
    shapes = [z_even.shape] * 2 + [
        (n, 8, cols) for n in (own, len(CORNERS), len(CORNERS), own // 2 + len(CORNERS))
    ]
    return pl.pallas_call(
        relay_kernel,
        out_shape=[jax.ShapeDtypeStruct(shape, jnp.float32) for shape in shapes],
        in_specs=[pl.BlockSpec(memory_space=VMEM)] * 6,
        out_specs=[pl.BlockSpec(memory_space=VMEM)] * 6,
        compiler_params=pltpu.CompilerParams(vmem_limit_bytes=16 * 2**20),
    )(arrays, z_even, z_odd, y_odd, d_even, d_odd)


def krylov_kernel(
    counts, arrays, before, after, ring_odd, d_before, d_after, relay,
    fields, moments,
    m_pad, w_pad, free, b_pad, v1, v2, acc, sums,
):
    _, nz, ny = counts
    zi, yi = lax.axis_index("gz"), lax.axis_index("gy")
    _, depth, rows, cols = arrays.shape
    z_is_even, y_is_even = zi % 2 == 0, yi % 2 == 0
    wide = rows + 8
    f32 = jnp.float32
    ring_row = lax.broadcasted_iota(jnp.int32, (8, cols), 0)
    half = ring_row < 4
    own = slice(0, rows)
    ring = slice(rows, wide)

    def put(a, plane, where, values):
        if a == 0:
            m_pad[0, plane, where, :] = jnp.where(
                values == 0, 1.0, jnp.where(values == 1, PAIR, 0.0)
            )
            m_pad[1, plane, where, :] = jnp.where(
                values == 2, 1.0, jnp.where(values == 3, PAIR, 0.0)
            )
        else:
            w_pad[a - 1, plane, where, :] = values

    for a in range(4):
        for p in range(depth):
            put(a, LO + p, own, arrays[a, p])
    for n, (a, i) in enumerate(Z_PLANES):
        put(a, LO + depth + i, own, after[n])
        if LO - Z_WIDTHS[a] + i >= 0:
            put(a, LO - Z_WIDTHS[a] + i, own, before[n])

    from_even = half == y_is_even
    for k in range(2 * depth):
        pair = relay[k]
        for j, tile_even in enumerate((pair, pltpu.roll(pair, 4, 0))):
            a, p = divmod(2 * k + j, depth)
            put(a, LO + p, ring, jnp.where(from_even, tile_even, ring_odd[2 * k + j]))
    for n, (a, i) in enumerate(CORNERS):
        pair = relay[2 * depth + n]
        put(a, LO - CORNER_WIDTHS[a] + i, ring, jnp.where(from_even, pair, d_before[n]))
        put(a, LO + depth + i, ring, jnp.where(from_even, pltpu.roll(pair, 4, 0), d_after[n]))
    zero_tile = jnp.zeros((8, cols), f32)
    put(0, LO + depth + 3, ring, zero_tile)
    put(3, LO + depth + 2, ring, zero_tile)
    put(3, 0, ring, zero_tile)

    w_pad[0, LO + depth - 1] = jnp.where(zi == nz - 1, 0.0, w_pad[0, LO + depth - 1])
    w_pad[0, LO - 1] = jnp.where(zi == 0, 0.0, w_pad[0, LO - 1])
    x_end = slice(cols - 128, cols)
    last_x = lax.broadcasted_iota(jnp.int32, (wide, 128), 1) == 127
    at_end = (yi == ny - 1) & (ring_row == 7)
    at_start = (yi == 0) & (ring_row == 7)
    for p in range(LO + depth + 3):
        here = slice(rows - 8, rows)
        w_pad[1, p, here, :] = jnp.where(at_end, 0.0, w_pad[1, p, here, :])
        w_pad[1, p, ring, :] = jnp.where(at_start, 0.0, w_pad[1, p, ring, :])
        w_pad[2, p, :, x_end] = jnp.where(last_x, 0.0, w_pad[2, p, :, x_end])

    lanes = [slice(l, l + 128) for l in range(0, cols, 128)]
    lane = lax.broadcasted_iota(jnp.int32, (8, 128), 1)
    row = lax.broadcasted_iota(jnp.int32, (8, 128), 0)

    row_tiles = range(0, wide, 8)

    def tile(ref, index, r):
        return [ref[(*index, slice(r, r + 8), l)] for l in lanes]

    def plane(ref, *index):
        return [tile(ref, index, r) for r in row_tiles]

    def store(ref, index, r, values):
        for l, x in zip(lanes, values):
            ref[(*index, slice(r, r + 8), l)] = x

    def store_plane(ref, index, values):
        for r, x in zip(row_tiles, values):
            store(ref, index, r, x)

    def each(f, *planes):
        return [[f(*x) for x in zip(*rows_)] for rows_ in zip(*planes)]

    def next_x(v):
        return [x[1:] + [pltpu.roll(x[0], 127, 1)] for x in v]

    def prev_x(v):
        return [[pltpu.roll(x[-1], 1, 1)] + x[:-1] for x in v]

    def next_y(v):
        pair = lambda a, b: pltpu.roll(jnp.where(row == 0, b, a), 7, 0)
        return each(pair, v, v[1:] + v[:1])

    def prev_y(v):
        pair = lambda a, b: pltpu.roll(jnp.where(row == 7, b, a), 1, 0)
        return each(pair, v, v[-1:] + v[:-1])

    def times(x, y):
        return each(lambda a, b: a * b, x, y)

    def in_groups(first, end, body):
        steps, rest = divmod(end - first, GROUP)

        def step(i, _):
            body(first + GROUP * i, GROUP)
            return 0

        lax.fori_loop(0, steps, step, 0)
        if rest:
            body(end - rest, rest)

    def prepare(start, count):
        for h in range(2):
            m = [plane(m_pad, h, start + j) for j in (-1, 0)]
            from_behind = times(plane(w_pad, 0, start - 1), m[0])
            here = m[1]
            for j in range(count):
                p = start + j
                ahead = plane(m_pad, h, p + 1)
                w_z, w_y, w_x = (plane(w_pad, i, p) for i in range(3))
                sums_ = each(
                    lambda a, b, c, d, e, f: (a + b) + (c + d) + (e + f),
                    times(w_z, ahead), from_behind,
                    times(w_y, next_y(here)), prev_y(times(w_y, here)),
                    times(w_x, next_x(here)), prev_x(times(w_x, here)),
                )
                if h == 0:
                    other = plane(m_pad, 1, p)
                    u = each(lambda a, b: jnp.where(a + b == 0.0, 1.0, 0.0), here, other)
                    store_plane(free, (p,), u)
                else:
                    u = plane(free, p)
                sums_ = times(sums_, u)
                second = each(lambda x: jnp.floor(x * (1.0 / PAIR)), sums_)
                store_plane(b_pad, (2 * h, p), each(lambda x, y: x - PAIR * y, sums_, second))
                store_plane(b_pad, (2 * h + 1, p), second)
                from_behind = times(w_z, here)
                here = ahead

    in_groups(1, LO + depth + 3, prepare)

    def flow(w, x, y):
        return each(lambda a, b, c: a * (b - c), w, x, y)

    def apply(source, target):
        def body(start, count):
            for c in range(LABELS):
                here = plane(source, c, start)
                from_behind = flow(plane(w_pad, 0, start - 1), here, plane(source, c, start - 1))
                for j in range(count):
                    p = start + j
                    ahead = plane(source, c, p + 1)
                    f_z = flow(plane(w_pad, 0, p), ahead, here)
                    f_y = flow(plane(w_pad, 1, p), next_y(here), here)
                    f_x = flow(plane(w_pad, 2, p), next_x(here), here)
                    store_plane(target, (c, p), each(
                        lambda u, a, b, c, d, e, f: u * ((a - b) + (c - d) + (e - f)),
                        plane(free, p), from_behind, f_z, prev_y(f_y), f_y, prev_x(f_x), f_x,
                    ))
                    from_behind, here = f_z, ahead
        return body

    in_groups(2, LO + depth + 2, apply(b_pad, v1))
    in_groups(3, LO + depth + 1, apply(v1, v2))

    half_pairs = [(a, b) for a in range(LABELS) for b in range(a, LABELS)]
    all_pairs = [(a, b) for a in range(LABELS) for b in range(LABELS)]

    def total(products):
        while len(products) > 1:
            products = [x + y for x, y in zip(products[::2], products[1::2])] + (
                [products[-1]] if len(products) % 2 else []
            )
        return products[0]

    def add_up(first, parts):
        for n, part in enumerate(parts):
            acc[first + n] = acc[first + n] + total(part)

    own_tiles = range(0, rows, 8)

    def accumulate(p, _):
        parts = [[] for _ in range(30)]
        for r in own_tiles:
            bs = [tile(b_pad, (c, p), r) for c in range(LABELS)]
            abs_ = [tile(v1, (c, p), r) for c in range(LABELS)]
            for l in range(len(lanes)):
                b, ab = [x[l] for x in bs], [x[l] for x in abs_]
                products = [b[i] * b[j] for i, j in half_pairs]
                products += [b[i] * ab[j] for i, j in half_pairs]
                products += [ab[i] * ab[j] for i, j in half_pairs]
                for part, product in zip(parts, products):
                    part.append(product)
            for c in range(LABELS):
                store(fields, (0, c, p - LO), r, bs[c])
                store(fields, (1, c, p - LO), r, abs_[c])
        add_up(0, parts)
        return 0

    def accumulate_last(p, _):
        parts = [[] for _ in range(36)]
        w_z, w_y, w_x = (plane(w_pad, i, p) for i in range(3))
        degree = each(
            lambda a, b, c, d, e, f: (a + b) + (c + d) + (e + f),
            w_z, plane(w_pad, 0, p - 1), w_y, prev_y(w_y), w_x, prev_x(w_x),
        )
        qs, aabs_ = [], []
        for c in range(LABELS):
            v = plane(v2, c, p)
            qs.append(each(
                lambda d, x, a, b, e: d * x - 2.0 * (a + b + e),
                degree, v, times(w_z, plane(v2, c, p + 1)), times(w_y, next_y(v)),
                times(w_x, next_x(v)),
            ))
            aabs_.append(v)
        for t, r in enumerate(own_tiles):
            abs_ = [tile(v1, (c, p), r) for c in range(LABELS)]
            for l in range(len(lanes)):
                ab, aab, q = [x[l] for x in abs_], [x[t][l] for x in aabs_], [x[t][l] for x in qs]
                products = [ab[i] * aab[j] for i, j in half_pairs]
                products += [aab[i] * aab[j] for i, j in half_pairs]
                products += [aab[i] * q[j] for i, j in all_pairs]
                for part, product in zip(parts, products):
                    part.append(product)
            for c in range(LABELS):
                store(fields, (2, c, p - LO), r, aabs_[c][t])
        add_up(30, parts)
        return 0

    zero = jnp.zeros((8, 128), f32)
    for n in range(66):
        acc[n] = zero
    lax.fori_loop(LO, LO + depth, accumulate, 0)
    lax.fori_loop(LO, LO + depth, accumulate_last, 0)
    low, high = [acc[n] for n in range(30)], [acc[30 + n] for n in range(36)]
    kept = {}
    for k in range(5):
        part = low[10 * k : 10 * k + 10] if k < 3 else high[10 * (k - 3) : 10 * (k - 3) + 10]
        for (a, b), x in zip(half_pairs, part):
            kept[k, a, b] = kept[k, b, a] = x
    last = dict(zip(all_pairs, high[20:]))
    for a, b in half_pairs:
        kept[5, a, b] = kept[5, b, a] = 0.5 * (last[a, b] + last[b, a])
    for k in range(6):
        for a, b in half_pairs:
            x = jnp.sum(kept[k, a, b], axis=0, keepdims=True)
            for i, j in {(a, b), (b, a)}:
                at = (2 * k + j // 2) * 8 + (j % 2) * 4 + i
                sums[at : at + 1, :] = x
    packed = zero
    for g in range(12):
        x = jnp.sum(sums[8 * g : 8 * g + 8, :], axis=1, keepdims=True)
        packed = jnp.where(lane == g, x, packed)
    moments[...] = packed


def krylov(counts, arrays, halos):
    _, depth, rows, cols = arrays.shape
    planes, wide = depth + LO + HI, rows + 8
    f32 = jnp.float32
    return pl.pallas_call(
        functools.partial(krylov_kernel, counts),
        out_shape=[
            jax.ShapeDtypeStruct((3, LABELS, depth, rows, cols), f32),
            jax.ShapeDtypeStruct((8, 128), f32),
        ],
        in_specs=[pl.BlockSpec(memory_space=VMEM)] * 7,
        out_specs=[pl.BlockSpec(memory_space=VMEM)] * 2,
        scratch_shapes=[
            VMEM((2, planes, wide, cols), f32),
            VMEM((3, planes, wide, cols), f32),
            VMEM((planes, wide, cols), f32),
            VMEM((LABELS, planes, wide, cols), f32),
            VMEM((LABELS, planes, wide, cols), f32),
            VMEM((LABELS, planes, wide, cols), f32),
            VMEM((66, 8, 128), f32),
            VMEM((96, 128), f32),
        ],
        compiler_params=pltpu.CompilerParams(vmem_limit_bytes=48 * 2**20),
    )(arrays, *halos)


def combine_kernel(mine, theirs, fields, natural, out, coeffs, mixed):
    f32 = jnp.float32
    _, depth, rows, cols = natural.shape
    sums = mine[...] + theirs[...]
    lane = lax.broadcasted_iota(jnp.int32, (8, 128), 1)
    row = lax.broadcasted_iota(jnp.int32, (8, 128), 0)

    def splat(column):
        return jnp.broadcast_to(column, (8, 128))

    columns = {}
    for k in range(6):
        for h in range(2):
            x = splat(sums[:, 2 * k + h : 2 * k + h + 1])
            columns[k, 2 * h] = x
            columns[k, 2 * h + 1] = pltpu.roll(x, 4, 0)
    blocks = []
    for i in range(3):
        x = jnp.zeros((8, 128), f32)
        for j, k in enumerate((i + 1, i + 2, i + 3, i)):
            for b in range(LABELS):
                x = jnp.where(lane == 4 * j + b, columns[k, b], x)
        blocks.append(x)
    system = [
        jnp.where(row < 4, blocks[0], pltpu.roll(blocks[1], 4, 0)),
        jnp.where(row < 4, blocks[2], 0.0),
    ]
    start = list(system)
    for k in range(3 * LABELS):
        n, r = divmod(k, 8)
        pivot_row = system[n][r : r + 1, :]
        pivot = pivot_row[:, k : k + 1]
        sound = pivot > PIVOT_FLOOR * start[n][r : r + 1, k : k + 1]
        scale = jnp.where(sound, 1.0 / jnp.where(sound, pivot, 1.0), 0.0)
        pivot_row = pivot_row * scale
        for m in range(2):
            x = system[m] - system[m][:, k : k + 1] * pivot_row
            system[m] = jnp.where(row == r, pivot_row, x) if m == n else x
    for c in range(LABELS):
        for m in range(2):
            at = 3 * LABELS + c
            coeffs[c, 8 * m : 8 * m + 8, :] = splat(system[m][:, at : at + 1])

    for first in range(0, LABELS, 2):
        weights = {
            (c, k): jnp.broadcast_to(coeffs[c, k : k + 1, :], (8, 128))
            for c in (first, first + 1)
            for k in range(3 * LABELS)
        }

        def body(p, _):
            for r in range(0, rows, 8):
                for l in range(0, cols, 128):
                    cut = (p, slice(r, r + 8), slice(l, l + 128))
                    v = [fields[(k // LABELS, k % LABELS) + cut] for k in range(3 * LABELS)]
                    for c in (first, first + 1):
                        s = [v[k] * weights[c, k] for k in range(3 * LABELS)]
                        while len(s) > 1:
                            s = [x + y for x, y in zip(s[::2], s[1::2])] + (
                                [s[-1]] if len(s) % 2 else []
                            )
                        mixed[(c,) + cut] = s[0]
            return 0

        lax.fori_loop(0, depth, body, 0)

    back = interleave(cols, back=True)
    for c in range(LABELS):
        x = mixed[c].reshape(depth * rows, cols)
        high = x.astype(jnp.bfloat16)
        low = (x - high.astype(f32)).astype(jnp.bfloat16)
        x = jnp.dot(high, back, preferred_element_type=f32)
        x = x + jnp.dot(low, back, preferred_element_type=f32)
        out[c] = jnp.where(natural[0] == c, 1.0, x.reshape(depth, rows, cols))


def combined(mine, theirs, fields, natural):
    return pl.pallas_call(
        combine_kernel,
        out_shape=jax.ShapeDtypeStruct((LABELS,) + natural.shape[1:], jnp.float32),
        in_specs=[pl.BlockSpec(memory_space=VMEM)] * 4,
        out_specs=pl.BlockSpec(memory_space=VMEM),
        scratch_shapes=[
            VMEM((LABELS, 16, 128), jnp.float32),
            VMEM((LABELS,) + natural.shape[1:], jnp.float32),
        ],
        compiler_params=pltpu.CompilerParams(vmem_limit_bytes=32 * 2**20),
    )(mine, theirs, fields, natural)


def per_device(counts, tags, depth_affinity, row_affinity, column_affinity):
    parts, nz, ny = counts
    natural = jnp.stack([tags, depth_affinity, row_affinity, column_affinity])
    axes = ("parts", "gz", "gy")
    ze, zo = (lambda z: even_partner(z, nz)), (lambda z: odd_partner(z, nz))
    ye, yo = (lambda y: even_partner(y, ny)), (lambda y: odd_partner(y, ny))

    def swap(array, pz, py):
        def pair(z, y):
            if pz and pz(z) == z:
                return z, ye(y)
            if py and py(y) == y:
                return z, y
            return pz(z) if pz else z, py(y) if py else y
        return exchanged(array, axes, counts, pair)

    arrays, z_even, z_odd, y_odd, d_even, d_odd = pack(natural)
    *sorted_halos, relay = relayed(
        arrays, swap(z_even, ze, None), swap(z_odd, zo, None), swap(y_odd, None, yo),
        swap(d_even, ze, yo), swap(d_odd, zo, yo),
    )
    halos = [*sorted_halos, swap(relay, None, ye)]
    fields, moments = krylov(counts, arrays, halos)

    steps = [lambda z, y: (z, y ^ 1)]
    steps += [lambda z, y, d=d: (z, y ^ d ^ 1) for d in powers(ny)[1:]]
    steps += [lambda z, y, d=d: (z ^ d, y ^ 1) for d in powers(nz)]
    for n, pair in enumerate(steps):
        theirs = exchanged(moments, axes, counts, pair)
        if n < len(steps) - 1:
            moments = moments + theirs
    return combined(moments, theirs, fields, natural)


def powers(count):
    return [1 << n for n in range(count.bit_length() - 1)]


def solution(mesh):
    counts = tuple(mesh.shape[axis] for axis in ("parts", "gz", "gy"))
    placed = P(("parts", "gz"), "gy", None)
    return jax.shard_map(
        functools.partial(per_device, counts),
        mesh=mesh,
        in_specs=(placed,) * 4,
        out_specs=P(None, ("parts", "gz"), "gy", None),
        check_vma=False,
    )
```

```python
import functools

import jax
import jax.numpy as jnp
from jax import lax
from jax.experimental import pallas as pl
from jax.experimental.pallas import tpu as pltpu
from jax.sharding import PartitionSpec as P

LABELS = 4
PIVOT_FLOOR = 1e-7
LO, HI = 3, 4
Z_WIDTHS = (4, 3, 3, 3)
Z_PLANES = [(a, i) for a, width in enumerate(Z_WIDTHS) for i in range(width)]
CORNER_WIDTHS = (3, 3, 3, 2)
CORNERS = [(a, i) for a, width in enumerate(CORNER_WIDTHS) for i in range(width)]
PAIR = 4096.0
CHUNKS = 4
GROUP = 4
VMEM = pltpu.VMEM


def even_partner(i, count):
    return i ^ 1 if (i ^ 1) < count else i


def odd_partner(i, count):
    j = ((i + 1) ^ 1) - 1
    return j if 0 <= j < count else i


def exchanged(array, axes, counts, pair):
    parts, nz, ny = counts
    route = []
    for p in range(parts):
        for z in range(nz):
            for y in range(ny):
                q = (p,) + pair(z, y)
                if q == (p, z, y):
                    q = (even_partner(p, parts), z, y)
                source, target = ((a * nz + b) * ny + c for a, b, c in ((p, z, y), q))
                if source != target:
                    route.append((source, target))
    return lax.ppermute(array, axes, route)


def tile_pairs(sources, up, out):
    rows, cols = sources[0][0].shape[-2:]
    row = lax.broadcasted_iota(jnp.int32, (8, cols), 0)
    tile = pl.multiple_of(up * (rows - 8), 8)
    first = (row >= 4) == (up == 1)
    for k in range(0, len(sources), 2):
        (ra, *pa), (rb, *pb) = sources[k], sources[min(k + 1, len(sources) - 1)]
        a = ra[(*pa, pl.ds(tile, 8), slice(None))]
        b = rb[(*pb, pl.ds(tile, 8), slice(None))]
        out[k // 2] = jnp.where(first, a, pltpu.roll(b, 4, 0))


def interleave(cols, back=False):
    tiles = cols // 128
    i, j = (lax.broadcasted_iota(jnp.int32, (cols, cols), n) for n in ((1, 0) if back else (0, 1)))
    return (i == tiles * (j % 128) + j // 128).astype(jnp.float32).astype(jnp.bfloat16)


def pack_kernel(natural, arrays, z_even, z_odd, y_odd, d_even, d_odd):
    cols = natural.shape[-1]
    flat = natural[...].reshape(-1, cols).astype(jnp.float32).astype(jnp.bfloat16)
    turned = jnp.dot(flat, interleave(cols), preferred_element_type=jnp.float32)
    turned = turned.reshape(arrays.shape)
    arrays[0] = turned[0]
    arrays[1:] = turned[1:] + 1.0
    z_is_odd, y_is_odd = lax.axis_index("gz") % 2, lax.axis_index("gy") % 2
    depth = arrays.shape[1]
    z_ups, y_ups = (1 - z_is_odd, z_is_odd), (1 - y_is_odd, y_is_odd)
    for up, out in zip(z_ups, (z_even, z_odd)):
        for n, (a, i) in enumerate(Z_PLANES):
            out[n] = arrays[a, up * (depth - Z_WIDTHS[a]) + i]
    planes = [(arrays, a, p) for a in range(4) for p in range(depth)]
    tile_pairs(planes, y_ups[1], y_odd)
    for up, out in zip(z_ups, (d_even, d_odd)):
        corners = [(arrays, a, up * (depth - CORNER_WIDTHS[a]) + i) for a, i in CORNERS]
        tile_pairs(corners, y_ups[1], out)


def pack(arrays):
    _, depth, rows, cols = arrays.shape
    sizes = [(len(Z_PLANES), rows)] * 2 + [(2 * depth, 8)] + [(len(CORNERS) // 2 + 1, 8)] * 2
    return pl.pallas_call(
        pack_kernel,
        out_shape=[jax.ShapeDtypeStruct(arrays.shape, jnp.float32)]
        + [jax.ShapeDtypeStruct((*size, cols), jnp.float32) for size in sizes],
        in_specs=[pl.BlockSpec(memory_space=VMEM)],
        out_specs=[pl.BlockSpec(memory_space=VMEM)] * 6,
        compiler_params=pltpu.CompilerParams(vmem_limit_bytes=16 * 2**20),
    )(arrays)


def relay_kernel(
    arrays, z_even, z_odd, y_odd, d_even, d_odd, before, after, ring, d_before, d_after, relay
):
    z_is_even = lax.axis_index("gz") % 2 == 0
    y_is_odd = lax.axis_index("gy") % 2
    for n in range(len(Z_PLANES)):
        e, o = z_even[n], z_odd[n]
        before[n] = jnp.where(z_is_even, o, e)
        after[n] = jnp.where(z_is_even, e, o)
    sources = [(arrays, a, p) for a in range(4) for p in range(arrays.shape[1])]
    for a, i in CORNERS:
        n = Z_PLANES.index((a, 0))
        sources += [(before, n + Z_WIDTHS[a] - CORNER_WIDTHS[a] + i), (after, n + i)]
    tile_pairs(sources, 1 - y_is_odd, relay)

    def unpack(out, n, pair):
        out[n] = pair
        if n + 1 < out.shape[0]:
            out[n + 1] = pltpu.roll(pair, 4, 0)

    for k in range(y_odd.shape[0]):
        unpack(ring, 2 * k, y_odd[k])
    for k in range(d_even.shape[0]):
        e, o = d_even[k], d_odd[k]
        unpack(d_before, 2 * k, jnp.where(z_is_even, o, e))
        unpack(d_after, 2 * k, jnp.where(z_is_even, e, o))


def relayed(arrays, z_even, z_odd, y_odd, d_even, d_odd):
    cols = z_even.shape[2]
    own = 2 * y_odd.shape[0]
    shapes = [z_even.shape] * 2 + [
        (n, 8, cols) for n in (own, len(CORNERS), len(CORNERS), own // 2 + len(CORNERS))
    ]
    return pl.pallas_call(
        relay_kernel,
        out_shape=[jax.ShapeDtypeStruct(shape, jnp.float32) for shape in shapes],
        in_specs=[pl.BlockSpec(memory_space=VMEM)] * 6,
        out_specs=[pl.BlockSpec(memory_space=VMEM)] * 6,
        compiler_params=pltpu.CompilerParams(vmem_limit_bytes=16 * 2**20),
    )(arrays, z_even, z_odd, y_odd, d_even, d_odd)


def krylov_kernel(
    counts, arrays, before, after, ring_odd, d_before, d_after, relay,
    fields, moments,
    m_pad, w_pad, free, b_pad, v1, v2, acc, sums,
):
    _, nz, ny = counts
    zi, yi = lax.axis_index("gz"), lax.axis_index("gy")
    _, depth, rows, cols = arrays.shape
    z_is_even, y_is_even = zi % 2 == 0, yi % 2 == 0
    wide = rows + 8
    f32 = jnp.float32
    ring_row = lax.broadcasted_iota(jnp.int32, (8, cols), 0)
    half = ring_row < 4
    own = slice(0, rows)
    ring = slice(rows, wide)

    def put(a, plane, where, values):
        if a == 0:
            m_pad[0, plane, where, :] = jnp.where(
                values == 0, 1.0, jnp.where(values == 1, PAIR, 0.0)
            )
            m_pad[1, plane, where, :] = jnp.where(
                values == 2, 1.0, jnp.where(values == 3, PAIR, 0.0)
            )
        else:
            w_pad[a - 1, plane, where, :] = values

    for a in range(4):
        for p in range(depth):
            put(a, LO + p, own, arrays[a, p])
    for n, (a, i) in enumerate(Z_PLANES):
        put(a, LO + depth + i, own, after[n])
        if LO - Z_WIDTHS[a] + i >= 0:
            put(a, LO - Z_WIDTHS[a] + i, own, before[n])

    from_even = half == y_is_even
    for k in range(2 * depth):
        pair = relay[k]
        for j, tile_even in enumerate((pair, pltpu.roll(pair, 4, 0))):
            a, p = divmod(2 * k + j, depth)
            put(a, LO + p, ring, jnp.where(from_even, tile_even, ring_odd[2 * k + j]))
    for n, (a, i) in enumerate(CORNERS):
        pair = relay[2 * depth + n]
        put(a, LO - CORNER_WIDTHS[a] + i, ring, jnp.where(from_even, pair, d_before[n]))
        put(a, LO + depth + i, ring, jnp.where(from_even, pltpu.roll(pair, 4, 0), d_after[n]))
    zero_tile = jnp.zeros((8, cols), f32)
    put(0, LO + depth + 3, ring, zero_tile)
    put(3, LO + depth + 2, ring, zero_tile)
    put(3, 0, ring, zero_tile)

    w_pad[0, LO + depth - 1] = jnp.where(zi == nz - 1, 0.0, w_pad[0, LO + depth - 1])
    w_pad[0, LO - 1] = jnp.where(zi == 0, 0.0, w_pad[0, LO - 1])
    x_end = slice(cols - 128, cols)
    last_x = lax.broadcasted_iota(jnp.int32, (wide, 128), 1) == 127
    at_end = (yi == ny - 1) & (ring_row == 7)
    at_start = (yi == 0) & (ring_row == 7)
    for p in range(LO + depth + 3):
        here = slice(rows - 8, rows)
        w_pad[1, p, here, :] = jnp.where(at_end, 0.0, w_pad[1, p, here, :])
        w_pad[1, p, ring, :] = jnp.where(at_start, 0.0, w_pad[1, p, ring, :])
        w_pad[2, p, :, x_end] = jnp.where(last_x, 0.0, w_pad[2, p, :, x_end])

    lanes = [slice(l, l + 128) for l in range(0, cols, 128)]
    lane = lax.broadcasted_iota(jnp.int32, (8, 128), 1)
    row = lax.broadcasted_iota(jnp.int32, (8, 128), 0)

    row_tiles = range(0, wide, 8)

    def tile(ref, index, r):
        return [ref[(*index, slice(r, r + 8), l)] for l in lanes]

    def plane(ref, *index):
        return [tile(ref, index, r) for r in row_tiles]

    def store(ref, index, r, values):
        for l, x in zip(lanes, values):
            ref[(*index, slice(r, r + 8), l)] = x

    def store_plane(ref, index, values):
        for r, x in zip(row_tiles, values):
            store(ref, index, r, x)

    def each(f, *planes):
        return [[f(*x) for x in zip(*rows_)] for rows_ in zip(*planes)]

    def next_x(v):
        return [x[1:] + [pltpu.roll(x[0], 127, 1)] for x in v]

    def prev_x(v):
        return [[pltpu.roll(x[-1], 1, 1)] + x[:-1] for x in v]

    def next_y(v):
        pair = lambda a, b: pltpu.roll(jnp.where(row == 0, b, a), 7, 0)
        return each(pair, v, v[1:] + v[:1])

    def prev_y(v):
        pair = lambda a, b: pltpu.roll(jnp.where(row == 7, b, a), 1, 0)
        return each(pair, v, v[-1:] + v[:-1])

    def times(x, y):
        return each(lambda a, b: a * b, x, y)

    def in_groups(first, end, body):
        steps, rest = divmod(end - first, GROUP)

        def step(i, _):
            body(first + GROUP * i, GROUP)
            return 0

        lax.fori_loop(0, steps, step, 0)
        if rest:
            body(end - rest, rest)

    def prepare(start, count):
        for h in range(2):
            m = [plane(m_pad, h, start + j) for j in (-1, 0)]
            from_behind = times(plane(w_pad, 0, start - 1), m[0])
            here = m[1]
            for j in range(count):
                p = start + j
                ahead = plane(m_pad, h, p + 1)
                w_z, w_y, w_x = (plane(w_pad, i, p) for i in range(3))
                sums_ = each(
                    lambda a, b, c, d, e, f: (a + b) + (c + d) + (e + f),
                    times(w_z, ahead), from_behind,
                    times(w_y, next_y(here)), prev_y(times(w_y, here)),
                    times(w_x, next_x(here)), prev_x(times(w_x, here)),
                )
                if h == 0:
                    other = plane(m_pad, 1, p)
                    u = each(lambda a, b: jnp.where(a + b == 0.0, 1.0, 0.0), here, other)
                    store_plane(free, (p,), u)
                else:
                    u = plane(free, p)
                sums_ = times(sums_, u)
                second = each(lambda x: jnp.floor(x * (1.0 / PAIR)), sums_)
                store_plane(b_pad, (2 * h, p), each(lambda x, y: x - PAIR * y, sums_, second))
                store_plane(b_pad, (2 * h + 1, p), second)
                from_behind = times(w_z, here)
                here = ahead

    in_groups(1, LO + depth + 3, prepare)

    def flow(w, x, y):
        return each(lambda a, b, c: a * (b - c), w, x, y)

    def apply(source, target):
        def body(start, count):
            for c in range(LABELS):
                here = plane(source, c, start)
                from_behind = flow(plane(w_pad, 0, start - 1), here, plane(source, c, start - 1))
                for j in range(count):
                    p = start + j
                    ahead = plane(source, c, p + 1)
                    f_z = flow(plane(w_pad, 0, p), ahead, here)
                    f_y = flow(plane(w_pad, 1, p), next_y(here), here)
                    f_x = flow(plane(w_pad, 2, p), next_x(here), here)
                    store_plane(target, (c, p), each(
                        lambda u, a, b, c, d, e, f: u * ((a - b) + (c - d) + (e - f)),
                        plane(free, p), from_behind, f_z, prev_y(f_y), f_y, prev_x(f_x), f_x,
                    ))
                    from_behind, here = f_z, ahead
        return body

    in_groups(2, LO + depth + 2, apply(b_pad, v1))
    in_groups(3, LO + depth + 1, apply(v1, v2))

    half_pairs = [(a, b) for a in range(LABELS) for b in range(a, LABELS)]
    all_pairs = [(a, b) for a in range(LABELS) for b in range(LABELS)]

    def total(products):
        while len(products) > 1:
            products = [x + y for x, y in zip(products[::2], products[1::2])] + (
                [products[-1]] if len(products) % 2 else []
            )
        return products[0]

    def add_up(first, parts):
        for n, part in enumerate(parts):
            acc[first + n] = acc[first + n] + total(part)

    own_tiles = range(0, rows, 8)

    def accumulate(p, _):
        parts = [[] for _ in range(30)]
        for r in own_tiles:
            bs = [tile(b_pad, (c, p), r) for c in range(LABELS)]
            abs_ = [tile(v1, (c, p), r) for c in range(LABELS)]
            for l in range(len(lanes)):
                b, ab = [x[l] for x in bs], [x[l] for x in abs_]
                products = [b[i] * b[j] for i, j in half_pairs]
                products += [b[i] * ab[j] for i, j in half_pairs]
                products += [ab[i] * ab[j] for i, j in half_pairs]
                for part, product in zip(parts, products):
                    part.append(product)
            for c in range(LABELS):
                store(fields, (0, c, p - LO), r, bs[c])
                store(fields, (1, c, p - LO), r, abs_[c])
        add_up(0, parts)
        return 0

    def accumulate_last(p, _):
        parts = [[] for _ in range(36)]
        w_z, w_y, w_x = (plane(w_pad, i, p) for i in range(3))
        degree = each(
            lambda a, b, c, d, e, f: (a + b) + (c + d) + (e + f),
            w_z, plane(w_pad, 0, p - 1), w_y, prev_y(w_y), w_x, prev_x(w_x),
        )
        qs, aabs_ = [], []
        for c in range(LABELS):
            v = plane(v2, c, p)
            qs.append(each(
                lambda d, x, a, b, e: d * x - 2.0 * (a + b + e),
                degree, v, times(w_z, plane(v2, c, p + 1)), times(w_y, next_y(v)),
                times(w_x, next_x(v)),
            ))
            aabs_.append(v)
        for t, r in enumerate(own_tiles):
            abs_ = [tile(v1, (c, p), r) for c in range(LABELS)]
            for l in range(len(lanes)):
                ab, aab, q = [x[l] for x in abs_], [x[t][l] for x in aabs_], [x[t][l] for x in qs]
                products = [ab[i] * aab[j] for i, j in half_pairs]
                products += [aab[i] * aab[j] for i, j in half_pairs]
                products += [aab[i] * q[j] for i, j in all_pairs]
                for part, product in zip(parts, products):
                    part.append(product)
            for c in range(LABELS):
                store(fields, (2, c, p - LO), r, aabs_[c][t])
        add_up(30, parts)
        return 0

    zero = jnp.zeros((8, 128), f32)
    for n in range(66):
        acc[n] = zero
    lax.fori_loop(LO, LO + depth, accumulate, 0)
    lax.fori_loop(LO, LO + depth, accumulate_last, 0)
    low, high = [acc[n] for n in range(30)], [acc[30 + n] for n in range(36)]
    kept = {}
    for k in range(5):
        part = low[10 * k : 10 * k + 10] if k < 3 else high[10 * (k - 3) : 10 * (k - 3) + 10]
        for (a, b), x in zip(half_pairs, part):
            kept[k, a, b] = kept[k, b, a] = x
    last = dict(zip(all_pairs, high[20:]))
    for a, b in half_pairs:
        kept[5, a, b] = kept[5, b, a] = 0.5 * (last[a, b] + last[b, a])
    for k in range(6):
        for a, b in half_pairs:
            x = jnp.sum(kept[k, a, b], axis=0, keepdims=True)
            for i, j in {(a, b), (b, a)}:
                at = (2 * k + j // 2) * 8 + (j % 2) * 4 + i
                sums[at : at + 1, :] = x
    packed = zero
    for g in range(12):
        x = jnp.sum(sums[8 * g : 8 * g + 8, :], axis=1, keepdims=True)
        packed = jnp.where(lane == g, x, packed)
    moments[...] = packed


def krylov(counts, arrays, halos):
    _, depth, rows, cols = arrays.shape
    planes, wide = depth + LO + HI, rows + 8
    f32 = jnp.float32
    return pl.pallas_call(
        functools.partial(krylov_kernel, counts),
        out_shape=[
            jax.ShapeDtypeStruct((3, LABELS, depth, rows, cols), f32),
            jax.ShapeDtypeStruct((8, 128), f32),
        ],
        in_specs=[pl.BlockSpec(memory_space=VMEM)] * 7,
        out_specs=[pl.BlockSpec(memory_space=VMEM)] * 2,
        scratch_shapes=[
            VMEM((2, planes, wide, cols), f32),
            VMEM((3, planes, wide, cols), f32),
            VMEM((planes, wide, cols), f32),
            VMEM((LABELS, planes, wide, cols), f32),
            VMEM((LABELS, planes, wide, cols), f32),
            VMEM((LABELS, planes, wide, cols), f32),
            VMEM((66, 8, 128), f32),
            VMEM((96, 128), f32),
        ],
        compiler_params=pltpu.CompilerParams(vmem_limit_bytes=48 * 2**20),
    )(arrays, *halos)


def solved(moment, sides, floor):
    n = 3 * LABELS
    system = {
        (i, j): moment(i // LABELS + j // LABELS + 1, i % LABELS, j % LABELS)
        for i in range(n) for j in range(i + 1)
    }
    right = dict(enumerate(sides))
    first = {k: system[k, k] for k in range(n)}
    lower, inverse = {}, {}
    for k in range(n):
        pivot = system[k, k]
        sound = pivot > floor * first[k]
        inverse[k] = jnp.where(sound, 1.0 / jnp.where(sound, pivot, 1.0), 0.0)
        for i in range(k + 1, n):
            lower[i, k] = system[i, k] * inverse[k]
        for i in range(k + 1, n):
            for j in range(k + 1, i + 1):
                system[i, j] = system[i, j] - lower[i, k] * system[j, k]
            right[i] = right[i] - lower[i, k] * right[k]
    for k in reversed(range(n)):
        x = right[k] * inverse[k]
        for i in range(k + 1, n):
            x = x - lower[i, k] * right[i]
        right[k] = x
    return [right[k] for k in range(n)]


def combine_kernel(mine, theirs, fields, natural, out, spread, coeffs, mixed, buffer, sems):
    f32 = jnp.float32
    _, depth, rows, cols = natural.shape
    sums = mine[...] + theirs[...]
    columns = [jnp.broadcast_to(sums[:, g : g + 1], (8, 128)) for g in range(12)]
    for g in range(12):
        spread[g] = columns[g]

    def moment(k, a, b):
        a, b = min(a, b), max(a, b)
        at = (b % 2) * 4 + a
        return jnp.broadcast_to(spread[2 * k + b // 2, at : at + 1, :], (8, 128))

    sides = []
    for k in range(3):
        for a in range(LABELS):
            x = columns[2 * k + a // 2]
            sides.append(pltpu.roll(x, 4, 0) if a % 2 else x)
    for k, x in enumerate(solved(moment, sides, PIVOT_FLOOR)):
        coeffs[k] = x

    back = interleave(cols, back=True)
    chunk = depth // CHUNKS

    def combine(n):
        for first in range(0, LABELS, 2):
            weights = {
                (k, c): jnp.broadcast_to(coeffs[k, c : c + 1, :], (8, 128))
                for k in range(3 * LABELS) for c in (first, first + 1)
            }
            for p in range(n * chunk, n * chunk + chunk):
                for r in range(0, rows, 8):
                    for l in range(0, cols, 128):
                        cut = (p, slice(r, r + 8), slice(l, l + 128))
                        v = [fields[(k // LABELS, k % LABELS) + cut] for k in range(3 * LABELS)]
                        for c in (first, first + 1):
                            s = [v[k] * weights[k, c] for k in range(3 * LABELS)]
                            while len(s) > 1:
                                s = [x + y for x, y in zip(s[::2], s[1::2])] + (
                                    [s[-1]] if len(s) % 2 else []
                                )
                            mixed[(c,) + cut] = s[0]

    def turn_back(n):
        planes = slice(n * chunk, n * chunk + chunk)
        x = mixed[:, planes].reshape(LABELS * chunk * rows, cols)
        high = x.astype(jnp.bfloat16)
        low = (x - high.astype(f32)).astype(jnp.bfloat16)
        x = jnp.dot(high, back, preferred_element_type=f32)
        x = x + jnp.dot(low, back, preferred_element_type=f32)
        x = x.reshape(LABELS, chunk, rows, cols)
        for c in range(LABELS):
            buffer[c, planes] = jnp.where(natural[0, planes] == c, 1.0, x[c])

    copies = [
        pltpu.make_async_copy(
            buffer.at[:, n * chunk : (n + 1) * chunk], out.at[:, n * chunk : (n + 1) * chunk],
            sems.at[n],
        )
        for n in range(CHUNKS)
    ]
    combine(0)
    for n in range(CHUNKS):
        if n + 1 < CHUNKS:
            combine(n + 1)
        turn_back(n)
        copies[n].start()
    for copy in copies:
        copy.wait()


def combined(mine, theirs, fields, natural):
    _, depth, rows, cols = natural.shape
    f32 = jnp.float32
    return pl.pallas_call(
        combine_kernel,
        out_shape=jax.ShapeDtypeStruct((LABELS, depth, rows, cols), f32),
        in_specs=[pl.BlockSpec(memory_space=VMEM)] * 4,
        out_specs=pl.BlockSpec(memory_space=pltpu.HBM),
        scratch_shapes=[
            VMEM((12, 8, 128), f32),
            VMEM((3 * LABELS, 8, 128), f32),
            VMEM((LABELS, depth, rows, cols), f32),
            VMEM((LABELS, depth, rows, cols), f32),
            pltpu.SemaphoreType.DMA((CHUNKS,)),
        ],
        compiler_params=pltpu.CompilerParams(vmem_limit_bytes=32 * 2**20),
    )(mine, theirs, fields, natural)


def per_device(counts, tags, depth_affinity, row_affinity, column_affinity):
    parts, nz, ny = counts
    natural = jnp.stack([tags, depth_affinity, row_affinity, column_affinity])
    axes = ("parts", "gz", "gy")
    ze, zo = (lambda z: even_partner(z, nz)), (lambda z: odd_partner(z, nz))
    ye, yo = (lambda y: even_partner(y, ny)), (lambda y: odd_partner(y, ny))

    def swap(array, pz, py):
        def pair(z, y):
            if pz and pz(z) == z:
                return z, ye(y)
            if py and py(y) == y:
                return z, y
            return pz(z) if pz else z, py(y) if py else y
        return exchanged(array, axes, counts, pair)

    arrays, z_even, z_odd, y_odd, d_even, d_odd = pack(natural)
    *sorted_halos, relay = relayed(
        arrays, swap(z_even, ze, None), swap(z_odd, zo, None), swap(y_odd, None, yo),
        swap(d_even, ze, yo), swap(d_odd, zo, yo),
    )
    halos = [*sorted_halos, swap(relay, None, ye)]
    fields, moments = krylov(counts, arrays, halos)

    steps = [lambda z, y: (z, y ^ 1)]
    steps += [lambda z, y, d=d: (z, y ^ d ^ 1) for d in powers(ny)[1:]]
    steps += [lambda z, y, d=d: (z ^ d, y ^ 1) for d in powers(nz)]
    for n, pair in enumerate(steps):
        theirs = exchanged(moments, axes, counts, pair)
        if n < len(steps) - 1:
            moments = moments + theirs
    return combined(moments, theirs, fields, natural)


def powers(count):
    return [1 << n for n in range(count.bit_length() - 1)]


def solution(mesh):
    counts = tuple(mesh.shape[axis] for axis in ("parts", "gz", "gy"))
    placed = P(("parts", "gz"), "gy", None)
    return jax.shard_map(
        functools.partial(per_device, counts),
        mesh=mesh,
        in_specs=(placed,) * 4,
        out_specs=P(None, ("parts", "gz"), "gy", None),
        check_vma=False,
    )
```

```python
import functools
import types

import jax
import jax.numpy as jnp
from jax import lax
from jax.experimental import pallas as pl
from jax.experimental.pallas import tpu as pltpu
from jax.sharding import PartitionSpec as P

LABELS = 4
PIVOT_FLOOR = 1e-7
LO, HI = 3, 4
Z_WIDTHS = (4, 3, 3, 3)
Z_PLANES = [(a, i) for a, width in enumerate(Z_WIDTHS) for i in range(width)]
CORNER_WIDTHS = (3, 3, 3, 2)
CORNERS = [(a, i) for a, width in enumerate(CORNER_WIDTHS) for i in range(width)]
PAIR = 4096.0
CHUNKS = 4
VMEM = pltpu.VMEM


def even_partner(i, count):
    return i ^ 1 if (i ^ 1) < count else i


def odd_partner(i, count):
    j = ((i + 1) ^ 1) - 1
    return j if 0 <= j < count else i


def exchanged(array, axes, counts, pair):
    parts, nz, ny = counts
    route = []
    for p in range(parts):
        for z in range(nz):
            for y in range(ny):
                q = (p,) + pair(z, y)
                if q == (p, z, y):
                    q = (even_partner(p, parts), z, y)
                source, target = ((a * nz + b) * ny + c for a, b, c in ((p, z, y), q))
                if source != target:
                    route.append((source, target))
    return lax.ppermute(array, axes, route)


def tile_pairs(sources, up, out):
    rows, cols = sources[0][0].shape[-2:]
    row = lax.broadcasted_iota(jnp.int32, (8, cols), 0)
    tile = pl.multiple_of(up * (rows - 8), 8)
    first = (row >= 4) == (up == 1)
    for k in range(0, len(sources), 2):
        (ra, *pa), (rb, *pb) = sources[k], sources[min(k + 1, len(sources) - 1)]
        a = ra[(*pa, pl.ds(tile, 8), slice(None))]
        b = rb[(*pb, pl.ds(tile, 8), slice(None))]
        out[k // 2] = jnp.where(first, a, pltpu.roll(b, 4, 0))


def interleave(cols, back=False):
    tiles = cols // 128
    i, j = (lax.broadcasted_iota(jnp.int32, (cols, cols), n) for n in ((1, 0) if back else (0, 1)))
    return (i == tiles * (j % 128) + j // 128).astype(jnp.float32).astype(jnp.bfloat16)


def pack_kernel(natural, arrays, z_even, z_odd, y_even, y_odd, d_even, d_odd):
    cols = natural.shape[-1]
    flat = natural[...].reshape(-1, cols).astype(jnp.float32).astype(jnp.bfloat16)
    turned = jnp.dot(flat, interleave(cols), preferred_element_type=jnp.float32)
    turned = turned.reshape(arrays.shape)
    arrays[0] = turned[0]
    arrays[1:] = turned[1:] + 1.0
    z_is_odd, y_is_odd = lax.axis_index("gz") % 2, lax.axis_index("gy") % 2
    depth = arrays.shape[1]
    z_ups, y_ups = (1 - z_is_odd, z_is_odd), (1 - y_is_odd, y_is_odd)
    for up, out in zip(z_ups, (z_even, z_odd)):
        for n, (a, i) in enumerate(Z_PLANES):
            out[n] = arrays[a, up * (depth - Z_WIDTHS[a]) + i]
    planes = [(arrays, a, p) for a in range(4) for p in range(depth)]
    for up, out in zip(y_ups, (y_even, y_odd)):
        tile_pairs(planes, up, out)
    for up, out in zip(z_ups, (d_even, d_odd)):
        corners = [(arrays, a, up * (depth - CORNER_WIDTHS[a]) + i) for a, i in CORNERS]
        tile_pairs(corners, y_ups[1], out)


def pack(arrays):
    _, depth, rows, cols = arrays.shape
    sizes = [(len(Z_PLANES), rows)] * 2 + [(2 * depth, 8)] * 2 + [(len(CORNERS) // 2 + 1, 8)] * 2
    return pl.pallas_call(
        pack_kernel,
        out_shape=[jax.ShapeDtypeStruct(arrays.shape, jnp.float32)]
        + [jax.ShapeDtypeStruct((*size, cols), jnp.float32) for size in sizes],
        in_specs=[pl.BlockSpec(memory_space=VMEM)],
        out_specs=[pl.BlockSpec(memory_space=VMEM)] * 7,
        compiler_params=pltpu.CompilerParams(vmem_limit_bytes=16 * 2**20),
    )(arrays)


def relay_kernel(
    z_even, z_odd, y_odd, d_even, d_odd, before, after, d_before, d_after, relay
):
    z_is_even = lax.axis_index("gz") % 2 == 0
    y_is_odd = lax.axis_index("gy") % 2
    for n in range(len(Z_PLANES)):
        e, o = z_even[n], z_odd[n]
        before[n] = jnp.where(z_is_even, o, e)
        after[n] = jnp.where(z_is_even, e, o)
    sources = []
    for a, i in CORNERS:
        n = Z_PLANES.index((a, 0))
        sources += [(before, n + Z_WIDTHS[a] - CORNER_WIDTHS[a] + i), (after, n + i)]
    tile_pairs(sources, 1 - y_is_odd, relay)

    def unpack(out, n, pair):
        out[n] = pair
        if n + 1 < out.shape[0]:
            out[n + 1] = pltpu.roll(pair, 4, 0)

    for k in range(d_even.shape[0]):
        e, o = d_even[k], d_odd[k]
        unpack(d_before, 2 * k, jnp.where(z_is_even, o, e))
        unpack(d_after, 2 * k, jnp.where(z_is_even, e, o))


def relayed(z_even, z_odd, y_odd, d_even, d_odd):
    cols = z_even.shape[2]
    shapes = [z_even.shape] * 2 + [(len(CORNERS), 8, cols)] * 3
    return pl.pallas_call(
        relay_kernel,
        out_shape=[jax.ShapeDtypeStruct(shape, jnp.float32) for shape in shapes],
        in_specs=[pl.BlockSpec(memory_space=VMEM)] * 5,
        out_specs=[pl.BlockSpec(memory_space=VMEM)] * 5,
        compiler_params=pltpu.CompilerParams(vmem_limit_bytes=16 * 2**20),
    )(z_even, z_odd, y_odd, d_even, d_odd)


def krylov_steps(counts, depth, rows, cols, m_pad, w_pad, free, b_pad, v1, v2, acc, fields, loops):
    _, nz, ny = counts
    zi, yi = lax.axis_index("gz"), lax.axis_index("gy")
    wide = rows + 8
    f32 = jnp.float32
    ring_row = lax.broadcasted_iota(jnp.int32, (8, cols), 0)
    own = slice(0, rows)
    ring = slice(rows, wide)

    def put(a, plane, where, values):
        if a == 0:
            m_pad[0, plane, where, :] = jnp.where(
                values == 0, 1.0, jnp.where(values == 1, PAIR, 0.0)
            )
            m_pad[1, plane, where, :] = jnp.where(
                values == 2, 1.0, jnp.where(values == 3, PAIR, 0.0)
            )
        else:
            w_pad[a - 1, plane, where, :] = values

    def cut_edges(planes):
        for p, at_rim in ((LO + depth - 1, zi == nz - 1), (LO - 1, zi == 0)):
            if p in planes:
                w_pad[0, p] = jnp.where(at_rim, 0.0, w_pad[0, p])
        x_end = slice(cols - 128, cols)
        last_x = lax.broadcasted_iota(jnp.int32, (wide, 128), 1) == 127
        at_end = (yi == ny - 1) & (ring_row == 7)
        at_start = (yi == 0) & (ring_row == 7)
        for p in planes:
            here = slice(rows - 8, rows)
            w_pad[1, p, here, :] = jnp.where(at_end, 0.0, w_pad[1, p, here, :])
            w_pad[1, p, ring, :] = jnp.where(at_start, 0.0, w_pad[1, p, ring, :])
            w_pad[2, p, :, x_end] = jnp.where(last_x, 0.0, w_pad[2, p, :, x_end])

    lanes = [slice(l, l + 128) for l in range(0, cols, 128)]
    lane = lax.broadcasted_iota(jnp.int32, (8, 128), 1)
    row = lax.broadcasted_iota(jnp.int32, (8, 128), 0)

    row_tiles = range(0, wide, 8)

    def tile(ref, index, r):
        return [ref[(*index, slice(r, r + 8), l)] for l in lanes]

    def plane(ref, *index):
        return [tile(ref, index, r) for r in row_tiles]

    def store(ref, index, r, values):
        for l, x in zip(lanes, values):
            ref[(*index, slice(r, r + 8), l)] = x

    def store_plane(ref, index, values):
        for r, x in zip(row_tiles, values):
            store(ref, index, r, x)

    def each(f, *planes):
        return [[f(*x) for x in zip(*rows_)] for rows_ in zip(*planes)]

    def next_x(v):
        return [x[1:] + [pltpu.roll(x[0], 127, 1)] for x in v]

    def prev_x(v):
        return [[pltpu.roll(x[-1], 1, 1)] + x[:-1] for x in v]

    def next_y(v):
        pair = lambda a, b: pltpu.roll(jnp.where(row == 0, b, a), 7, 0)
        return each(pair, v, v[1:] + v[:1])

    def prev_y(v):
        pair = lambda a, b: pltpu.roll(jnp.where(row == 7, b, a), 1, 0)
        return each(pair, v, v[-1:] + v[:-1])

    def times(x, y):
        return each(lambda a, b: a * b, x, y)

    def repeated(count, body):
        if loops:
            lax.fori_loop(0, count, body, 0)
        else:
            for n in range(count):
                body(n, 0)

    def prepare(*ranges):
        def body(h, _):
            for start, count in ranges:
                here = plane(m_pad, h, start)
                from_behind = times(plane(w_pad, 0, start - 1), plane(m_pad, h, start - 1))
                for p in range(start, start + count):
                    ahead = plane(m_pad, h, p + 1)
                    w_z, w_y, w_x = (plane(w_pad, i, p) for i in range(3))
                    sums_ = each(
                        lambda a, b, c, d, e, f: (a + b) + (c + d) + (e + f),
                        times(w_z, ahead), from_behind,
                        times(w_y, next_y(here)), prev_y(times(w_y, here)),
                        times(w_x, next_x(here)), prev_x(times(w_x, here)),
                    )
                    other = plane(m_pad, 1 - h, p)
                    u = each(lambda a, b: jnp.where(a + b == 0.0, 1.0, 0.0), here, other)
                    store_plane(free, (p,), u)
                    sums_ = times(sums_, u)
                    second = each(lambda x: jnp.floor(x * (1.0 / PAIR)), sums_)
                    store_plane(b_pad, (2 * h, p), each(lambda x, y: x - PAIR * y, sums_, second))
                    store_plane(b_pad, (2 * h + 1, p), second)
                    from_behind = times(w_z, here)
                    here = ahead
            return 0

        repeated(2, body)

    def flow(w, x, y):
        return each(lambda a, b, c: a * (b - c), w, x, y)

    def apply(source, target, *ranges):
        def body(c, _):
            for start, count in ranges:
                here = plane(source, c, start)
                from_behind = flow(plane(w_pad, 0, start - 1), here, plane(source, c, start - 1))
                for p in range(start, start + count):
                    ahead = plane(source, c, p + 1)
                    f_z = flow(plane(w_pad, 0, p), ahead, here)
                    f_y = flow(plane(w_pad, 1, p), next_y(here), here)
                    f_x = flow(plane(w_pad, 2, p), next_x(here), here)
                    store_plane(target, (c, p), each(
                        lambda u, a, b, c, d, e, f: u * ((a - b) + (c - d) + (e - f)),
                        plane(free, p), from_behind, f_z, prev_y(f_y), f_y, prev_x(f_x), f_x,
                    ))
                    from_behind, here = f_z, ahead
            return 0

        repeated(LABELS, body)

    half_pairs = [(a, b) for a in range(LABELS) for b in range(a, LABELS)]
    all_pairs = [(a, b) for a in range(LABELS) for b in range(LABELS)]

    def total(products):
        while len(products) > 1:
            products = [x + y for x, y in zip(products[::2], products[1::2])] + (
                [products[-1]] if len(products) % 2 else []
            )
        return products[0]

    def add_up(first, parts):
        for n, part in enumerate(parts):
            acc[first + n] = acc[first + n] + total(part)

    own_tiles = range(0, rows, 8)

    def accumulate(p, _):
        parts = [[] for _ in range(30)]
        for r in own_tiles:
            bs = [tile(b_pad, (c, p), r) for c in range(LABELS)]
            abs_ = [tile(v1, (c, p), r) for c in range(LABELS)]
            for l in range(len(lanes)):
                b, ab = [x[l] for x in bs], [x[l] for x in abs_]
                products = [b[i] * b[j] for i, j in half_pairs]
                products += [b[i] * ab[j] for i, j in half_pairs]
                products += [ab[i] * ab[j] for i, j in half_pairs]
                for part, product in zip(parts, products):
                    part.append(product)
            for c in range(LABELS):
                if fields is not None:
                    store(fields, (0, c, p - LO), r, bs[c])
                    store(fields, (1, c, p - LO), r, abs_[c])
        add_up(0, parts)
        return 0

    def accumulate_last(p, _):
        parts = [[] for _ in range(36)]
        w_z, w_y, w_x = (plane(w_pad, i, p) for i in range(3))
        degree = each(
            lambda a, b, c, d, e, f: (a + b) + (c + d) + (e + f),
            w_z, plane(w_pad, 0, p - 1), w_y, prev_y(w_y), w_x, prev_x(w_x),
        )
        qs, aabs_ = [], []
        for c in range(LABELS):
            v = plane(v2, c, p)
            qs.append(each(
                lambda d, x, a, b, e: d * x - 2.0 * (a + b + e),
                degree, v, times(w_z, plane(v2, c, p + 1)), times(w_y, next_y(v)),
                times(w_x, next_x(v)),
            ))
            aabs_.append(v)
        for t, r in enumerate(own_tiles):
            abs_ = [tile(v1, (c, p), r) for c in range(LABELS)]
            for l in range(len(lanes)):
                ab, aab, q = [x[l] for x in abs_], [x[t][l] for x in aabs_], [x[t][l] for x in qs]
                products = [ab[i] * aab[j] for i, j in half_pairs]
                products += [aab[i] * aab[j] for i, j in half_pairs]
                products += [aab[i] * q[j] for i, j in all_pairs]
                for part, product in zip(parts, products):
                    part.append(product)
            for c in range(LABELS):
                if fields is not None:
                    store(fields, (2, c, p - LO), r, aabs_[c][t])
        add_up(30, parts)
        return 0

    return types.SimpleNamespace(
        put=put, cut_edges=cut_edges, prepare=prepare,
        first=functools.partial(apply, b_pad, v1), second=functools.partial(apply, v1, v2), accumulate=accumulate, accumulate_last=accumulate_last,
        half_pairs=half_pairs, all_pairs=all_pairs, own=own, ring=ring,
    )


def unpacked(even, odd, y_is_even):
    half = lax.broadcasted_iota(jnp.int32, even.shape, 0) < 4
    from_even = half == y_is_even
    return jnp.where(from_even, even, odd), pltpu.roll(jnp.where(from_even, odd, even), 4, 0)


def inner_kernel(
    counts, arrays, y_even, y_odd, m_pad, w_pad, free, b_pad, v1, v2, acc
):
    _, depth, rows, cols = arrays.shape
    y_is_even = lax.axis_index("gy") % 2 == 0
    do = krylov_steps(counts, depth, rows, cols, m_pad, w_pad, free, b_pad, v1, v2, acc, None, False)
    for a in range(4):
        for p in range(depth):
            do.put(a, LO + p, do.own, arrays[a, p])
    for k in range(2 * depth):
        for j, x in enumerate(unpacked(y_even[k], y_odd[k], y_is_even)):
            a, p = divmod(2 * k + j, depth)
            do.put(a, LO + p, do.ring, x)
    do.cut_edges(range(LO, LO + depth))
    do.prepare((LO + 1, depth - 2))
    do.first((LO + 2, depth - 4))
    do.second((LO + 3, depth - 6))
    for n in range(66):
        acc[n] = jnp.zeros((8, 128), jnp.float32)
    lax.fori_loop(LO + 2, LO + depth - 2, do.accumulate, 0)
    lax.fori_loop(LO + 3, LO + depth - 4, do.accumulate_last, 0)


def padded_shapes(depth, rows, cols):
    planes, wide = depth + LO + HI, rows + 8
    sizes = [(2,), (3,), (), (LABELS,), (LABELS,), (LABELS,)]
    return [(*size, planes, wide, cols) for size in sizes] + [(66, 8, 128)]


def inner(counts, arrays, y_even, y_odd):
    _, depth, rows, cols = arrays.shape
    f32 = jnp.float32
    return pl.pallas_call(
        functools.partial(inner_kernel, counts),
        out_shape=[jax.ShapeDtypeStruct(x, f32) for x in padded_shapes(depth, rows, cols)],
        in_specs=[pl.BlockSpec(memory_space=VMEM)] * 3,
        out_specs=[pl.BlockSpec(memory_space=VMEM)] * 7,
        cost_estimate=pl.CostEstimate(flops=10**7, bytes_accessed=10**6, transcendentals=0),
        compiler_params=pltpu.CompilerParams(vmem_limit_bytes=20 * 2**20),
    )(arrays, y_even, y_odd)


def outer_kernel(
    counts, before, after, d_before, d_after, relay,
    m_in, w_in, free_in, b_in, v1_in, v2_in, acc_in,
    fields, moments,
    m_pad, w_pad, free, b_pad, v1, v2, acc, sums,
):
    depth, rows, cols = fields.shape[2:]
    f32 = jnp.float32
    y_is_even = lax.axis_index("gy") % 2 == 0
    do = krylov_steps(counts, depth, rows, cols, m_pad, w_pad, free, b_pad, v1, v2, acc, fields, True)
    for n, (a, i) in enumerate(Z_PLANES):
        do.put(a, LO + depth + i, do.own, after[n])
        if LO - Z_WIDTHS[a] + i >= 0:
            do.put(a, LO - Z_WIDTHS[a] + i, do.own, before[n])
    for n, (a, i) in enumerate(CORNERS):
        even = relay[n]
        even_after = pltpu.roll(even, 4, 0)
        do.put(a, LO - CORNER_WIDTHS[a] + i, do.ring, unpacked(even, d_before[n], y_is_even)[0])
        do.put(a, LO + depth + i, do.ring, unpacked(even_after, d_after[n], y_is_even)[0])
    zero_tile = jnp.zeros((8, cols), f32)
    do.put(0, LO + depth + 3, do.ring, zero_tile)
    do.put(3, LO + depth + 2, do.ring, zero_tile)
    do.put(3, 0, do.ring, zero_tile)
    low, high = LO, LO + depth
    for source, target, planes in (
        (m_in, m_pad, (low, low + 1, high - 2, high - 1)),
        (w_in, w_pad, range(low, high)),
        (b_in, b_pad, (low + 1, low + 2, high - 3, high - 2)),
        (v1_in, v1, (low + 2, low + 3, high - 4, high - 3)),
        (v2_in, v2, (low + 3, high - 4)),
    ):
        for p in planes:
            for c in range(source.shape[0]):
                target[c, p] = source[c, p]
    for p in (low + 1, low + 2, high - 3, high - 2):
        free[p] = free_in[p]
    for n in range(66):
        acc[n] = acc_in[n]
    do.cut_edges([p for p in range(high + 3) if p not in range(low, high)])

    do.prepare((1, low), (high - 1, 4))
    do.first((2, low), (high - 2, 4))
    do.second((3, low), (high - 3, 4))
    lax.fori_loop(0, 4, lambda i, x: do.accumulate(low + i + (i // 2) * (depth - 4), x), 0)
    lax.fori_loop(
        0, depth - 1, lambda i, x: do.accumulate_last(low + i + jnp.where(i >= 3, 1, 0), x), 0
    )

    half_pairs, all_pairs = do.half_pairs, do.all_pairs
    low, high = [acc[n] for n in range(30)], [acc[30 + n] for n in range(36)]
    kept = {}
    for k in range(5):
        part = low[10 * k : 10 * k + 10] if k < 3 else high[10 * (k - 3) : 10 * (k - 3) + 10]
        for (a, b), x in zip(half_pairs, part):
            kept[k, a, b] = kept[k, b, a] = x
    last = dict(zip(all_pairs, high[20:]))
    for a, b in half_pairs:
        kept[5, a, b] = kept[5, b, a] = 0.5 * (last[a, b] + last[b, a])
    for k in range(6):
        for a, b in half_pairs:
            x = jnp.sum(kept[k, a, b], axis=0, keepdims=True)
            for i, j in {(a, b), (b, a)}:
                at = (2 * k + j // 2) * 8 + (j % 2) * 4 + i
                sums[at : at + 1, :] = x
    lane = lax.broadcasted_iota(jnp.int32, (8, 128), 1)
    packed = jnp.zeros((8, 128), f32)
    for g in range(12):
        x = jnp.sum(sums[8 * g : 8 * g + 8, :], axis=1, keepdims=True)
        packed = jnp.where(lane == g, x, packed)
    moments[...] = packed


def outer(counts, shape, halos, insides):
    _, depth, rows, cols = shape
    f32 = jnp.float32
    return pl.pallas_call(
        functools.partial(outer_kernel, counts),
        out_shape=[
            jax.ShapeDtypeStruct((3, LABELS, depth, rows, cols), f32),
            jax.ShapeDtypeStruct((8, 128), f32),
        ],
        in_specs=[pl.BlockSpec(memory_space=VMEM)] * 12,
        out_specs=[pl.BlockSpec(memory_space=VMEM)] * 2,
        scratch_shapes=[VMEM(x, f32) for x in padded_shapes(depth, rows, cols)]
        + [VMEM((96, 128), f32)],
        compiler_params=pltpu.CompilerParams(vmem_limit_bytes=28 * 2**20),
    )(*halos, *insides)


def solved(moment, sides, floor):
    n = 3 * LABELS
    system = {
        (i, j): moment(i // LABELS + j // LABELS + 1, i % LABELS, j % LABELS)
        for i in range(n) for j in range(i + 1)
    }
    right = dict(enumerate(sides))
    first = {k: system[k, k] for k in range(n)}
    lower, inverse = {}, {}
    for k in range(n):
        pivot = system[k, k]
        sound = pivot > floor * first[k]
        inverse[k] = jnp.where(sound, 1.0 / jnp.where(sound, pivot, 1.0), 0.0)
        for i in range(k + 1, n):
            lower[i, k] = system[i, k] * inverse[k]
        for i in range(k + 1, n):
            for j in range(k + 1, i + 1):
                system[i, j] = system[i, j] - lower[i, k] * system[j, k]
            right[i] = right[i] - lower[i, k] * right[k]
    for k in reversed(range(n)):
        x = right[k] * inverse[k]
        for i in range(k + 1, n):
            x = x - lower[i, k] * right[i]
        right[k] = x
    return [right[k] for k in range(n)]


def combine_kernel(
    mine, theirs, fields, b_in, v1_in, v2_in, natural, out, spread, coeffs, mixed, buffer, sems
):
    f32 = jnp.float32
    _, depth, rows, cols = natural.shape
    sums = mine[...] + theirs[...]
    columns = [jnp.broadcast_to(sums[:, g : g + 1], (8, 128)) for g in range(12)]
    for g in range(12):
        spread[g] = columns[g]

    def moment(k, a, b):
        a, b = min(a, b), max(a, b)
        at = (b % 2) * 4 + a
        return jnp.broadcast_to(spread[2 * k + b // 2, at : at + 1, :], (8, 128))

    sides = []
    for k in range(3):
        for a in range(LABELS):
            x = columns[2 * k + a // 2]
            sides.append(pltpu.roll(x, 4, 0) if a % 2 else x)
    for k, x in enumerate(solved(moment, sides, PIVOT_FLOOR)):
        coeffs[k] = x

    back = interleave(cols, back=True)
    chunk = depth // CHUNKS

    def field(k, p, cut):
        n, c = divmod(k, LABELS)
        inside = range(2, depth - 2) if n < 2 else range(3, depth - 4)
        if p in inside:
            return (b_in, v1_in, v2_in)[n][(c, LO + p) + cut]
        return fields[(n, c, p) + cut]

    def combine(n):
        for first in range(0, LABELS, 2):
            weights = {
                (k, c): jnp.broadcast_to(coeffs[k, c : c + 1, :], (8, 128))
                for k in range(3 * LABELS) for c in (first, first + 1)
            }
            for p in range(n * chunk, n * chunk + chunk):
                for r in range(0, rows, 8):
                    for l in range(0, cols, 128):
                        cut = (slice(r, r + 8), slice(l, l + 128))
                        v = [field(k, p, cut) for k in range(3 * LABELS)]
                        for c in (first, first + 1):
                            s = [v[k] * weights[k, c] for k in range(3 * LABELS)]
                            while len(s) > 1:
                                s = [x + y for x, y in zip(s[::2], s[1::2])] + (
                                    [s[-1]] if len(s) % 2 else []
                                )
                            mixed[(c, p) + cut] = s[0]

    def turn_back(n):
        planes = slice(n * chunk, n * chunk + chunk)
        x = mixed[:, planes].reshape(LABELS * chunk * rows, cols)
        high = x.astype(jnp.bfloat16)
        low = (x - high.astype(f32)).astype(jnp.bfloat16)
        x = jnp.dot(high, back, preferred_element_type=f32)
        x = x + jnp.dot(low, back, preferred_element_type=f32)
        x = x.reshape(LABELS, chunk, rows, cols)
        for c in range(LABELS):
            buffer[c, planes] = jnp.where(natural[0, planes] == c, 1.0, x[c])

    copies = [
        pltpu.make_async_copy(
            buffer.at[:, n * chunk : (n + 1) * chunk], out.at[:, n * chunk : (n + 1) * chunk],
            sems.at[n],
        )
        for n in range(CHUNKS)
    ]
    combine(0)
    for n in range(CHUNKS):
        if n + 1 < CHUNKS:
            combine(n + 1)
        turn_back(n)
        copies[n].start()
    for copy in copies:
        copy.wait()


def combined(mine, theirs, fields, insides, natural):
    _, depth, rows, cols = natural.shape
    f32 = jnp.float32
    return pl.pallas_call(
        combine_kernel,
        out_shape=jax.ShapeDtypeStruct((LABELS, depth, rows, cols), f32),
        in_specs=[pl.BlockSpec(memory_space=VMEM)] * 7,
        out_specs=pl.BlockSpec(memory_space=pltpu.HBM),
        scratch_shapes=[
            VMEM((12, 8, 128), f32),
            VMEM((3 * LABELS, 8, 128), f32),
            VMEM((LABELS, depth, rows, cols), f32),
            VMEM((LABELS, depth, rows, cols), f32),
            pltpu.SemaphoreType.DMA((CHUNKS,)),
        ],
        compiler_params=pltpu.CompilerParams(vmem_limit_bytes=32 * 2**20),
    )(mine, theirs, fields, *insides, natural)


def per_device(counts, tags, depth_affinity, row_affinity, column_affinity):
    parts, nz, ny = counts
    natural = jnp.stack([tags, depth_affinity, row_affinity, column_affinity])
    axes = ("parts", "gz", "gy")
    ze, zo = (lambda z: even_partner(z, nz)), (lambda z: odd_partner(z, nz))
    ye, yo = (lambda y: even_partner(y, ny)), (lambda y: odd_partner(y, ny))

    def swap(array, pz, py):
        def pair(z, y):
            if pz and pz(z) == z:
                return z, ye(y)
            if py and py(y) == y:
                return z, y
            return pz(z) if pz else z, py(y) if py else y
        return exchanged(array, axes, counts, pair)

    arrays, z_even, z_odd, y_even, y_odd, d_even, d_odd = pack(natural)
    y_odd = swap(y_odd, None, yo)
    insides = inner(counts, arrays, swap(y_even, None, ye), y_odd)
    *halos, relay = relayed(
        swap(z_even, ze, None), swap(z_odd, zo, None), y_odd, swap(d_even, ze, yo),
        swap(d_odd, zo, yo),
    )
    halos = [*halos, swap(relay, None, ye)]
    fields, moments = outer(counts, arrays.shape, halos, insides)

    steps = [lambda z, y: (z, y ^ 1)]
    steps += [lambda z, y, d=d: (z, y ^ d ^ 1) for d in powers(ny)[1:]]
    steps += [lambda z, y, d=d: (z ^ d, y ^ 1) for d in powers(nz)]
    for n, pair in enumerate(steps):
        theirs = exchanged(moments, axes, counts, pair)
        if n < len(steps) - 1:
            moments = moments + theirs
    return combined(moments, theirs, fields, insides[3:6], natural)


def powers(count):
    return [1 << n for n in range(count.bit_length() - 1)]


def solution(mesh):
    counts = tuple(mesh.shape[axis] for axis in ("parts", "gz", "gy"))
    placed = P(("parts", "gz"), "gy", None)
    return jax.shard_map(
        functools.partial(per_device, counts),
        mesh=mesh,
        in_specs=(placed,) * 4,
        out_specs=P(None, ("parts", "gz"), "gy", None),
        check_vma=False,
    )
```

```python
import functools
import types

import jax
import jax.numpy as jnp
from jax import lax
from jax.experimental import pallas as pl
from jax.experimental.pallas import tpu as pltpu
from jax.sharding import PartitionSpec as P

LABELS = 4
PIVOT_FLOOR = 1e-7
LO, HI = 3, 4
Z_WIDTHS = (4, 3, 3, 3)
Z_PLANES = [(a, i) for a, width in enumerate(Z_WIDTHS) for i in range(width)]
CORNER_WIDTHS = (3, 3, 3, 2)
CORNERS = [(a, i) for a, width in enumerate(CORNER_WIDTHS) for i in range(width)]
SLOTS = [
    (0, 0, 0, 1), (0, 4, 1, 1), (1, 0, 2, 1), (1, 4, 0, 2), (1, 6, 1, 2), (2, 0, 2, 2),
    (2, 2, 3, 1), (2, 4, 0, 3), (2, 5, 1, 3), (2, 6, 2, 3), (2, 7, 3, 2),
]
PAIR = 4096.0
CHUNKS = 4
VMEM = pltpu.VMEM


def even_partner(i, count):
    return i ^ 1 if (i ^ 1) < count else i


def odd_partner(i, count):
    j = ((i + 1) ^ 1) - 1
    return j if 0 <= j < count else i


def exchanged(array, axes, counts, pair):
    parts, nz, ny = counts
    route = []
    for p in range(parts):
        for z in range(nz):
            for y in range(ny):
                q = (p,) + pair(z, y)
                if q == (p, z, y):
                    q = (even_partner(p, parts), z, y)
                source, target = ((a * nz + b) * ny + c for a, b, c in ((p, z, y), q))
                if source != target:
                    route.append((source, target))
    return lax.ppermute(array, axes, route)


def tile_pairs(sources, up, out):
    rows, cols = sources[0][0].shape[-2:]
    row = lax.broadcasted_iota(jnp.int32, (8, cols), 0)
    tile = pl.multiple_of(up * (rows - 8), 8)
    first = (row >= 4) == (up == 1)
    for k in range(0, len(sources), 2):
        (ra, *pa), (rb, *pb) = sources[k], sources[min(k + 1, len(sources) - 1)]
        a = ra[(*pa, pl.ds(tile, 8), slice(None))]
        b = rb[(*pb, pl.ds(tile, 8), slice(None))]
        out[k // 2] = jnp.where(first, a, pltpu.roll(b, 4, 0))


def interleave(cols, back=False):
    tiles = cols // 128
    i, j = (lax.broadcasted_iota(jnp.int32, (cols, cols), n) for n in ((1, 0) if back else (0, 1)))
    return (i == tiles * (j % 128) + j // 128).astype(jnp.float32).astype(jnp.bfloat16)


def moved(tile, rows, up):
    rows %= 8
    if rows == 0:
        return tile
    return jnp.where(up == 1, pltpu.roll(tile, 8 - rows, 0), pltpu.roll(tile, rows, 0))


def pack_corner(arrays, z_up, y_up, out):
    _, depth, rows, cols = arrays.shape
    row = lax.broadcasted_iota(jnp.int32, (8, cols), 0)
    away = jnp.where(y_up == 1, 7 - row, row)
    tile = pl.multiple_of(y_up * (rows - 8), 8)
    packed = {}
    for t, first, a, k in SLOTS:
        x = arrays[a, z_up * (depth - 2 * k + 1) + k - 1, pl.ds(tile, 8), :]
        x = moved(x, first, y_up)
        packed[t] = jnp.where(away >= first, x, packed[t]) if first else x
    for t, x in packed.items():
        out[t] = x


def pack_kernel(natural, arrays, z_even, z_odd, y_even, y_odd, d_even, d_odd):
    cols = natural.shape[-1]
    flat = natural[...].reshape(-1, cols).astype(jnp.float32).astype(jnp.bfloat16)
    turned = jnp.dot(flat, interleave(cols), preferred_element_type=jnp.float32)
    turned = turned.reshape(arrays.shape)
    arrays[0] = turned[0]
    arrays[1:] = turned[1:] + 1.0
    z_is_odd, y_is_odd = lax.axis_index("gz") % 2, lax.axis_index("gy") % 2
    depth = arrays.shape[1]
    z_ups, y_ups = (1 - z_is_odd, z_is_odd), (1 - y_is_odd, y_is_odd)
    for up, out in zip(z_ups, (z_even, z_odd)):
        for n, (a, i) in enumerate(Z_PLANES):
            out[n] = arrays[a, up * (depth - Z_WIDTHS[a]) + i]
    planes = [(arrays, a, p) for a in range(4) for p in range(depth)]
    for up, out in zip(y_ups, (y_even, y_odd)):
        tile_pairs(planes, up, out)
    for up, out in zip(z_ups, (d_even, d_odd)):
        pack_corner(arrays, up, y_ups[1], out)


def pack(arrays):
    _, depth, rows, cols = arrays.shape
    sizes = [(len(Z_PLANES), rows)] * 2 + [(2 * depth, 8)] * 2 + [(3, 8)] * 2
    return pl.pallas_call(
        pack_kernel,
        out_shape=[jax.ShapeDtypeStruct(arrays.shape, jnp.float32)]
        + [jax.ShapeDtypeStruct((*size, cols), jnp.float32) for size in sizes],
        in_specs=[pl.BlockSpec(memory_space=VMEM)],
        out_specs=[pl.BlockSpec(memory_space=VMEM)] * 7,
        compiler_params=pltpu.CompilerParams(vmem_limit_bytes=16 * 2**20),
    )(arrays)


def relay_kernel(z_even, z_odd, y_odd, before, after, relay):
    z_is_even = lax.axis_index("gz") % 2 == 0
    y_is_odd = lax.axis_index("gy") % 2
    for n in range(len(Z_PLANES)):
        e, o = z_even[n], z_odd[n]
        before[n] = jnp.where(z_is_even, o, e)
        after[n] = jnp.where(z_is_even, e, o)
    sources = []
    for a, i in CORNERS:
        n = Z_PLANES.index((a, 0))
        sources += [(before, n + Z_WIDTHS[a] - CORNER_WIDTHS[a] + i), (after, n + i)]
    tile_pairs(sources, 1 - y_is_odd, relay)


def corner_kernel(d_even, d_odd, d_before, d_after):
    z_is_even = lax.axis_index("gz") % 2 == 0
    y_is_odd = lax.axis_index("gy") % 2
    for out, x, y in ((d_before, d_odd, d_even), (d_after, d_even, d_odd)):
        tiles = [jnp.where(z_is_even, x[t], y[t]) for t in range(3)]
        for t, first, a, k in SLOTS:
            i = CORNER_WIDTHS[a] - k if out is d_before else k - 1
            out[CORNERS.index((a, i))] = moved(tiles[t], -first, 1 - y_is_odd)


def cornered(d_even, d_odd):
    cols = d_even.shape[2]
    return pl.pallas_call(
        corner_kernel,
        out_shape=[jax.ShapeDtypeStruct((len(CORNERS), 8, cols), jnp.float32)] * 2,
        in_specs=[pl.BlockSpec(memory_space=VMEM)] * 2,
        out_specs=[pl.BlockSpec(memory_space=VMEM)] * 2,
        cost_estimate=pl.CostEstimate(flops=2 * 10**9, bytes_accessed=10**6, transcendentals=0),
        compiler_params=pltpu.CompilerParams(vmem_limit_bytes=16 * 2**20),
    )(d_even, d_odd)


def relayed(z_even, z_odd, y_odd):
    cols = z_even.shape[2]
    shapes = [z_even.shape] * 2 + [(len(CORNERS), 8, cols)]
    return pl.pallas_call(
        relay_kernel,
        out_shape=[jax.ShapeDtypeStruct(shape, jnp.float32) for shape in shapes],
        in_specs=[pl.BlockSpec(memory_space=VMEM)] * 3,
        out_specs=[pl.BlockSpec(memory_space=VMEM)] * 3,
        compiler_params=pltpu.CompilerParams(vmem_limit_bytes=16 * 2**20),
    )(z_even, z_odd, y_odd)


def krylov_steps(counts, depth, rows, cols, m_pad, w_pad, free, b_pad, v1, v2, acc, fields, loops):
    _, nz, ny = counts
    zi, yi = lax.axis_index("gz"), lax.axis_index("gy")
    wide = rows + 8
    f32 = jnp.float32
    ring_row = lax.broadcasted_iota(jnp.int32, (8, cols), 0)
    own = slice(0, rows)
    ring = slice(rows, wide)

    def put(a, plane, where, values):
        if a == 0:
            m_pad[0, plane, where, :] = jnp.where(
                values == 0, 1.0, jnp.where(values == 1, PAIR, 0.0)
            )
            m_pad[1, plane, where, :] = jnp.where(
                values == 2, 1.0, jnp.where(values == 3, PAIR, 0.0)
            )
        else:
            w_pad[a - 1, plane, where, :] = values

    def cut_edges(planes):
        for p, at_rim in ((LO + depth - 1, zi == nz - 1), (LO - 1, zi == 0)):
            if p in planes:
                w_pad[0, p] = jnp.where(at_rim, 0.0, w_pad[0, p])
        x_end = slice(cols - 128, cols)
        last_x = lax.broadcasted_iota(jnp.int32, (wide, 128), 1) == 127
        at_end = (yi == ny - 1) & (ring_row == 7)
        at_start = (yi == 0) & (ring_row == 7)
        for p in planes:
            here = slice(rows - 8, rows)
            w_pad[1, p, here, :] = jnp.where(at_end, 0.0, w_pad[1, p, here, :])
            w_pad[1, p, ring, :] = jnp.where(at_start, 0.0, w_pad[1, p, ring, :])
            w_pad[2, p, :, x_end] = jnp.where(last_x, 0.0, w_pad[2, p, :, x_end])

    lanes = [slice(l, l + 128) for l in range(0, cols, 128)]
    lane = lax.broadcasted_iota(jnp.int32, (8, 128), 1)
    row = lax.broadcasted_iota(jnp.int32, (8, 128), 0)

    row_tiles = range(0, wide, 8)

    def tile(ref, index, r):
        return [ref[(*index, slice(r, r + 8), l)] for l in lanes]

    def plane(ref, *index):
        return [tile(ref, index, r) for r in row_tiles]

    def store(ref, index, r, values):
        for l, x in zip(lanes, values):
            ref[(*index, slice(r, r + 8), l)] = x

    def store_plane(ref, index, values):
        for r, x in zip(row_tiles, values):
            store(ref, index, r, x)

    def each(f, *planes):
        return [[f(*x) for x in zip(*rows_)] for rows_ in zip(*planes)]

    def next_x(v):
        return [x[1:] + [pltpu.roll(x[0], 127, 1)] for x in v]

    def prev_x(v):
        return [[pltpu.roll(x[-1], 1, 1)] + x[:-1] for x in v]

    def next_y(v):
        pair = lambda a, b: pltpu.roll(jnp.where(row == 0, b, a), 7, 0)
        return each(pair, v, v[1:] + v[:1])

    def prev_y(v):
        pair = lambda a, b: pltpu.roll(jnp.where(row == 7, b, a), 1, 0)
        return each(pair, v, v[-1:] + v[:-1])

    def times(x, y):
        return each(lambda a, b: a * b, x, y)

    def repeated(count, body):
        if loops:
            lax.fori_loop(0, count, body, 0)
        else:
            for n in range(count):
                body(n, 0)

    def prepare(*ranges):
        def body(h, _):
            for start, count in ranges:
                here = plane(m_pad, h, start)
                from_behind = times(plane(w_pad, 0, start - 1), plane(m_pad, h, start - 1))
                for p in range(start, start + count):
                    ahead = plane(m_pad, h, p + 1)
                    w_z, w_y, w_x = (plane(w_pad, i, p) for i in range(3))
                    sums_ = each(
                        lambda a, b, c, d, e, f: (a + b) + (c + d) + (e + f),
                        times(w_z, ahead), from_behind,
                        times(w_y, next_y(here)), prev_y(times(w_y, here)),
                        times(w_x, next_x(here)), prev_x(times(w_x, here)),
                    )
                    other = plane(m_pad, 1 - h, p)
                    u = each(lambda a, b: jnp.where(a + b == 0.0, 1.0, 0.0), here, other)
                    store_plane(free, (p,), u)
                    sums_ = times(sums_, u)
                    second = each(lambda x: jnp.floor(x * (1.0 / PAIR)), sums_)
                    store_plane(b_pad, (2 * h, p), each(lambda x, y: x - PAIR * y, sums_, second))
                    store_plane(b_pad, (2 * h + 1, p), second)
                    from_behind = times(w_z, here)
                    here = ahead
            return 0

        repeated(2, body)

    def flow(w, x, y):
        return each(lambda a, b, c: a * (b - c), w, x, y)

    def apply(source, target, *ranges):
        def body(c, _):
            for start, count in ranges:
                here = plane(source, c, start)
                from_behind = flow(plane(w_pad, 0, start - 1), here, plane(source, c, start - 1))
                for p in range(start, start + count):
                    ahead = plane(source, c, p + 1)
                    f_z = flow(plane(w_pad, 0, p), ahead, here)
                    f_y = flow(plane(w_pad, 1, p), next_y(here), here)
                    f_x = flow(plane(w_pad, 2, p), next_x(here), here)
                    store_plane(target, (c, p), each(
                        lambda u, a, b, c, d, e, f: u * ((a - b) + (c - d) + (e - f)),
                        plane(free, p), from_behind, f_z, prev_y(f_y), f_y, prev_x(f_x), f_x,
                    ))
                    from_behind, here = f_z, ahead
            return 0

        repeated(LABELS, body)

    half_pairs = [(a, b) for a in range(LABELS) for b in range(a, LABELS)]
    all_pairs = [(a, b) for a in range(LABELS) for b in range(LABELS)]

    def total(products):
        while len(products) > 1:
            products = [x + y for x, y in zip(products[::2], products[1::2])] + (
                [products[-1]] if len(products) % 2 else []
            )
        return products[0]

    def add_up(first, parts):
        for n, part in enumerate(parts):
            acc[first + n] = acc[first + n] + total(part)

    own_tiles = range(0, rows, 8)

    def accumulate(p, _):
        parts = [[] for _ in range(30)]
        for r in own_tiles:
            bs = [tile(b_pad, (c, p), r) for c in range(LABELS)]
            abs_ = [tile(v1, (c, p), r) for c in range(LABELS)]
            for l in range(len(lanes)):
                b, ab = [x[l] for x in bs], [x[l] for x in abs_]
                products = [b[i] * b[j] for i, j in half_pairs]
                products += [b[i] * ab[j] for i, j in half_pairs]
                products += [ab[i] * ab[j] for i, j in half_pairs]
                for part, product in zip(parts, products):
                    part.append(product)
            for c in range(LABELS):
                if fields is not None:
                    store(fields, (0, c, p - LO), r, bs[c])
                    store(fields, (1, c, p - LO), r, abs_[c])
        add_up(0, parts)
        return 0

    def accumulate_last(p, _):
        parts = [[] for _ in range(36)]
        w_z, w_y, w_x = (plane(w_pad, i, p) for i in range(3))
        degree = each(
            lambda a, b, c, d, e, f: (a + b) + (c + d) + (e + f),
            w_z, plane(w_pad, 0, p - 1), w_y, prev_y(w_y), w_x, prev_x(w_x),
        )
        qs, aabs_ = [], []
        for c in range(LABELS):
            v = plane(v2, c, p)
            qs.append(each(
                lambda d, x, a, b, e: d * x - 2.0 * (a + b + e),
                degree, v, times(w_z, plane(v2, c, p + 1)), times(w_y, next_y(v)),
                times(w_x, next_x(v)),
            ))
            aabs_.append(v)
        for t, r in enumerate(own_tiles):
            abs_ = [tile(v1, (c, p), r) for c in range(LABELS)]
            for l in range(len(lanes)):
                ab, aab, q = [x[l] for x in abs_], [x[t][l] for x in aabs_], [x[t][l] for x in qs]
                products = [ab[i] * aab[j] for i, j in half_pairs]
                products += [aab[i] * aab[j] for i, j in half_pairs]
                products += [aab[i] * q[j] for i, j in all_pairs]
                for part, product in zip(parts, products):
                    part.append(product)
            for c in range(LABELS):
                if fields is not None:
                    store(fields, (2, c, p - LO), r, aabs_[c][t])
        add_up(30, parts)
        return 0

    return types.SimpleNamespace(
        put=put, cut_edges=cut_edges, prepare=prepare,
        first=functools.partial(apply, b_pad, v1), second=functools.partial(apply, v1, v2), accumulate=accumulate, accumulate_last=accumulate_last,
        half_pairs=half_pairs, all_pairs=all_pairs, own=own, ring=ring,
    )


def unpacked(even, odd, y_is_even):
    half = lax.broadcasted_iota(jnp.int32, even.shape, 0) < 4
    from_even = half == y_is_even
    return jnp.where(from_even, even, odd), pltpu.roll(jnp.where(from_even, odd, even), 4, 0)


def inner_kernel(
    counts, arrays, y_even, y_odd, m_pad, w_pad, free, b_pad, v1, v2, acc
):
    _, depth, rows, cols = arrays.shape
    y_is_even = lax.axis_index("gy") % 2 == 0
    do = krylov_steps(counts, depth, rows, cols, m_pad, w_pad, free, b_pad, v1, v2, acc, None, False)
    for a in range(4):
        for p in range(depth):
            do.put(a, LO + p, do.own, arrays[a, p])
    for k in range(2 * depth):
        for j, x in enumerate(unpacked(y_even[k], y_odd[k], y_is_even)):
            a, p = divmod(2 * k + j, depth)
            do.put(a, LO + p, do.ring, x)
    do.cut_edges(range(LO, LO + depth))
    do.prepare((LO + 1, depth - 2))
    do.first((LO + 2, depth - 4))
    do.second((LO + 3, depth - 6))
    for n in range(66):
        acc[n] = jnp.zeros((8, 128), jnp.float32)
    lax.fori_loop(LO + 2, LO + depth - 2, do.accumulate, 0)
    lax.fori_loop(LO + 3, LO + depth - 4, do.accumulate_last, 0)


def padded_shapes(depth, rows, cols):
    planes, wide = depth + LO + HI, rows + 8
    sizes = [(2,), (3,), (), (LABELS,), (LABELS,), (LABELS,)]
    return [(*size, planes, wide, cols) for size in sizes] + [(66, 8, 128)]


def inner(counts, arrays, y_even, y_odd):
    _, depth, rows, cols = arrays.shape
    f32 = jnp.float32
    return pl.pallas_call(
        functools.partial(inner_kernel, counts),
        out_shape=[jax.ShapeDtypeStruct(x, f32) for x in padded_shapes(depth, rows, cols)],
        in_specs=[pl.BlockSpec(memory_space=VMEM)] * 3,
        out_specs=[pl.BlockSpec(memory_space=VMEM)] * 7,
        cost_estimate=pl.CostEstimate(flops=10**7, bytes_accessed=10**6, transcendentals=0),
        compiler_params=pltpu.CompilerParams(vmem_limit_bytes=20 * 2**20),
    )(arrays, y_even, y_odd)


def outer_kernel(
    counts, before, after, d_before, d_after, relay,
    m_in, w_in, free_in, b_in, v1_in, v2_in, acc_in,
    fields, moments,
    m_pad, w_pad, free, b_pad, v1, v2, acc, sums,
):
    depth, rows, cols = fields.shape[2:]
    f32 = jnp.float32
    y_is_even = lax.axis_index("gy") % 2 == 0
    do = krylov_steps(counts, depth, rows, cols, m_pad, w_pad, free, b_pad, v1, v2, acc, fields, True)
    for n, (a, i) in enumerate(Z_PLANES):
        do.put(a, LO + depth + i, do.own, after[n])
        if LO - Z_WIDTHS[a] + i >= 0:
            do.put(a, LO - Z_WIDTHS[a] + i, do.own, before[n])
    for n, (a, i) in enumerate(CORNERS):
        even = relay[n]
        even_after = pltpu.roll(even, 4, 0)
        do.put(a, LO - CORNER_WIDTHS[a] + i, do.ring, unpacked(even, d_before[n], y_is_even)[0])
        do.put(a, LO + depth + i, do.ring, unpacked(even_after, d_after[n], y_is_even)[0])
    zero_tile = jnp.zeros((8, cols), f32)
    do.put(0, LO + depth + 3, do.ring, zero_tile)
    do.put(3, LO + depth + 2, do.ring, zero_tile)
    do.put(3, 0, do.ring, zero_tile)
    low, high = LO, LO + depth
    for source, target, planes in (
        (m_in, m_pad, (low, low + 1, high - 2, high - 1)),
        (w_in, w_pad, range(low, high)),
        (b_in, b_pad, (low + 1, low + 2, high - 3, high - 2)),
        (v1_in, v1, (low + 2, low + 3, high - 4, high - 3)),
        (v2_in, v2, (low + 3, high - 4)),
    ):
        for p in planes:
            for c in range(source.shape[0]):
                target[c, p] = source[c, p]
    for p in (low + 1, low + 2, high - 3, high - 2):
        free[p] = free_in[p]
    for n in range(66):
        acc[n] = acc_in[n]
    do.cut_edges([p for p in range(high + 3) if p not in range(low, high)])

    do.prepare((1, low), (high - 1, 4))
    do.first((2, low), (high - 2, 4))
    do.second((3, low), (high - 3, 4))
    lax.fori_loop(0, 4, lambda i, x: do.accumulate(low + i + (i // 2) * (depth - 4), x), 0)
    lax.fori_loop(
        0, depth - 1, lambda i, x: do.accumulate_last(low + i + jnp.where(i >= 3, 1, 0), x), 0
    )

    half_pairs, all_pairs = do.half_pairs, do.all_pairs
    low, high = [acc[n] for n in range(30)], [acc[30 + n] for n in range(36)]
    kept = {}
    for k in range(5):
        part = low[10 * k : 10 * k + 10] if k < 3 else high[10 * (k - 3) : 10 * (k - 3) + 10]
        for (a, b), x in zip(half_pairs, part):
            kept[k, a, b] = kept[k, b, a] = x
    last = dict(zip(all_pairs, high[20:]))
    for a, b in half_pairs:
        kept[5, a, b] = kept[5, b, a] = 0.5 * (last[a, b] + last[b, a])
    for k in range(6):
        for a, b in half_pairs:
            x = jnp.sum(kept[k, a, b], axis=0, keepdims=True)
            for i, j in {(a, b), (b, a)}:
                at = (2 * k + j // 2) * 8 + (j % 2) * 4 + i
                sums[at : at + 1, :] = x
    lane = lax.broadcasted_iota(jnp.int32, (8, 128), 1)
    packed = jnp.zeros((8, 128), f32)
    for g in range(12):
        x = jnp.sum(sums[8 * g : 8 * g + 8, :], axis=1, keepdims=True)
        packed = jnp.where(lane == g, x, packed)
    moments[...] = packed


def outer(counts, shape, halos, insides):
    _, depth, rows, cols = shape
    f32 = jnp.float32
    return pl.pallas_call(
        functools.partial(outer_kernel, counts),
        out_shape=[
            jax.ShapeDtypeStruct((3, LABELS, depth, rows, cols), f32),
            jax.ShapeDtypeStruct((8, 128), f32),
        ],
        in_specs=[pl.BlockSpec(memory_space=VMEM)] * 12,
        out_specs=[pl.BlockSpec(memory_space=VMEM)] * 2,
        scratch_shapes=[VMEM(x, f32) for x in padded_shapes(depth, rows, cols)]
        + [VMEM((96, 128), f32)],
        compiler_params=pltpu.CompilerParams(vmem_limit_bytes=28 * 2**20),
    )(*halos, *insides)


def solved(moment, sides, floor):
    n = 3 * LABELS
    system = {
        (i, j): moment(i // LABELS + j // LABELS + 1, i % LABELS, j % LABELS)
        for i in range(n) for j in range(i + 1)
    }
    right = dict(enumerate(sides))
    first = {k: system[k, k] for k in range(n)}
    lower, inverse = {}, {}
    for k in range(n):
        pivot = system[k, k]
        sound = pivot > floor * first[k]
        inverse[k] = jnp.where(sound, 1.0 / jnp.where(sound, pivot, 1.0), 0.0)
        for i in range(k + 1, n):
            lower[i, k] = system[i, k] * inverse[k]
        for i in range(k + 1, n):
            for j in range(k + 1, i + 1):
                system[i, j] = system[i, j] - lower[i, k] * system[j, k]
            right[i] = right[i] - lower[i, k] * right[k]
    for k in reversed(range(n)):
        x = right[k] * inverse[k]
        for i in range(k + 1, n):
            x = x - lower[i, k] * right[i]
        right[k] = x
    return [right[k] for k in range(n)]


def combine_kernel(
    mine, theirs, fields, b_in, v1_in, v2_in, natural, out, spread, coeffs, mixed, buffer, sems
):
    f32 = jnp.float32
    _, depth, rows, cols = natural.shape
    sums = mine[...] + theirs[...]
    columns = [jnp.broadcast_to(sums[:, g : g + 1], (8, 128)) for g in range(12)]
    for g in range(12):
        spread[g] = columns[g]

    def moment(k, a, b):
        a, b = min(a, b), max(a, b)
        at = (b % 2) * 4 + a
        return jnp.broadcast_to(spread[2 * k + b // 2, at : at + 1, :], (8, 128))

    sides = []
    for k in range(3):
        for a in range(LABELS):
            x = columns[2 * k + a // 2]
            sides.append(pltpu.roll(x, 4, 0) if a % 2 else x)
    for k, x in enumerate(solved(moment, sides, PIVOT_FLOOR)):
        coeffs[k] = x

    back = interleave(cols, back=True)
    chunk = depth // CHUNKS

    def field(k, p, cut):
        n, c = divmod(k, LABELS)
        inside = range(2, depth - 2) if n < 2 else range(3, depth - 4)
        if p in inside:
            return (b_in, v1_in, v2_in)[n][(c, LO + p) + cut]
        return fields[(n, c, p) + cut]

    def combine(n):
        for first in range(0, LABELS, 2):
            weights = {
                (k, c): jnp.broadcast_to(coeffs[k, c : c + 1, :], (8, 128))
                for k in range(3 * LABELS) for c in (first, first + 1)
            }
            for p in range(n * chunk, n * chunk + chunk):
                for r in range(0, rows, 8):
                    for l in range(0, cols, 128):
                        cut = (slice(r, r + 8), slice(l, l + 128))
                        v = [field(k, p, cut) for k in range(3 * LABELS)]
                        for c in (first, first + 1):
                            s = [v[k] * weights[k, c] for k in range(3 * LABELS)]
                            while len(s) > 1:
                                s = [x + y for x, y in zip(s[::2], s[1::2])] + (
                                    [s[-1]] if len(s) % 2 else []
                                )
                            mixed[(c, p) + cut] = s[0]

    def turn_back(n):
        planes = slice(n * chunk, n * chunk + chunk)
        x = mixed[:, planes].reshape(LABELS * chunk * rows, cols)
        high = x.astype(jnp.bfloat16)
        low = (x - high.astype(f32)).astype(jnp.bfloat16)
        x = jnp.dot(high, back, preferred_element_type=f32)
        x = x + jnp.dot(low, back, preferred_element_type=f32)
        x = x.reshape(LABELS, chunk, rows, cols)
        for c in range(LABELS):
            buffer[c, planes] = jnp.where(natural[0, planes] == c, 1.0, x[c])

    copies = [
        pltpu.make_async_copy(
            buffer.at[:, n * chunk : (n + 1) * chunk], out.at[:, n * chunk : (n + 1) * chunk],
            sems.at[n],
        )
        for n in range(CHUNKS)
    ]
    combine(0)
    for n in range(CHUNKS):
        if n + 1 < CHUNKS:
            combine(n + 1)
        turn_back(n)
        copies[n].start()
    for copy in copies:
        copy.wait()


def combined(mine, theirs, fields, insides, natural):
    _, depth, rows, cols = natural.shape
    f32 = jnp.float32
    return pl.pallas_call(
        combine_kernel,
        out_shape=jax.ShapeDtypeStruct((LABELS, depth, rows, cols), f32),
        in_specs=[pl.BlockSpec(memory_space=VMEM)] * 7,
        out_specs=pl.BlockSpec(memory_space=pltpu.HBM),
        scratch_shapes=[
            VMEM((12, 8, 128), f32),
            VMEM((3 * LABELS, 8, 128), f32),
            VMEM((LABELS, depth, rows, cols), f32),
            VMEM((LABELS, depth, rows, cols), f32),
            pltpu.SemaphoreType.DMA((CHUNKS,)),
        ],
        compiler_params=pltpu.CompilerParams(vmem_limit_bytes=32 * 2**20),
    )(mine, theirs, fields, *insides, natural)


def per_device(counts, tags, depth_affinity, row_affinity, column_affinity):
    parts, nz, ny = counts
    natural = jnp.stack([tags, depth_affinity, row_affinity, column_affinity])
    axes = ("parts", "gz", "gy")
    ze, zo = (lambda z: even_partner(z, nz)), (lambda z: odd_partner(z, nz))
    ye, yo = (lambda y: even_partner(y, ny)), (lambda y: odd_partner(y, ny))

    def swap(array, pz, py):
        def pair(z, y):
            if pz and pz(z) == z:
                return z, ye(y)
            if py and py(y) == y:
                return z, y
            return pz(z) if pz else z, py(y) if py else y
        return exchanged(array, axes, counts, pair)

    arrays, z_even, z_odd, y_even, y_odd, d_even, d_odd = pack(natural)
    y_odd = swap(y_odd, None, yo)
    insides = inner(counts, arrays, swap(y_even, None, ye), y_odd)
    before, after, relay = relayed(swap(z_even, ze, None), swap(z_odd, zo, None), y_odd)
    corners = cornered(swap(d_even, ze, yo), swap(d_odd, zo, yo))
    halos = [before, after, *corners, swap(relay, None, ye)]
    fields, moments = outer(counts, arrays.shape, halos, insides)

    steps = [lambda z, y: (z, y ^ 1)]
    steps += [lambda z, y, d=d: (z, y ^ d ^ 1) for d in powers(ny)[1:]]
    steps += [lambda z, y, d=d: (z ^ d, y ^ 1) for d in powers(nz)]
    for n, pair in enumerate(steps):
        theirs = exchanged(moments, axes, counts, pair)
        if n < len(steps) - 1:
            moments = moments + theirs
    return combined(moments, theirs, fields, insides[3:6], natural)


def powers(count):
    return [1 << n for n in range(count.bit_length() - 1)]


def solution(mesh):
    counts = tuple(mesh.shape[axis] for axis in ("parts", "gz", "gy"))
    placed = P(("parts", "gz"), "gy", None)
    return jax.shard_map(
        functools.partial(per_device, counts),
        mesh=mesh,
        in_specs=(placed,) * 4,
        out_specs=P(None, ("parts", "gz"), "gy", None),
        check_vma=False,
    )
```

```python
import functools
import types

import jax
import jax.numpy as jnp
from jax import lax
from jax.experimental import pallas as pl
from jax.experimental.pallas import tpu as pltpu
from jax.sharding import PartitionSpec as P

LABELS = 4
PIVOT_FLOOR = 1e-7
LO, HI = 3, 4
Z_WIDTHS = (4, 3, 3, 3)
Z_PLANES = [(a, i) for a, width in enumerate(Z_WIDTHS) for i in range(width)]
CORNER_WIDTHS = (3, 3, 3, 2)
CORNERS = [(a, i) for a, width in enumerate(CORNER_WIDTHS) for i in range(width)]
SLOTS = [
    (0, 0, 0, 1), (0, 4, 1, 1), (1, 0, 2, 1), (1, 4, 0, 2), (1, 6, 1, 2), (2, 0, 2, 2),
    (2, 2, 3, 1), (2, 4, 0, 3), (2, 5, 1, 3), (2, 6, 2, 3), (2, 7, 3, 2),
]
PAIR = 4096.0
CHUNKS = 8
VMEM = pltpu.VMEM


def even_partner(i, count):
    return i ^ 1 if (i ^ 1) < count else i


def odd_partner(i, count):
    j = ((i + 1) ^ 1) - 1
    return j if 0 <= j < count else i


def exchanged(array, axes, counts, pair):
    parts, nz, ny = counts
    route = []
    for p in range(parts):
        for z in range(nz):
            for y in range(ny):
                q = (p,) + pair(z, y)
                if q == (p, z, y):
                    q = (even_partner(p, parts), z, y)
                source, target = ((a * nz + b) * ny + c for a, b, c in ((p, z, y), q))
                if source != target:
                    route.append((source, target))
    return lax.ppermute(array, axes, route)


def tile_pairs(sources, up, out):
    rows, cols = sources[0][0].shape[-2:]
    row = lax.broadcasted_iota(jnp.int32, (8, cols), 0)
    tile = pl.multiple_of(up * (rows - 8), 8)
    first = (row >= 4) == (up == 1)
    for k in range(0, len(sources), 2):
        (ra, *pa), (rb, *pb) = sources[k], sources[min(k + 1, len(sources) - 1)]
        a = ra[(*pa, pl.ds(tile, 8), slice(None))]
        b = rb[(*pb, pl.ds(tile, 8), slice(None))]
        out[k // 2] = jnp.where(first, a, pltpu.roll(b, 4, 0))


def interleave(cols, back=False):
    tiles = cols // 128
    i, j = (lax.broadcasted_iota(jnp.int32, (cols, cols), n) for n in ((1, 0) if back else (0, 1)))
    return (i == tiles * (j % 128) + j // 128).astype(jnp.float32).astype(jnp.bfloat16)


def moved(tile, rows, up):
    rows %= 8
    if rows == 0:
        return tile
    return jnp.where(up == 1, pltpu.roll(tile, 8 - rows, 0), pltpu.roll(tile, rows, 0))


def pack_corner(arrays, z_up, y_up, out):
    _, depth, rows, cols = arrays.shape
    row = lax.broadcasted_iota(jnp.int32, (8, cols), 0)
    away = jnp.where(y_up == 1, 7 - row, row)
    tile = pl.multiple_of(y_up * (rows - 8), 8)
    packed = {}
    for t, first, a, k in SLOTS:
        x = arrays[a, z_up * (depth - 2 * k + 1) + k - 1, pl.ds(tile, 8), :]
        x = moved(x, first, y_up)
        packed[t] = jnp.where(away >= first, x, packed[t]) if first else x
    for t, x in packed.items():
        out[t] = x


def pack_kernel(natural, arrays, z_even, z_odd):
    cols = natural.shape[-1]
    flat = natural[...].reshape(-1, cols).astype(jnp.float32).astype(jnp.bfloat16)
    turned = jnp.dot(flat, interleave(cols), preferred_element_type=jnp.float32)
    turned = turned.reshape(arrays.shape)
    arrays[0] = turned[0]
    arrays[1:] = turned[1:] + 1.0
    z_is_odd = lax.axis_index("gz") % 2
    depth = arrays.shape[1]
    z_ups = (1 - z_is_odd, z_is_odd)
    for up, out in zip(z_ups, (z_even, z_odd)):
        for n, (a, i) in enumerate(Z_PLANES):
            out[n] = arrays[a, up * (depth - Z_WIDTHS[a]) + i]


def pack_rest_kernel(arrays, y_even, y_odd, d_even, d_odd):
    z_is_odd, y_is_odd = lax.axis_index("gz") % 2, lax.axis_index("gy") % 2
    depth = arrays.shape[1]
    z_ups, y_ups = (1 - z_is_odd, z_is_odd), (1 - y_is_odd, y_is_odd)
    planes = [(arrays, a, p) for a in range(4) for p in range(depth)]
    for up, out in zip(y_ups, (y_even, y_odd)):
        tile_pairs(planes, up, out)
    for up, out in zip(z_ups, (d_even, d_odd)):
        pack_corner(arrays, up, y_ups[1], out)


def packed(kernel, shapes, arrays):
    return pl.pallas_call(
        kernel,
        out_shape=[jax.ShapeDtypeStruct(shape, jnp.float32) for shape in shapes],
        in_specs=[pl.BlockSpec(memory_space=VMEM)],
        out_specs=[pl.BlockSpec(memory_space=VMEM)] * len(shapes),
        compiler_params=pltpu.CompilerParams(vmem_limit_bytes=16 * 2**20),
    )(arrays)


def pack(natural):
    _, depth, rows, cols = natural.shape
    arrays, *z = packed(
        pack_kernel, [natural.shape] + [(len(Z_PLANES), rows, cols)] * 2, natural
    )
    shapes = [(2 * depth, 8, cols)] * 2 + [(3, 8, cols)] * 2
    return arrays, *z, *packed(pack_rest_kernel, shapes, arrays)


def relay_kernel(z_even, z_odd, y_odd, before, after, relay):
    z_is_even = lax.axis_index("gz") % 2 == 0
    y_is_odd = lax.axis_index("gy") % 2
    for n in range(len(Z_PLANES)):
        e, o = z_even[n], z_odd[n]
        before[n] = jnp.where(z_is_even, o, e)
        after[n] = jnp.where(z_is_even, e, o)
    sources = []
    for a, i in CORNERS:
        n = Z_PLANES.index((a, 0))
        sources += [(before, n + Z_WIDTHS[a] - CORNER_WIDTHS[a] + i), (after, n + i)]
    tile_pairs(sources, 1 - y_is_odd, relay)


def corner_kernel(d_even, d_odd, d_before, d_after):
    z_is_even = lax.axis_index("gz") % 2 == 0
    y_is_odd = lax.axis_index("gy") % 2
    for out, x, y in ((d_before, d_odd, d_even), (d_after, d_even, d_odd)):
        tiles = [jnp.where(z_is_even, x[t], y[t]) for t in range(3)]
        for t, first, a, k in SLOTS:
            i = CORNER_WIDTHS[a] - k if out is d_before else k - 1
            out[CORNERS.index((a, i))] = moved(tiles[t], -first, 1 - y_is_odd)


def cornered(d_even, d_odd):
    cols = d_even.shape[2]
    return pl.pallas_call(
        corner_kernel,
        out_shape=[jax.ShapeDtypeStruct((len(CORNERS), 8, cols), jnp.float32)] * 2,
        in_specs=[pl.BlockSpec(memory_space=VMEM)] * 2,
        out_specs=[pl.BlockSpec(memory_space=VMEM)] * 2,
        cost_estimate=pl.CostEstimate(flops=2 * 10**9, bytes_accessed=10**6, transcendentals=0),
        compiler_params=pltpu.CompilerParams(vmem_limit_bytes=16 * 2**20),
    )(d_even, d_odd)


def relayed(z_even, z_odd, y_odd):
    cols = z_even.shape[2]
    shapes = [z_even.shape] * 2 + [(len(CORNERS), 8, cols)]
    return pl.pallas_call(
        relay_kernel,
        out_shape=[jax.ShapeDtypeStruct(shape, jnp.float32) for shape in shapes],
        in_specs=[pl.BlockSpec(memory_space=VMEM)] * 3,
        out_specs=[pl.BlockSpec(memory_space=VMEM)] * 3,
        compiler_params=pltpu.CompilerParams(vmem_limit_bytes=16 * 2**20),
    )(z_even, z_odd, y_odd)


def krylov_steps(
    counts, depth, rows, cols, m_pad, w_pad, free, b_pad, v1, v2, acc, fields, loops, given=None
):
    def at(p, ref, n, margin):
        inside = LO + margin <= p < LO + depth - margin
        return given[n] if given is not None and inside else ref

    def m_at(p):
        return at(p, m_pad, 0, 0)

    def w_at(p):
        return at(p, w_pad, 1, 0)

    def free_at(p):
        return at(p, free, 2, 1)

    _, nz, ny = counts
    zi, yi = lax.axis_index("gz"), lax.axis_index("gy")
    wide = rows + 8
    f32 = jnp.float32
    ring_row = lax.broadcasted_iota(jnp.int32, (8, cols), 0)
    own = slice(0, rows)
    ring = slice(rows, wide)

    def put(a, plane, where, values):
        if a == 0:
            m_pad[0, plane, where, :] = jnp.where(
                values == 0, 1.0, jnp.where(values == 1, PAIR, 0.0)
            )
            m_pad[1, plane, where, :] = jnp.where(
                values == 2, 1.0, jnp.where(values == 3, PAIR, 0.0)
            )
        else:
            w_pad[a - 1, plane, where, :] = values

    def cut_edges(planes):
        for p, at_rim in ((LO + depth - 1, zi == nz - 1), (LO - 1, zi == 0)):
            if p in planes:
                w_pad[0, p] = jnp.where(at_rim, 0.0, w_pad[0, p])
        x_end = slice(cols - 128, cols)
        last_x = lax.broadcasted_iota(jnp.int32, (wide, 128), 1) == 127
        at_end = (yi == ny - 1) & (ring_row == 7)
        at_start = (yi == 0) & (ring_row == 7)
        for p in planes:
            here = slice(rows - 8, rows)
            w_pad[1, p, here, :] = jnp.where(at_end, 0.0, w_pad[1, p, here, :])
            w_pad[1, p, ring, :] = jnp.where(at_start, 0.0, w_pad[1, p, ring, :])
            w_pad[2, p, :, x_end] = jnp.where(last_x, 0.0, w_pad[2, p, :, x_end])

    lanes = [slice(l, l + 128) for l in range(0, cols, 128)]
    lane = lax.broadcasted_iota(jnp.int32, (8, 128), 1)
    row = lax.broadcasted_iota(jnp.int32, (8, 128), 0)

    row_tiles = range(0, wide, 8)

    def tile(ref, index, r):
        return [ref[(*index, slice(r, r + 8), l)] for l in lanes]

    def plane(ref, *index):
        return [tile(ref, index, r) for r in row_tiles]

    def store(ref, index, r, values):
        for l, x in zip(lanes, values):
            ref[(*index, slice(r, r + 8), l)] = x

    def store_plane(ref, index, values):
        for r, x in zip(row_tiles, values):
            store(ref, index, r, x)

    def each(f, *planes):
        return [[f(*x) for x in zip(*rows_)] for rows_ in zip(*planes)]

    def next_x(v):
        return [x[1:] + [pltpu.roll(x[0], 127, 1)] for x in v]

    def prev_x(v):
        return [[pltpu.roll(x[-1], 1, 1)] + x[:-1] for x in v]

    def next_y(v):
        pair = lambda a, b: pltpu.roll(jnp.where(row == 0, b, a), 7, 0)
        return each(pair, v, v[1:] + v[:1])

    def prev_y(v):
        pair = lambda a, b: pltpu.roll(jnp.where(row == 7, b, a), 1, 0)
        return each(pair, v, v[-1:] + v[:-1])

    def times(x, y):
        return each(lambda a, b: a * b, x, y)

    def repeated(count, body):
        if loops:
            lax.fori_loop(0, count, body, 0)
        else:
            for n in range(count):
                body(n, 0)

    def prepare(*ranges):
        def body(h, _):
            for start, count in ranges:
                here = plane(m_at(start), h, start)
                from_behind = times(
                    plane(w_at(start - 1), 0, start - 1), plane(m_at(start - 1), h, start - 1)
                )
                for p in range(start, start + count):
                    ahead = plane(m_at(p + 1), h, p + 1)
                    w_z, w_y, w_x = (plane(w_at(p), i, p) for i in range(3))
                    sums_ = each(
                        lambda a, b, c, d, e, f: (a + b) + (c + d) + (e + f),
                        times(w_z, ahead), from_behind,
                        times(w_y, next_y(here)), prev_y(times(w_y, here)),
                        times(w_x, next_x(here)), prev_x(times(w_x, here)),
                    )
                    other = plane(m_at(p), 1 - h, p)
                    u = each(lambda a, b: jnp.where(a + b == 0.0, 1.0, 0.0), here, other)
                    store_plane(free, (p,), u)
                    sums_ = times(sums_, u)
                    second = each(lambda x: jnp.floor(x * (1.0 / PAIR)), sums_)
                    store_plane(b_pad, (2 * h, p), each(lambda x, y: x - PAIR * y, sums_, second))
                    store_plane(b_pad, (2 * h + 1, p), second)
                    from_behind = times(w_z, here)
                    here = ahead
            return 0

        repeated(2, body)

    def flow(w, x, y):
        return each(lambda a, b, c: a * (b - c), w, x, y)

    def apply(source, n, margin, target, *ranges):
        def v_at(p):
            return at(p, source, n, margin)

        def body(c, _):
            for start, count in ranges:
                here = plane(v_at(start), c, start)
                behind = plane(v_at(start - 1), c, start - 1)
                from_behind = flow(plane(w_at(start - 1), 0, start - 1), here, behind)
                for p in range(start, start + count):
                    ahead = plane(v_at(p + 1), c, p + 1)
                    f_z = flow(plane(w_at(p), 0, p), ahead, here)
                    f_y = flow(plane(w_at(p), 1, p), next_y(here), here)
                    f_x = flow(plane(w_at(p), 2, p), next_x(here), here)
                    store_plane(target, (c, p), each(
                        lambda u, a, b, c, d, e, f: u * ((a - b) + (c - d) + (e - f)),
                        plane(free_at(p), p), from_behind, f_z, prev_y(f_y), f_y, prev_x(f_x), f_x,
                    ))
                    from_behind, here = f_z, ahead
            return 0

        repeated(LABELS, body)

    half_pairs = [(a, b) for a in range(LABELS) for b in range(a, LABELS)]
    all_pairs = [(a, b) for a in range(LABELS) for b in range(LABELS)]

    def total(products):
        while len(products) > 1:
            products = [x + y for x, y in zip(products[::2], products[1::2])] + (
                [products[-1]] if len(products) % 2 else []
            )
        return products[0]

    def add_up(first, parts):
        for n, part in enumerate(parts):
            acc[first + n] = acc[first + n] + total(part)

    own_tiles = range(0, rows, 8)

    def accumulate(p, _):
        parts = [[] for _ in range(30)]
        for r in own_tiles:
            bs = [tile(b_pad, (c, p), r) for c in range(LABELS)]
            abs_ = [tile(v1, (c, p), r) for c in range(LABELS)]
            for l in range(len(lanes)):
                b, ab = [x[l] for x in bs], [x[l] for x in abs_]
                products = [b[i] * b[j] for i, j in half_pairs]
                products += [b[i] * ab[j] for i, j in half_pairs]
                products += [ab[i] * ab[j] for i, j in half_pairs]
                for part, product in zip(parts, products):
                    part.append(product)
            for c in range(LABELS):
                if fields is not None:
                    store(fields, (0, c, p - LO), r, bs[c])
                    store(fields, (1, c, p - LO), r, abs_[c])
        add_up(0, parts)
        return 0

    def accumulate_last(p, _):
        parts = [[] for _ in range(36)]
        own_w = w_pad if given is None else given[1]
        w_z, w_y, w_x = (plane(own_w, i, p) for i in range(3))
        w_zb = plane(own_w, 0, jnp.maximum(p - 1, LO))
        if given is not None:
            w_zb = each(lambda a, b: jnp.where(p == LO, a, b), plane(w_pad, 0, LO - 1), w_zb)
        degree = each(
            lambda a, b, c, d, e, f: (a + b) + (c + d) + (e + f),
            w_z, w_zb, w_y, prev_y(w_y), w_x, prev_x(w_x),
        )
        qs, aabs_ = [], []
        for c in range(LABELS):
            v = plane(v2, c, p)
            qs.append(each(
                lambda d, x, a, b, e: d * x - 2.0 * (a + b + e),
                degree, v, times(w_z, plane(v2, c, p + 1)), times(w_y, next_y(v)),
                times(w_x, next_x(v)),
            ))
            aabs_.append(v)
        for t, r in enumerate(own_tiles):
            abs_ = [tile(v1, (c, p), r) for c in range(LABELS)]
            for l in range(len(lanes)):
                ab, aab, q = [x[l] for x in abs_], [x[t][l] for x in aabs_], [x[t][l] for x in qs]
                products = [ab[i] * aab[j] for i, j in half_pairs]
                products += [aab[i] * aab[j] for i, j in half_pairs]
                products += [aab[i] * q[j] for i, j in all_pairs]
                for part, product in zip(parts, products):
                    part.append(product)
            for c in range(LABELS):
                if fields is not None:
                    store(fields, (2, c, p - LO), r, aabs_[c][t])
        add_up(30, parts)
        return 0

    return types.SimpleNamespace(
        put=put, cut_edges=cut_edges, prepare=prepare,
        first=functools.partial(apply, b_pad, 3, 1, v1),
        second=functools.partial(apply, v1, 4, 2, v2), accumulate=accumulate, accumulate_last=accumulate_last,
        half_pairs=half_pairs, all_pairs=all_pairs, own=own, ring=ring,
    )


def unpacked(even, odd, y_is_even):
    half = lax.broadcasted_iota(jnp.int32, even.shape, 0) < 4
    from_even = half == y_is_even
    return jnp.where(from_even, even, odd), pltpu.roll(jnp.where(from_even, odd, even), 4, 0)


def inner_kernel(
    counts, arrays, y_even, y_odd, m_pad, w_pad, free, b_pad, v1, v2, acc
):
    _, depth, rows, cols = arrays.shape
    y_is_even = lax.axis_index("gy") % 2 == 0
    do = krylov_steps(counts, depth, rows, cols, m_pad, w_pad, free, b_pad, v1, v2, acc, None, False)
    for a in range(4):
        for p in range(depth):
            do.put(a, LO + p, do.own, arrays[a, p])
    for k in range(2 * depth):
        for j, x in enumerate(unpacked(y_even[k], y_odd[k], y_is_even)):
            a, p = divmod(2 * k + j, depth)
            do.put(a, LO + p, do.ring, x)
    do.cut_edges(range(LO, LO + depth))
    do.prepare((LO + 1, depth - 2))
    do.first((LO + 2, depth - 4))
    do.second((LO + 3, depth - 6))
    for n in range(66):
        acc[n] = jnp.zeros((8, 128), jnp.float32)
    lax.fori_loop(LO + 2, LO + depth - 2, do.accumulate, 0)
    lax.fori_loop(LO + 3, LO + depth - 4, do.accumulate_last, 0)


def padded_shapes(depth, rows, cols):
    planes, wide = depth + LO + HI, rows + 8
    sizes = [(2,), (3,), (), (LABELS,), (LABELS,), (LABELS,)]
    return [(*size, planes, wide, cols) for size in sizes] + [(66, 8, 128)]


def inner(counts, arrays, y_even, y_odd):
    _, depth, rows, cols = arrays.shape
    f32 = jnp.float32
    return pl.pallas_call(
        functools.partial(inner_kernel, counts),
        out_shape=[jax.ShapeDtypeStruct(x, f32) for x in padded_shapes(depth, rows, cols)],
        in_specs=[pl.BlockSpec(memory_space=VMEM)] * 3,
        out_specs=[pl.BlockSpec(memory_space=VMEM)] * 7,
        cost_estimate=pl.CostEstimate(flops=10**7, bytes_accessed=10**6, transcendentals=0),
        compiler_params=pltpu.CompilerParams(vmem_limit_bytes=20 * 2**20),
    )(arrays, y_even, y_odd)


def outer_kernel(
    counts, before, after, d_before, d_after, relay,
    m_in, w_in, free_in, b_in, v1_in, v2_in, acc_in,
    fields, moments,
    m_pad, w_pad, free, b_pad, v1, v2, acc, sums,
):
    depth, rows, cols = fields.shape[2:]
    f32 = jnp.float32
    y_is_even = lax.axis_index("gy") % 2 == 0
    given = (m_in, w_in, free_in, b_in, v1_in)
    do = krylov_steps(
        counts, depth, rows, cols, m_pad, w_pad, free, b_pad, v1, v2, acc, fields, True, given
    )
    for n, (a, i) in enumerate(Z_PLANES):
        do.put(a, LO + depth + i, do.own, after[n])
        if LO - Z_WIDTHS[a] + i >= 0:
            do.put(a, LO - Z_WIDTHS[a] + i, do.own, before[n])
    for n, (a, i) in enumerate(CORNERS):
        even = relay[n]
        even_after = pltpu.roll(even, 4, 0)
        do.put(a, LO - CORNER_WIDTHS[a] + i, do.ring, unpacked(even, d_before[n], y_is_even)[0])
        do.put(a, LO + depth + i, do.ring, unpacked(even_after, d_after[n], y_is_even)[0])
    zero_tile = jnp.zeros((8, cols), f32)
    do.put(0, LO + depth + 3, do.ring, zero_tile)
    do.put(3, LO + depth + 2, do.ring, zero_tile)
    do.put(3, 0, do.ring, zero_tile)
    low, high = LO, LO + depth
    for source, target, planes in (
        (b_in, b_pad, (low + 1, high - 2)),
        (v1_in, v1, (low + 2, high - 4, high - 3)),
        (v2_in, v2, (low + 3, high - 4)),
    ):
        for p in planes:
            for c in range(LABELS):
                target[c, p] = source[c, p]
    for n in range(66):
        acc[n] = acc_in[n]
    do.cut_edges([p for p in range(high + 3) if p not in range(low, high)])

    do.prepare((1, low), (high - 1, 4))
    do.first((2, low), (high - 2, 4))
    do.second((3, low), (high - 3, 4))
    lax.fori_loop(0, 4, lambda i, x: do.accumulate(low + i + (i // 2) * (depth - 4), x), 0)
    lax.fori_loop(
        0, depth - 1, lambda i, x: do.accumulate_last(low + i + jnp.where(i >= 3, 1, 0), x), 0
    )

    half_pairs, all_pairs = do.half_pairs, do.all_pairs
    low, high = [acc[n] for n in range(30)], [acc[30 + n] for n in range(36)]
    kept = {}
    for k in range(5):
        part = low[10 * k : 10 * k + 10] if k < 3 else high[10 * (k - 3) : 10 * (k - 3) + 10]
        for (a, b), x in zip(half_pairs, part):
            kept[k, a, b] = kept[k, b, a] = x
    last = dict(zip(all_pairs, high[20:]))
    for a, b in half_pairs:
        kept[5, a, b] = kept[5, b, a] = 0.5 * (last[a, b] + last[b, a])
    for k in range(6):
        for a, b in half_pairs:
            x = jnp.sum(kept[k, a, b], axis=0, keepdims=True)
            for i, j in {(a, b), (b, a)}:
                at = (2 * k + j // 2) * 8 + (j % 2) * 4 + i
                sums[at : at + 1, :] = x
    lane = lax.broadcasted_iota(jnp.int32, (8, 128), 1)
    packed = jnp.zeros((8, 128), f32)
    for g in range(12):
        x = jnp.sum(sums[8 * g : 8 * g + 8, :], axis=1, keepdims=True)
        packed = jnp.where(lane == g, x, packed)
    moments[...] = packed


def outer(counts, shape, halos, insides):
    _, depth, rows, cols = shape
    f32 = jnp.float32
    return pl.pallas_call(
        functools.partial(outer_kernel, counts),
        out_shape=[
            jax.ShapeDtypeStruct((3, LABELS, depth, rows, cols), f32),
            jax.ShapeDtypeStruct((8, 128), f32),
        ],
        in_specs=[pl.BlockSpec(memory_space=VMEM)] * 12,
        out_specs=[pl.BlockSpec(memory_space=VMEM)] * 2,
        scratch_shapes=[VMEM(x, f32) for x in padded_shapes(depth, rows, cols)]
        + [VMEM((96, 128), f32)],
        compiler_params=pltpu.CompilerParams(vmem_limit_bytes=28 * 2**20),
    )(*halos, *insides)


def solved(moment, sides, floor):
    n = 3 * LABELS
    system = {
        (i, j): moment(i // LABELS + j // LABELS + 1, i % LABELS, j % LABELS)
        for i in range(n) for j in range(i + 1)
    }
    right = dict(enumerate(sides))
    first = {k: system[k, k] for k in range(n)}
    lower, inverse = {}, {}
    for k in range(n):
        pivot = system[k, k]
        sound = pivot > floor * first[k]
        inverse[k] = jnp.where(sound, 1.0 / pivot, 0.0)
        for i in range(k + 1, n):
            lower[i, k] = system[i, k] * inverse[k]
        for i in range(k + 1, n):
            for j in range(k + 1, i + 1):
                system[i, j] = system[i, j] - lower[i, k] * system[j, k]
            right[i] = right[i] - lower[i, k] * right[k]
    for k in reversed(range(n)):
        x = right[k] * inverse[k]
        for i in range(k + 1, n):
            x = x - lower[i, k] * right[i]
        right[k] = x
    return [right[k] for k in range(n)]


def combine_kernel(
    mine, theirs, fields, b_in, v1_in, v2_in, natural, out, spread, coeffs, mixed, buffer, sems
):
    f32 = jnp.float32
    _, depth, rows, cols = natural.shape
    sums = mine[...] + theirs[...]
    columns = [jnp.broadcast_to(sums[:, g : g + 1], (8, 128)) for g in range(12)]
    for g in range(12):
        spread[g] = columns[g]

    def moment(k, a, b):
        a, b = min(a, b), max(a, b)
        at = (b % 2) * 4 + a
        return jnp.broadcast_to(spread[2 * k + b // 2, at : at + 1, :], (8, 128))

    sides = []
    for k in range(3):
        for a in range(LABELS):
            x = columns[2 * k + a // 2]
            sides.append(pltpu.roll(x, 4, 0) if a % 2 else x)
    for k, x in enumerate(solved(moment, sides, PIVOT_FLOOR)):
        coeffs[k] = x

    back = interleave(cols, back=True)
    back = jnp.concatenate([back, back], axis=0)
    chunk = depth // CHUNKS

    def field(k, p, cut):
        n, c = divmod(k, LABELS)
        inside = range(2, depth - 2) if n < 2 else range(3, depth - 4)
        if p in inside:
            return (b_in, v1_in, v2_in)[n][(c, LO + p) + cut]
        return fields[(n, c, p) + cut]

    def combine(n):
        for first in range(0, LABELS, 2):
            weights = {
                (k, c): jnp.broadcast_to(coeffs[k, c : c + 1, :], (8, 128))
                for k in range(3 * LABELS) for c in (first, first + 1)
            }
            for p in range(n * chunk, n * chunk + chunk):
                for r in range(0, rows, 8):
                    for l in range(0, cols, 128):
                        cut = (slice(r, r + 8), slice(l, l + 128))
                        v = [field(k, p, cut) for k in range(3 * LABELS)]
                        for c in (first, first + 1):
                            s = [v[k] * weights[k, c] for k in range(3 * LABELS)]
                            while len(s) > 1:
                                s = [x + y for x, y in zip(s[::2], s[1::2])] + (
                                    [s[-1]] if len(s) % 2 else []
                                )
                            mixed[(c, p) + cut] = s[0]

    def turn_back(n):
        planes = slice(n * chunk, n * chunk + chunk)
        x = mixed[:, planes].reshape(LABELS * chunk * rows, cols)
        high = x.astype(jnp.bfloat16)
        low = (x - high.astype(f32)).astype(jnp.bfloat16)
        x = jnp.dot(jnp.concatenate([high, low], axis=1), back, preferred_element_type=f32)
        x = x.reshape(LABELS, chunk, rows, cols)
        for c in range(LABELS):
            buffer[c, planes] = jnp.where(natural[0, planes] == c, 1.0, x[c])

    copies = [
        pltpu.make_async_copy(
            buffer.at[:, n * chunk : (n + 1) * chunk], out.at[:, n * chunk : (n + 1) * chunk],
            sems.at[n],
        )
        for n in range(CHUNKS)
    ]
    combine(0)
    for n in range(CHUNKS):
        if n + 1 < CHUNKS:
            combine(n + 1)
        turn_back(n)
        copies[n].start()
    for copy in copies:
        copy.wait()


def combined(mine, theirs, fields, insides, natural):
    _, depth, rows, cols = natural.shape
    f32 = jnp.float32
    return pl.pallas_call(
        combine_kernel,
        out_shape=jax.ShapeDtypeStruct((LABELS, depth, rows, cols), f32),
        in_specs=[pl.BlockSpec(memory_space=VMEM)] * 7,
        out_specs=pl.BlockSpec(memory_space=pltpu.HBM),
        scratch_shapes=[
            VMEM((12, 8, 128), f32),
            VMEM((3 * LABELS, 8, 128), f32),
            VMEM((LABELS, depth, rows, cols), f32),
            VMEM((LABELS, depth, rows, cols), f32),
            pltpu.SemaphoreType.DMA((CHUNKS,)),
        ],
        compiler_params=pltpu.CompilerParams(vmem_limit_bytes=32 * 2**20),
    )(mine, theirs, fields, *insides, natural)


def per_device(counts, tags, depth_affinity, row_affinity, column_affinity):
    parts, nz, ny = counts
    natural = jnp.stack([tags, depth_affinity, row_affinity, column_affinity])
    axes = ("parts", "gz", "gy")
    ze, zo = (lambda z: even_partner(z, nz)), (lambda z: odd_partner(z, nz))
    ye, yo = (lambda y: even_partner(y, ny)), (lambda y: odd_partner(y, ny))

    def swap(array, pz, py):
        def pair(z, y):
            if pz and pz(z) == z:
                return z, ye(y)
            if py and py(y) == y:
                return z, y
            return pz(z) if pz else z, py(y) if py else y
        return exchanged(array, axes, counts, pair)

    arrays, z_even, z_odd, y_even, y_odd, d_even, d_odd = pack(natural)
    y_odd = swap(y_odd, None, yo)
    insides = inner(counts, arrays, swap(y_even, None, ye), y_odd)
    before, after, relay = relayed(swap(z_even, ze, None), swap(z_odd, zo, None), y_odd)
    corners = cornered(swap(d_even, ze, yo), swap(d_odd, zo, yo))
    halos = [before, after, *corners, swap(relay, None, ye)]
    fields, moments = outer(counts, arrays.shape, halos, insides)

    steps = [lambda z, y: (z, y ^ 1)]
    steps += [lambda z, y, d=d: (z, y ^ d ^ 1) for d in powers(ny)[1:]]
    steps += [lambda z, y, d=d: (z ^ d, y ^ 1) for d in powers(nz)]
    for n, pair in enumerate(steps):
        theirs = exchanged(moments, axes, counts, pair)
        if n < len(steps) - 1:
            moments = moments + theirs
    return combined(moments, theirs, fields, insides[3:6], natural)


def powers(count):
    return [1 << n for n in range(count.bit_length() - 1)]


def solution(mesh):
    counts = tuple(mesh.shape[axis] for axis in ("parts", "gz", "gy"))
    placed = P(("parts", "gz"), "gy", None)
    return jax.shard_map(
        functools.partial(per_device, counts),
        mesh=mesh,
        in_specs=(placed,) * 4,
        out_specs=P(None, ("parts", "gz"), "gy", None),
        check_vma=False,
    )
```

```python
import functools
import types

import jax
import jax.numpy as jnp
from jax import lax
from jax.experimental import pallas as pl
from jax.experimental.pallas import tpu as pltpu
from jax.sharding import PartitionSpec as P

LABELS = 4
PIVOT_FLOOR = 1e-7
LO, HI = 3, 4
Z_WIDTHS = (4, 3, 3, 3)
Z_PLANES = [(a, i) for a, width in enumerate(Z_WIDTHS) for i in range(width)]
CORNER_WIDTHS = (3, 3, 3, 2)
CORNERS = [(a, i) for a, width in enumerate(CORNER_WIDTHS) for i in range(width)]
SLOTS = [
    (0, 0, 0, 1), (0, 4, 1, 1), (1, 0, 2, 1), (1, 4, 0, 2), (1, 6, 1, 2), (2, 0, 2, 2),
    (2, 2, 3, 1), (2, 4, 0, 3), (2, 5, 1, 3), (2, 6, 2, 3), (2, 7, 3, 2),
]
PAIR = 4096.0
CHUNKS = 8
VMEM = pltpu.VMEM


def even_partner(i, count):
    return i ^ 1 if (i ^ 1) < count else i


def odd_partner(i, count):
    j = ((i + 1) ^ 1) - 1
    return j if 0 <= j < count else i


def exchanged(array, axes, counts, pair):
    parts, nz, ny = counts
    route = []
    for p in range(parts):
        for z in range(nz):
            for y in range(ny):
                q = (p,) + pair(z, y)
                if q == (p, z, y):
                    q = (even_partner(p, parts), z, y)
                source, target = ((a * nz + b) * ny + c for a, b, c in ((p, z, y), q))
                if source != target:
                    route.append((source, target))
    return lax.ppermute(array, axes, route)


def tile_pairs(sources, up, out):
    rows, cols = sources[0][0].shape[-2:]
    row = lax.broadcasted_iota(jnp.int32, (8, cols), 0)
    tile = pl.multiple_of(up * (rows - 8), 8)
    first = (row >= 4) == (up == 1)
    for k in range(0, len(sources), 2):
        (ra, *pa), (rb, *pb) = sources[k], sources[min(k + 1, len(sources) - 1)]
        a = ra[(*pa, pl.ds(tile, 8), slice(None))]
        b = rb[(*pb, pl.ds(tile, 8), slice(None))]
        out[k // 2] = jnp.where(first, a, pltpu.roll(b, 4, 0))


def interleave(cols, back=False):
    tiles = cols // 128
    i, j = (lax.broadcasted_iota(jnp.int32, (cols, cols), n) for n in ((1, 0) if back else (0, 1)))
    return (i == tiles * (j % 128) + j // 128).astype(jnp.float32).astype(jnp.bfloat16)


def moved(tile, rows, up):
    rows %= 8
    if rows == 0:
        return tile
    return jnp.where(up == 1, pltpu.roll(tile, 8 - rows, 0), pltpu.roll(tile, rows, 0))


def pack_corner(arrays, z_up, y_up, out):
    _, depth, rows, cols = arrays.shape
    row = lax.broadcasted_iota(jnp.int32, (8, cols), 0)
    away = jnp.where(y_up == 1, 7 - row, row)
    tile = pl.multiple_of(y_up * (rows - 8), 8)
    packed = {}
    for t, first, a, k in SLOTS:
        x = arrays[a, z_up * (depth - 2 * k + 1) + k - 1, pl.ds(tile, 8), :]
        x = moved(x, first, y_up)
        packed[t] = jnp.where(away >= first, x, packed[t]) if first else x
    for t, x in packed.items():
        out[t] = x


def pack_kernel(natural, arrays, z_even, z_odd):
    cols = natural.shape[-1]
    flat = natural[...].reshape(-1, cols).astype(jnp.float32).astype(jnp.bfloat16)
    turned = jnp.dot(flat, interleave(cols), preferred_element_type=jnp.float32)
    turned = turned.reshape(arrays.shape)
    arrays[0] = turned[0]
    arrays[1:] = turned[1:] + 1.0
    z_is_odd = lax.axis_index("gz") % 2
    depth = arrays.shape[1]
    z_ups = (1 - z_is_odd, z_is_odd)
    for up, out in zip(z_ups, (z_even, z_odd)):
        for n, (a, i) in enumerate(Z_PLANES):
            out[n] = arrays[a, up * (depth - Z_WIDTHS[a]) + i]


def pack_rest_kernel(arrays, y_even, y_odd, d_even, d_odd):
    z_is_odd, y_is_odd = lax.axis_index("gz") % 2, lax.axis_index("gy") % 2
    depth = arrays.shape[1]
    z_ups, y_ups = (1 - z_is_odd, z_is_odd), (1 - y_is_odd, y_is_odd)
    planes = [(arrays, a, p) for a in range(4) for p in range(depth)]
    for up, out in zip(y_ups, (y_even, y_odd)):
        tile_pairs(planes, up, out)
    for up, out in zip(z_ups, (d_even, d_odd)):
        pack_corner(arrays, up, y_ups[1], out)


def packed(kernel, shapes, arrays):
    return pl.pallas_call(
        kernel,
        out_shape=[jax.ShapeDtypeStruct(shape, jnp.float32) for shape in shapes],
        in_specs=[pl.BlockSpec(memory_space=VMEM)],
        out_specs=[pl.BlockSpec(memory_space=VMEM)] * len(shapes),
        compiler_params=pltpu.CompilerParams(vmem_limit_bytes=16 * 2**20),
    )(arrays)


def pack(natural):
    _, depth, rows, cols = natural.shape
    arrays, *z = packed(
        pack_kernel, [natural.shape] + [(len(Z_PLANES), rows, cols)] * 2, natural
    )
    shapes = [(2 * depth, 8, cols)] * 2 + [(3, 8, cols)] * 2
    return arrays, *z, *packed(pack_rest_kernel, shapes, arrays)


def relay_kernel(z_even, z_odd, y_odd, before, after, relay):
    z_is_even = lax.axis_index("gz") % 2 == 0
    y_is_odd = lax.axis_index("gy") % 2
    for n in range(len(Z_PLANES)):
        e, o = z_even[n], z_odd[n]
        before[n] = jnp.where(z_is_even, o, e)
        after[n] = jnp.where(z_is_even, e, o)
    sources = []
    for a, i in CORNERS:
        n = Z_PLANES.index((a, 0))
        sources += [(before, n + Z_WIDTHS[a] - CORNER_WIDTHS[a] + i), (after, n + i)]
    tile_pairs(sources, 1 - y_is_odd, relay)


def corner_kernel(d_even, d_odd, d_before, d_after):
    z_is_even = lax.axis_index("gz") % 2 == 0
    y_is_odd = lax.axis_index("gy") % 2
    for out, x, y in ((d_before, d_odd, d_even), (d_after, d_even, d_odd)):
        tiles = [jnp.where(z_is_even, x[t], y[t]) for t in range(3)]
        for t, first, a, k in SLOTS:
            i = CORNER_WIDTHS[a] - k if out is d_before else k - 1
            out[CORNERS.index((a, i))] = moved(tiles[t], -first, 1 - y_is_odd)


def cornered(d_even, d_odd):
    cols = d_even.shape[2]
    return pl.pallas_call(
        corner_kernel,
        out_shape=[jax.ShapeDtypeStruct((len(CORNERS), 8, cols), jnp.float32)] * 2,
        in_specs=[pl.BlockSpec(memory_space=VMEM)] * 2,
        out_specs=[pl.BlockSpec(memory_space=VMEM)] * 2,
        cost_estimate=pl.CostEstimate(flops=2 * 10**9, bytes_accessed=10**6, transcendentals=0),
        compiler_params=pltpu.CompilerParams(vmem_limit_bytes=16 * 2**20),
    )(d_even, d_odd)


def relayed(z_even, z_odd, y_odd):
    cols = z_even.shape[2]
    shapes = [z_even.shape] * 2 + [(len(CORNERS), 8, cols)]
    return pl.pallas_call(
        relay_kernel,
        out_shape=[jax.ShapeDtypeStruct(shape, jnp.float32) for shape in shapes],
        in_specs=[pl.BlockSpec(memory_space=VMEM)] * 3,
        out_specs=[pl.BlockSpec(memory_space=VMEM)] * 3,
        compiler_params=pltpu.CompilerParams(vmem_limit_bytes=16 * 2**20),
    )(z_even, z_odd, y_odd)


def krylov_steps(
    counts, depth, rows, cols, m_pad, w_pad, free, b_pad, v1, v2, acc, fields, loops, given=None
):
    def at(p, ref, n, margin):
        inside = LO + margin <= p < LO + depth - margin
        return given[n] if given is not None and inside else ref

    def m_at(p):
        return at(p, m_pad, 0, 0)

    def w_at(p):
        return at(p, w_pad, 1, 0)

    def free_at(p):
        return at(p, free, 2, 1)

    _, nz, ny = counts
    zi, yi = lax.axis_index("gz"), lax.axis_index("gy")
    wide = rows + 8
    f32 = jnp.float32
    ring_row = lax.broadcasted_iota(jnp.int32, (8, cols), 0)
    own = slice(0, rows)
    ring = slice(rows, wide)

    def put(a, plane, where, values):
        if a == 0:
            m_pad[0, plane, where, :] = jnp.where(
                values == 0, 1.0, jnp.where(values == 1, PAIR, 0.0)
            )
            m_pad[1, plane, where, :] = jnp.where(
                values == 2, 1.0, jnp.where(values == 3, PAIR, 0.0)
            )
        else:
            w_pad[a - 1, plane, where, :] = values

    def cut_edges(planes):
        for p, at_rim in ((LO + depth - 1, zi == nz - 1), (LO - 1, zi == 0)):
            if p in planes:
                w_pad[0, p] = jnp.where(at_rim, 0.0, w_pad[0, p])
        x_end = slice(cols - 128, cols)
        last_x = lax.broadcasted_iota(jnp.int32, (wide, 128), 1) == 127
        at_end = (yi == ny - 1) & (ring_row == 7)
        at_start = (yi == 0) & (ring_row == 7)
        for p in planes:
            here = slice(rows - 8, rows)
            w_pad[1, p, here, :] = jnp.where(at_end, 0.0, w_pad[1, p, here, :])
            w_pad[1, p, ring, :] = jnp.where(at_start, 0.0, w_pad[1, p, ring, :])
            w_pad[2, p, :, x_end] = jnp.where(last_x, 0.0, w_pad[2, p, :, x_end])

    lanes = [slice(l, l + 128) for l in range(0, cols, 128)]
    lane = lax.broadcasted_iota(jnp.int32, (8, 128), 1)
    row = lax.broadcasted_iota(jnp.int32, (8, 128), 0)

    row_tiles = range(0, wide, 8)

    def tile(ref, index, r):
        return [ref[(*index, slice(r, r + 8), l)] for l in lanes]

    def plane(ref, *index):
        return [tile(ref, index, r) for r in row_tiles]

    def store(ref, index, r, values):
        for l, x in zip(lanes, values):
            ref[(*index, slice(r, r + 8), l)] = x

    def store_plane(ref, index, values):
        for r, x in zip(row_tiles, values):
            store(ref, index, r, x)

    def each(f, *planes):
        return [[f(*x) for x in zip(*rows_)] for rows_ in zip(*planes)]

    def next_x(v):
        return [x[1:] + [pltpu.roll(x[0], 127, 1)] for x in v]

    def prev_x(v):
        return [[pltpu.roll(x[-1], 1, 1)] + x[:-1] for x in v]

    def next_y(v):
        pair = lambda a, b: pltpu.roll(jnp.where(row == 0, b, a), 7, 0)
        return each(pair, v, v[1:] + v[:1])

    def prev_y(v):
        pair = lambda a, b: pltpu.roll(jnp.where(row == 7, b, a), 1, 0)
        return each(pair, v, v[-1:] + v[:-1])

    def times(x, y):
        return each(lambda a, b: a * b, x, y)

    def repeated(count, body):
        if loops:
            lax.fori_loop(0, count, body, 0)
        else:
            for n in range(count):
                body(n, 0)

    def prepare(*ranges):
        def body(h, _):
            for start, count in ranges:
                here = plane(m_at(start), h, start)
                from_behind = times(
                    plane(w_at(start - 1), 0, start - 1), plane(m_at(start - 1), h, start - 1)
                )
                for p in range(start, start + count):
                    ahead = plane(m_at(p + 1), h, p + 1)
                    w_z, w_y, w_x = (plane(w_at(p), i, p) for i in range(3))
                    sums_ = each(
                        lambda a, b, c, d, e, f: (a + b) + (c + d) + (e + f),
                        times(w_z, ahead), from_behind,
                        times(w_y, next_y(here)), prev_y(times(w_y, here)),
                        times(w_x, next_x(here)), prev_x(times(w_x, here)),
                    )
                    other = plane(m_at(p), 1 - h, p)
                    u = each(lambda a, b: jnp.where(a + b == 0.0, 1.0, 0.0), here, other)
                    store_plane(free, (p,), u)
                    sums_ = times(sums_, u)
                    second = each(lambda x: jnp.floor(x * (1.0 / PAIR)), sums_)
                    store_plane(b_pad, (2 * h, p), each(lambda x, y: x - PAIR * y, sums_, second))
                    store_plane(b_pad, (2 * h + 1, p), second)
                    from_behind = times(w_z, here)
                    here = ahead
            return 0

        for n in range(2):
            body(n, 0)

    def flow(w, x, y):
        return each(lambda a, b, c: a * (b - c), w, x, y)

    def apply(source, n, margin, target, *ranges):
        def v_at(p):
            return at(p, source, n, margin)

        def body(c, _):
            for start, count in ranges:
                here = plane(v_at(start), c, start)
                behind = plane(v_at(start - 1), c, start - 1)
                from_behind = flow(plane(w_at(start - 1), 0, start - 1), here, behind)
                for p in range(start, start + count):
                    ahead = plane(v_at(p + 1), c, p + 1)
                    f_z = flow(plane(w_at(p), 0, p), ahead, here)
                    f_y = flow(plane(w_at(p), 1, p), next_y(here), here)
                    f_x = flow(plane(w_at(p), 2, p), next_x(here), here)
                    store_plane(target, (c, p), each(
                        lambda u, a, b, c, d, e, f: u * ((a - b) + (c - d) + (e - f)),
                        plane(free_at(p), p), from_behind, f_z, prev_y(f_y), f_y, prev_x(f_x), f_x,
                    ))
                    from_behind, here = f_z, ahead
            return 0

        repeated(LABELS // 2, lambda n, x: body(2 * n + 1, body(2 * n, x)))

    half_pairs = [(a, b) for a in range(LABELS) for b in range(a, LABELS)]
    all_pairs = [(a, b) for a in range(LABELS) for b in range(LABELS)]

    def total(products):
        while len(products) > 1:
            products = [x + y for x, y in zip(products[::2], products[1::2])] + (
                [products[-1]] if len(products) % 2 else []
            )
        return products[0]

    def add_up(first, parts):
        for n, part in enumerate(parts):
            acc[first + n] = acc[first + n] + total(part)

    own_tiles = range(0, rows, 8)

    def accumulate(p, _):
        parts = [[] for _ in range(30)]
        for r in own_tiles:
            bs = [tile(b_pad, (c, p), r) for c in range(LABELS)]
            abs_ = [tile(v1, (c, p), r) for c in range(LABELS)]
            for l in range(len(lanes)):
                b, ab = [x[l] for x in bs], [x[l] for x in abs_]
                products = [b[i] * b[j] for i, j in half_pairs]
                products += [b[i] * ab[j] for i, j in half_pairs]
                products += [ab[i] * ab[j] for i, j in half_pairs]
                for part, product in zip(parts, products):
                    part.append(product)
            for c in range(LABELS):
                if fields is not None:
                    store(fields, (0, c, p - LO), r, bs[c])
                    store(fields, (1, c, p - LO), r, abs_[c])
        add_up(0, parts)
        return 0

    def accumulate_last(p, _):
        parts = [[] for _ in range(36)]
        own_w = w_pad if given is None else given[1]
        w_z, w_y, w_x = (plane(own_w, i, p) for i in range(3))
        w_zb = plane(own_w, 0, jnp.maximum(p - 1, LO))
        if given is not None:
            w_zb = each(lambda a, b: jnp.where(p == LO, a, b), plane(w_pad, 0, LO - 1), w_zb)
        degree = each(
            lambda a, b, c, d, e, f: (a + b) + (c + d) + (e + f),
            w_z, w_zb, w_y, prev_y(w_y), w_x, prev_x(w_x),
        )
        qs, aabs_ = [], []
        for c in range(LABELS):
            v = plane(v2, c, p)
            qs.append(each(
                lambda d, x, a, b, e: d * x - 2.0 * (a + b + e),
                degree, v, times(w_z, plane(v2, c, p + 1)), times(w_y, next_y(v)),
                times(w_x, next_x(v)),
            ))
            aabs_.append(v)
        for t, r in enumerate(own_tiles):
            abs_ = [tile(v1, (c, p), r) for c in range(LABELS)]
            for l in range(len(lanes)):
                ab, aab, q = [x[l] for x in abs_], [x[t][l] for x in aabs_], [x[t][l] for x in qs]
                products = [ab[i] * aab[j] for i, j in half_pairs]
                products += [aab[i] * aab[j] for i, j in half_pairs]
                products += [aab[i] * q[j] for i, j in all_pairs]
                for part, product in zip(parts, products):
                    part.append(product)
            for c in range(LABELS):
                if fields is not None:
                    store(fields, (2, c, p - LO), r, aabs_[c][t])
        add_up(30, parts)
        return 0

    return types.SimpleNamespace(
        put=put, cut_edges=cut_edges, prepare=prepare,
        first=functools.partial(apply, b_pad, 3, 1, v1),
        second=functools.partial(apply, v1, 4, 2, v2), accumulate=accumulate, accumulate_last=accumulate_last,
        half_pairs=half_pairs, all_pairs=all_pairs, own=own, ring=ring,
    )


def unpacked(even, odd, y_is_even):
    half = lax.broadcasted_iota(jnp.int32, even.shape, 0) < 4
    from_even = half == y_is_even
    return jnp.where(from_even, even, odd), pltpu.roll(jnp.where(from_even, odd, even), 4, 0)


def inner_kernel(
    counts, arrays, y_even, y_odd, m_pad, w_pad, free, b_pad, v1, v2, acc
):
    _, depth, rows, cols = arrays.shape
    y_is_even = lax.axis_index("gy") % 2 == 0
    do = krylov_steps(counts, depth, rows, cols, m_pad, w_pad, free, b_pad, v1, v2, acc, None, False)
    for a in range(4):
        for p in range(depth):
            do.put(a, LO + p, do.own, arrays[a, p])
    for k in range(2 * depth):
        for j, x in enumerate(unpacked(y_even[k], y_odd[k], y_is_even)):
            a, p = divmod(2 * k + j, depth)
            do.put(a, LO + p, do.ring, x)
    do.cut_edges(range(LO, LO + depth))
    do.prepare((LO + 1, depth - 2))
    do.first((LO + 2, depth - 4))
    do.second((LO + 3, depth - 6))
    for n in range(66):
        acc[n] = jnp.zeros((8, 128), jnp.float32)
    lax.fori_loop(LO + 2, LO + depth - 2, do.accumulate, 0)
    lax.fori_loop(LO + 3, LO + depth - 4, do.accumulate_last, 0)


def padded_shapes(depth, rows, cols):
    planes, wide = depth + LO + HI, rows + 8
    sizes = [(2,), (3,), (), (LABELS,), (LABELS,), (LABELS,)]
    return [(*size, planes, wide, cols) for size in sizes] + [(66, 8, 128)]


def inner(counts, arrays, y_even, y_odd):
    _, depth, rows, cols = arrays.shape
    f32 = jnp.float32
    return pl.pallas_call(
        functools.partial(inner_kernel, counts),
        out_shape=[jax.ShapeDtypeStruct(x, f32) for x in padded_shapes(depth, rows, cols)],
        in_specs=[pl.BlockSpec(memory_space=VMEM)] * 3,
        out_specs=[pl.BlockSpec(memory_space=VMEM)] * 7,
        cost_estimate=pl.CostEstimate(flops=10**7, bytes_accessed=10**6, transcendentals=0),
        compiler_params=pltpu.CompilerParams(vmem_limit_bytes=20 * 2**20),
    )(arrays, y_even, y_odd)


def outer_kernel(
    counts, before, after, d_before, d_after, relay,
    m_in, w_in, free_in, b_in, v1_in, v2_in, acc_in,
    fields, moments,
    m_pad, w_pad, free, b_pad, v1, v2, acc, sums,
):
    depth, rows, cols = fields.shape[2:]
    f32 = jnp.float32
    y_is_even = lax.axis_index("gy") % 2 == 0
    given = (m_in, w_in, free_in, b_in, v1_in)
    do = krylov_steps(
        counts, depth, rows, cols, m_pad, w_pad, free, b_pad, v1, v2, acc, fields, True, given
    )
    for n, (a, i) in enumerate(Z_PLANES):
        do.put(a, LO + depth + i, do.own, after[n])
        if LO - Z_WIDTHS[a] + i >= 0:
            do.put(a, LO - Z_WIDTHS[a] + i, do.own, before[n])
    for n, (a, i) in enumerate(CORNERS):
        even = relay[n]
        even_after = pltpu.roll(even, 4, 0)
        do.put(a, LO - CORNER_WIDTHS[a] + i, do.ring, unpacked(even, d_before[n], y_is_even)[0])
        do.put(a, LO + depth + i, do.ring, unpacked(even_after, d_after[n], y_is_even)[0])
    zero_tile = jnp.zeros((8, cols), f32)
    do.put(0, LO + depth + 3, do.ring, zero_tile)
    do.put(3, LO + depth + 2, do.ring, zero_tile)
    do.put(3, 0, do.ring, zero_tile)
    low, high = LO, LO + depth
    for source, target, planes in (
        (b_in, b_pad, (low + 1, high - 2)),
        (v1_in, v1, (low + 2, high - 4, high - 3)),
        (v2_in, v2, (low + 3, high - 4)),
    ):
        for p in planes:
            for c in range(LABELS):
                target[c, p] = source[c, p]
    for n in range(66):
        acc[n] = acc_in[n]
    do.cut_edges([p for p in range(high + 3) if p not in range(low, high)])

    do.prepare((1, low), (high - 1, 4))
    do.first((2, low), (high - 2, 4))
    do.second((3, low), (high - 3, 4))
    lax.fori_loop(0, 4, lambda i, x: do.accumulate(low + i + (i // 2) * (depth - 4), x), 0)
    lax.fori_loop(
        0, depth - 1, lambda i, x: do.accumulate_last(low + i + jnp.where(i >= 3, 1, 0), x), 0
    )

    half_pairs, all_pairs = do.half_pairs, do.all_pairs
    low, high = [acc[n] for n in range(30)], [acc[30 + n] for n in range(36)]
    kept = {}
    for k in range(5):
        part = low[10 * k : 10 * k + 10] if k < 3 else high[10 * (k - 3) : 10 * (k - 3) + 10]
        for (a, b), x in zip(half_pairs, part):
            kept[k, a, b] = kept[k, b, a] = x
    last = dict(zip(all_pairs, high[20:]))
    for a, b in half_pairs:
        kept[5, a, b] = kept[5, b, a] = 0.5 * (last[a, b] + last[b, a])
    for k in range(6):
        for a, b in half_pairs:
            x = jnp.sum(kept[k, a, b], axis=0, keepdims=True)
            for i, j in {(a, b), (b, a)}:
                at = (2 * k + j // 2) * 8 + (j % 2) * 4 + i
                sums[at : at + 1, :] = x
    lane = lax.broadcasted_iota(jnp.int32, (8, 128), 1)
    packed = jnp.zeros((8, 128), f32)
    for g in range(12):
        x = jnp.sum(sums[8 * g : 8 * g + 8, :], axis=1, keepdims=True)
        packed = jnp.where(lane == g, x, packed)
    moments[...] = packed


def outer(counts, shape, halos, insides):
    _, depth, rows, cols = shape
    f32 = jnp.float32
    return pl.pallas_call(
        functools.partial(outer_kernel, counts),
        out_shape=[
            jax.ShapeDtypeStruct((3, LABELS, depth, rows, cols), f32),
            jax.ShapeDtypeStruct((8, 128), f32),
        ],
        in_specs=[pl.BlockSpec(memory_space=VMEM)] * 12,
        out_specs=[pl.BlockSpec(memory_space=VMEM)] * 2,
        scratch_shapes=[VMEM(x, f32) for x in padded_shapes(depth, rows, cols)]
        + [VMEM((96, 128), f32)],
        compiler_params=pltpu.CompilerParams(vmem_limit_bytes=28 * 2**20),
    )(*halos, *insides)


def solved(moment, sides, floor):
    n = 3 * LABELS
    system = {
        (i, j): moment(i // LABELS + j // LABELS + 1, i % LABELS, j % LABELS)
        for i in range(n) for j in range(i + 1)
    }
    right = dict(enumerate(sides))
    first = {k: system[k, k] for k in range(n)}
    lower, inverse = {}, {}
    for k in range(n):
        pivot = system[k, k]
        sound = pivot > floor * first[k]
        inverse[k] = jnp.where(sound, 1.0 / pivot, 0.0)
        for i in range(k + 1, n):
            lower[i, k] = system[i, k] * inverse[k]
        for i in range(k + 1, n):
            for j in range(k + 1, i + 1):
                system[i, j] = system[i, j] - lower[i, k] * system[j, k]
            right[i] = right[i] - lower[i, k] * right[k]
    for k in reversed(range(n)):
        x = right[k] * inverse[k]
        for i in range(k + 1, n):
            x = x - lower[i, k] * right[i]
        right[k] = x
    return [right[k] for k in range(n)]


def combine_kernel(
    mine, theirs, fields, b_in, v1_in, v2_in, natural, out, spread, coeffs, mixed, buffer, sems
):
    f32 = jnp.float32
    _, depth, rows, cols = natural.shape
    sums = mine[...] + theirs[...]
    columns = [jnp.broadcast_to(sums[:, g : g + 1], (8, 128)) for g in range(12)]
    for g in range(12):
        spread[g] = columns[g]

    def moment(k, a, b):
        a, b = min(a, b), max(a, b)
        at = (b % 2) * 4 + a
        return jnp.broadcast_to(spread[2 * k + b // 2, at : at + 1, :], (8, 128))

    sides = []
    for k in range(3):
        for a in range(LABELS):
            x = columns[2 * k + a // 2]
            sides.append(pltpu.roll(x, 4, 0) if a % 2 else x)
    for k, x in enumerate(solved(moment, sides, PIVOT_FLOOR)):
        coeffs[k] = x

    back = interleave(cols, back=True)
    back = jnp.concatenate([back, back], axis=0)
    chunk = depth // CHUNKS

    def field(k, p, cut):
        n, c = divmod(k, LABELS)
        inside = range(2, depth - 2) if n < 2 else range(3, depth - 4)
        if p in inside:
            return (b_in, v1_in, v2_in)[n][(c, LO + p) + cut]
        return fields[(n, c, p) + cut]

    def combine(n):
        for first in range(0, LABELS, 2):
            weights = {
                (k, c): jnp.broadcast_to(coeffs[k, c : c + 1, :], (8, 128))
                for k in range(3 * LABELS) for c in (first, first + 1)
            }
            for p in range(n * chunk, n * chunk + chunk):
                for r in range(0, rows, 8):
                    for l in range(0, cols, 128):
                        cut = (slice(r, r + 8), slice(l, l + 128))
                        v = [field(k, p, cut) for k in range(3 * LABELS)]
                        for c in (first, first + 1):
                            s = [v[k] * weights[k, c] for k in range(3 * LABELS)]
                            while len(s) > 1:
                                s = [x + y for x, y in zip(s[::2], s[1::2])] + (
                                    [s[-1]] if len(s) % 2 else []
                                )
                            mixed[(c, p) + cut] = s[0]

    def turn_back(n):
        planes = slice(n * chunk, n * chunk + chunk)
        x = mixed[:, planes].reshape(LABELS * chunk * rows, cols)
        high = x.astype(jnp.bfloat16)
        low = (x - high.astype(f32)).astype(jnp.bfloat16)
        x = jnp.dot(jnp.concatenate([high, low], axis=1), back, preferred_element_type=f32)
        x = x.reshape(LABELS, chunk, rows, cols)
        for c in range(LABELS):
            buffer[c, planes] = jnp.where(natural[0, planes] == c, 1.0, x[c])

    copies = [
        pltpu.make_async_copy(
            buffer.at[:, n * chunk : (n + 1) * chunk], out.at[:, n * chunk : (n + 1) * chunk],
            sems.at[n],
        )
        for n in range(CHUNKS)
    ]
    combine(0)
    for n in range(CHUNKS):
        if n + 1 < CHUNKS:
            combine(n + 1)
        turn_back(n)
        copies[n].start()
    for copy in copies:
        copy.wait()


def combined(mine, theirs, fields, insides, natural):
    _, depth, rows, cols = natural.shape
    f32 = jnp.float32
    return pl.pallas_call(
        combine_kernel,
        out_shape=jax.ShapeDtypeStruct((LABELS, depth, rows, cols), f32),
        in_specs=[pl.BlockSpec(memory_space=VMEM)] * 7,
        out_specs=pl.BlockSpec(memory_space=pltpu.HBM),
        scratch_shapes=[
            VMEM((12, 8, 128), f32),
            VMEM((3 * LABELS, 8, 128), f32),
            VMEM((LABELS, depth, rows, cols), f32),
            VMEM((LABELS, depth, rows, cols), f32),
            pltpu.SemaphoreType.DMA((CHUNKS,)),
        ],
        compiler_params=pltpu.CompilerParams(vmem_limit_bytes=32 * 2**20),
    )(mine, theirs, fields, *insides, natural)


def per_device(counts, tags, depth_affinity, row_affinity, column_affinity):
    parts, nz, ny = counts
    natural = jnp.stack([tags, depth_affinity, row_affinity, column_affinity])
    axes = ("parts", "gz", "gy")
    ze, zo = (lambda z: even_partner(z, nz)), (lambda z: odd_partner(z, nz))
    ye, yo = (lambda y: even_partner(y, ny)), (lambda y: odd_partner(y, ny))

    def swap(array, pz, py):
        def pair(z, y):
            if pz and pz(z) == z:
                return z, ye(y)
            if py and py(y) == y:
                return z, y
            return pz(z) if pz else z, py(y) if py else y
        return exchanged(array, axes, counts, pair)

    arrays, z_even, z_odd, y_even, y_odd, d_even, d_odd = pack(natural)
    y_odd = swap(y_odd, None, yo)
    insides = inner(counts, arrays, swap(y_even, None, ye), y_odd)
    before, after, relay = relayed(swap(z_even, ze, None), swap(z_odd, zo, None), y_odd)
    corners = cornered(swap(d_even, ze, yo), swap(d_odd, zo, yo))
    halos = [before, after, *corners, swap(relay, None, ye)]
    fields, moments = outer(counts, arrays.shape, halos, insides)

    steps = [lambda z, y: (z, y ^ 1)]
    steps += [lambda z, y, d=d: (z, y ^ d ^ 1) for d in powers(ny)[1:]]
    steps += [lambda z, y, d=d: (z ^ d, y ^ 1) for d in powers(nz)]
    for n, pair in enumerate(steps):
        theirs = exchanged(moments, axes, counts, pair)
        if n < len(steps) - 1:
            moments = moments + theirs
    return combined(moments, theirs, fields, insides[3:6], natural)


def powers(count):
    return [1 << n for n in range(count.bit_length() - 1)]


def solution(mesh):
    counts = tuple(mesh.shape[axis] for axis in ("parts", "gz", "gy"))
    placed = P(("parts", "gz"), "gy", None)
    return jax.shard_map(
        functools.partial(per_device, counts),
        mesh=mesh,
        in_specs=(placed,) * 4,
        out_specs=P(None, ("parts", "gz"), "gy", None),
        check_vma=False,
    )
```
